256 devices in a mesh: section: 8 (over z), seq: 16 (over y_hi, x, core), tensor: 2 (over y_lo).
Axes of the slice: x: 4, y: 4 (y_hi: 2, y_lo: 2; y = y_hi * 2 + y_lo), z: 8, core: 2. Of those that a mesh axis runs over, the one named last changes fastest.
Arguments:
- hidden: bfloat16 [2048, 8192], P('seq', ('section', 'tensor')), may hold values from -6 to 6
- dec_gain: float32 [8192], P(('section', 'tensor')), may hold values from 0.5 to 1.5
- neigh_states: bfloat16 [4096, 8192], P('seq', ('section', 'tensor')), may hold values from -6 to 6
- enc_gain: float32 [8192], P(('section', 'tensor')), may hold values from 0.5 to 1.5
- w_query: bfloat16 [8192, 8192], P(('section', 'tensor'), 'seq'), may hold values from -0.0625 to 0.0625
- w_key: bfloat16 [8192, 8192], P(('section', 'tensor'), 'seq'), may hold values from -0.0625 to 0.0625
- w_value: bfloat16 [8192, 8192], P(('section', 'tensor'), 'seq'), may hold values from -0.0625 to 0.0625
- w_out: bfloat16 [8192, 8192], P('seq', ('section', 'tensor')), may hold values from -0.0625 to 0.0625
- neighbour_ids: int32 [32], replicated, may hold values from 0 to 31, each once
- neighbour_len: int32 [32], replicated, may hold values from 32 to 128, as said below
- cotangent: bfloat16 [2048, 8192], P('seq', ('section', 'tensor')), may hold values from -6 to 6
Outputs:
- layer_out: bfloat16 [2048, 8192], P('seq', ('section', 'tensor'))
- hidden_grad: float32 [2048, 8192], P('seq', ('section', 'tensor'))
- neighbour_grad: float32 [4096, 8192], P('seq', ('section', 'tensor'))
- dec_gain_grad: float32 [8192], P(('section', 'tensor'))
- enc_gain_grad: float32 [8192], P(('section', 'tensor'))
- query_weight_grad: float32 [8192, 8192], P(('section', 'tensor'), 'seq')
- key_weight_grad: float32 [8192, 8192], P(('section', 'tensor'), 'seq')
- value_weight_grad: float32 [8192, 8192], P(('section', 'tensor'), 'seq')
- out_weight_grad: float32 [8192, 8192], P('seq', ('section', 'tensor'))
The draws below stay inside these ranges and needn't reach their ends.
Inputs may be any that keep to these rules, and one draw needn't show every extreme that they name: `neighbour_ids`: each stored neighbour serves exactly one slot. `neighbour_len`: some stored neighbour is full.
All inputs are finite; a program needn't handle non-finite values.
Results may differ from the reference program's by a relative error of at most 0.0095.
Values may be sent and summed in bfloat16 or wider, within the bound.
A program may use at most 128 MiB of HBM per device.

```python
import jax
import jax.numpy as jnp
from jax import lax

D = 8192
HEADS = 64
HEAD = 128
BLOCK = 64
NEIGH = 1
NLEN = 128
QD = 8192
NCH = 32
TOK = 2048
NSTORE = 32
NT = 4096


def draw_neighbour_len(key, part):
    key = jax.random.fold_in(key, 7)
    drawn = jax.random.randint(key, (NSTORE,), NLEN // 4, NLEN + 1, dtype=jnp.int32)
    return drawn.at[0].set(NLEN)


def level_of(stream_key, extent, cuts, smallest, largest):
    factor_of, own = 1.0, jax.random.fold_in(stream_key, 6)
    for dim, blocks in cuts:
        heights = jnp.exp(jax.random.uniform(jax.random.fold_in(own, dim), (blocks,), jnp.float32, smallest / len(cuts), largest / len(cuts)))
        factor_of = factor_of * jnp.repeat(heights, extent[dim] // blocks).reshape([-1 if axis == dim else 1 for axis in range(len(extent))])
    return factor_of


def centred(key, shape, spread, most, split=(), kind=jnp.bfloat16):
    values = spread * jax.random.normal(key, shape, jnp.float32)
    if split:
        values = values * level_of(key, shape, split, -0.22, 0.18)
    return jnp.clip(values, -most, most).astype(kind)


def setup_inputs(seed: int = 0) -> dict:
    seeds = jax.random.split(jax.random.key(seed), 12)
    return {
        "hidden": centred(seeds[0], (TOK, D), 1.0, 6.0, ((0, 16), (1, 16))),
        "dec_gain": jnp.clip(1.0 + 0.1 * jax.random.normal(seeds[1], (D,), jnp.float32), 0.5, 1.5),
        "neigh_states": centred(seeds[2], (NT, D), 1.0, 6.0, ((0, 16), (1, 16))),
        "enc_gain": jnp.clip(1.0 + 0.1 * jax.random.normal(seeds[3], (D,), jnp.float32), 0.5, 1.5),
        "w_query": centred(seeds[4], (D, QD), D ** -0.5, 0.0625, ((0, 16), (1, 16))),
        "w_key": centred(seeds[5], (D, QD), D ** -0.5, 0.0625, ((0, 16), (1, 16))),
        "w_value": centred(seeds[6], (D, QD), D ** -0.5, 0.0625, ((0, 16), (1, 16))),
        "w_out": centred(seeds[7], (QD, D), QD ** -0.5, 0.0625, ((0, 16), (1, 16))),
        "neighbour_ids": jax.random.permutation(seeds[8], NSTORE).astype(jnp.int32),
        "neighbour_len": draw_neighbour_len(jax.random.fold_in(seeds[11], 71), 0),
        "cotangent": centred(seeds[10], (TOK, D), 1.0, 6.0, ((0, 16), (1, 16))),
    }


EPS = 1e-05

def normalize(rows, gain):
    values = rows.astype(jnp.float32)
    scale = lax.rsqrt(lax.optimization_barrier(jnp.mean(values * values, axis=-1, keepdims=True)) + EPS)
    unit = values * scale
    return (unit, scale, (unit * gain).astype(jnp.bfloat16))

def norm_back(unit, scale, gain, upstream):
    scaled = gain * upstream
    inner = lax.optimization_barrier(jnp.mean(scaled * unit, axis=-1, keepdims=True))
    return (scale * (scaled - unit * inner), lax.optimization_barrier(jnp.sum(upstream * unit, axis=0)))

def reference(hidden, dec_gain, neigh_states, enc_gain, w_query, w_key, w_value, w_out, neighbour_ids, neighbour_len, cotangent):
    dec_hat, dec_scale, dec_normed = normalize(hidden, dec_gain)
    enc_hat, enc_scale, enc_normed = normalize(neigh_states, enc_gain)
    queries = jnp.dot(dec_normed, w_query, preferred_element_type=jnp.float32).astype(jnp.bfloat16)
    offsets = jnp.arange(NLEN, dtype=jnp.int32)
    row_index = (neighbour_ids.astype(jnp.int32)[:, None] * NLEN + offsets[None, :]).reshape(-1)
    ordered = enc_normed[row_index]
    lengths = neighbour_len[neighbour_ids]
    keys = jnp.dot(ordered, w_key, preferred_element_type=jnp.float32).astype(jnp.bfloat16)
    values = jnp.dot(ordered, w_value, preferred_element_type=jnp.float32).astype(jnp.bfloat16)
    scale = HEAD ** (-0.5)
    q_four = queries.reshape(NCH, BLOCK, HEADS, HEAD).astype(jnp.float32)
    k_four = keys.reshape(NCH, NEIGH * NLEN, HEADS, HEAD).astype(jnp.float32)
    v_four = values.reshape(NCH, NEIGH * NLEN, HEADS, HEAD).astype(jnp.float32)
    scores = jnp.einsum('cihd,cjhd->chij', q_four, k_four) * scale
    positions = jnp.arange(NEIGH * NLEN, dtype=jnp.int32)
    valid = (positions % NLEN)[None, :] < jnp.repeat(lengths.reshape(NCH, NEIGH), NLEN, axis=1)
    scores = jnp.where(valid[:, None, None, :], scores, -jnp.inf)
    top = lax.optimization_barrier(jnp.max(scores, axis=-1, keepdims=True))
    expo = jnp.exp(scores - top)
    probs = expo / lax.optimization_barrier(jnp.sum(expo, axis=-1, keepdims=True))
    probs_low = probs.astype(jnp.bfloat16).astype(jnp.float32)
    attended = jnp.einsum('chij,cjhd->cihd', probs_low, v_four).reshape(TOK, QD).astype(jnp.bfloat16)
    layer_out = (hidden.astype(jnp.float32) + jnp.dot(attended, w_out, preferred_element_type=jnp.float32)).astype(jnp.bfloat16)
    out_weight_grad = jnp.dot(attended.T, cotangent, preferred_element_type=jnp.float32)
    attended_grad = jnp.dot(cotangent, w_out.T, preferred_element_type=jnp.float32).astype(jnp.bfloat16)
    grad_four = attended_grad.reshape(NCH, BLOCK, HEADS, HEAD).astype(jnp.float32)
    value_grad = jnp.einsum('chij,cihd->cjhd', probs_low, grad_four).reshape(NT, QD).astype(jnp.bfloat16)
    prob_grad = jnp.einsum('cihd,cjhd->chij', grad_four, v_four)
    score_grad = probs * (prob_grad - lax.optimization_barrier(jnp.sum(probs * prob_grad, axis=-1, keepdims=True))) * scale
    query_grad = jnp.einsum('chij,cjhd->cihd', score_grad, k_four, precision=lax.Precision.HIGHEST).reshape(TOK, QD).astype(jnp.bfloat16)
    key_grad = jnp.einsum('chij,cihd->cjhd', score_grad, q_four, precision=lax.Precision.HIGHEST).reshape(NT, QD).astype(jnp.bfloat16)
    query_weight_grad = jnp.dot(dec_normed.T, query_grad, preferred_element_type=jnp.float32)
    key_weight_grad = jnp.dot(ordered.T, key_grad, preferred_element_type=jnp.float32)
    value_weight_grad = jnp.dot(ordered.T, value_grad, preferred_element_type=jnp.float32)
    dec_input = jnp.dot(query_grad, w_query.T, preferred_element_type=jnp.float32)
    ordered_input = jnp.dot(key_grad, w_key.T, preferred_element_type=jnp.float32) + jnp.dot(value_grad, w_value.T, preferred_element_type=jnp.float32)
    inverse = jnp.zeros((NSTORE,), jnp.int32).at[neighbour_ids].set(jnp.arange(NSTORE, dtype=jnp.int32))
    back_index = (inverse[:, None] * NLEN + offsets[None, :]).reshape(-1)
    enc_input = ordered_input[back_index]
    dec_back, dec_gain_grad = norm_back(dec_hat, dec_scale, dec_gain, dec_input)
    hidden_grad = cotangent.astype(jnp.float32) + dec_back
    neighbour_grad, enc_gain_grad = norm_back(enc_hat, enc_scale, enc_gain, enc_input)
    return (layer_out, hidden_grad, neighbour_grad, dec_gain_grad, enc_gain_grad, query_weight_grad, key_weight_grad, value_weight_grad, out_weight_grad)
```

```python
import functools

import jax
import jax.numpy as jnp
from jax import lax
from jax.experimental import pallas as pl
from jax.experimental.pallas import tpu as pltpu
from jax.sharding import PartitionSpec as P

F32 = jnp.float32
BF16 = jnp.bfloat16
MESH = pl.DeviceIdType.MESH
EPS = 1e-05
WIDTH = 8192
ANY = pl.BlockSpec(memory_space=pl.ANY)
VMEM = pl.BlockSpec(memory_space=pltpu.VMEM)
SMEM = pl.BlockSpec(memory_space=pltpu.SMEM)
DMA = pltpu.SemaphoreType.DMA
RING = 16
DEPTH = 8


def place():
    z = lax.axis_index("section")
    s = lax.axis_index("seq")
    t = lax.axis_index("tensor")
    x = lax.div(lax.rem(s, 8), 2)
    y = lax.div(s, 8) * 2 + t
    return z, s, t, x, y, lax.rem(s, 2)


def ring_position(ring, x, y):
    return (y if ring == 0 else x) * 4 + lax.rem(x + y, 4)


def ring_chip(ring, p):
    a = lax.div(p, 4)
    b = lax.rem(lax.rem(p, 4) + 4 - a, 4)
    return (b, a) if ring == 0 else (a, b)


def seq_tensor(x, y, core):
    return lax.div(y, 2) * 8 + x * 2 + core, lax.rem(y, 2)


def ring_device(ring, p, core):
    x, y = ring_chip(ring, lax.rem(p + RING, RING))
    s, t = seq_tensor(x, y, core)
    return {"seq": s, "tensor": t}


def remote(src, dst, send_sem, recv_sem, device):
    return pltpu.make_async_remote_copy(
        src_ref=src,
        dst_ref=dst,
        send_sem=send_sem,
        recv_sem=recv_sem,
        device_id=device,
        device_id_type=MESH,
    )


def greet(devices):
    barrier = pltpu.get_barrier_semaphore()
    for device in devices:
        pl.semaphore_signal(barrier, inc=1, device_id=device, device_id_type=MESH)
    pl.semaphore_wait(barrier, len(devices))


def plane_neighbours(x, y, core, s):
    p1, p2 = ring_position(0, x, y), ring_position(1, x, y)
    return [
        ring_device(0, p1 + 1, core),
        ring_device(0, p1 - 1, core),
        ring_device(1, p2 + 1, core),
        ring_device(1, p2 - 1, core),
        {"seq": s + 1 - 2 * core},
    ]


def params(cid, mib=None):
    return pltpu.CompilerParams(
        collective_id=cid,
        has_side_effects=True,
        vmem_limit_bytes=None if mib is None else mib * 1024 * 1024,
    )


def small_kernel(groups, *refs):
    n = len(groups)
    ins, outs, slots = refs[:n], refs[n : 2 * n], refs[2 * n : 3 * n]
    send, recv = refs[3 * n], refs[3 * n + 1]
    z, s, t, _, _, _ = place()

    def peer(group, r):
        if group == "st":
            g = lax.rem(z * 2 + t + r, 16)
            return {"section": lax.div(g, 2), "tensor": lax.rem(g, 2)}, g
        g = lax.rem(s + r, 16)
        return {"seq": g}, g

    barrier = pltpu.get_barrier_semaphore()
    for group in groups:

        def hello(r, _, group=group):
            pl.semaphore_signal(
                barrier, inc=1, device_id=peer(group, r)[0], device_id_type=MESH
            )
            return 0

        lax.fori_loop(1, 16, hello, 0)
    pl.semaphore_wait(barrier, 15 * n)
    for k, group in enumerate(groups):
        mine = peer(group, 0)[1]

        def push(r, _, k=k, group=group, mine=mine):
            device, _g = peer(group, r)
            remote(
                ins[k], slots[k].at[mine], send.at[k, r], recv.at[k, mine], device
            ).start()
            return 0

        lax.fori_loop(1, 16, push, 0)
        slots[k][mine] = ins[k][...]
    for k, group in enumerate(groups):
        mine = peer(group, 0)[1]

        def take(r, _, k=k, group=group, mine=mine):
            device, g = peer(group, r)
            remote(ins[k], slots[k].at[g], send.at[k, r], recv.at[k, g], device).wait_recv()
            return 0

        lax.fori_loop(1, 16, take, 0)
        total = slots[k][0]
        for g in range(1, 16):
            total = total + slots[k][g]
        outs[k][...] = total
    for k, group in enumerate(groups):
        mine = peer(group, 0)[1]

        def drain(r, _, k=k, group=group, mine=mine):
            device, _g = peer(group, r)
            remote(
                ins[k], slots[k].at[mine], send.at[k, r], recv.at[k, mine], device
            ).wait_send()
            return 0

        lax.fori_loop(1, 16, drain, 0)


def small_sums(arrays, groups, cid):
    n = len(groups)
    return pl.pallas_call(
        functools.partial(small_kernel, groups),
        out_shape=[jax.ShapeDtypeStruct((8, 128), F32)] * n,
        in_specs=[VMEM] * n,
        out_specs=[VMEM] * n,
        scratch_shapes=[pltpu.VMEM((16, 8, 128), F32)] * n + [DMA((n, 16)), DMA((n, 16))],
        compiler_params=params(cid),
    )(*arrays)


def gather_kernel(
    cot,
    dec,
    enc,
    wq,
    wk,
    wv,
    wo,
    cot_all,
    dec_all,
    enc_all,
    wq_all,
    wk_all,
    wv_all,
    wo_all,
    send,
    recv,
    sib_send,
    sib_recv,
    own_sem,
    w_send,
    w_recv,
    w_own,
):
    z, s, t, x, y, core = place()
    sibling = {"seq": s + 1 - 2 * core}
    partner = {"tensor": 1 - t}
    greet(plane_neighbours(x, y, core, s))

    def slot(k, chip, c):
        so, to = seq_tensor(chip[0], chip[1], c)
        if k == 0:
            return cot_all.at[to, pl.ds(pl.multiple_of(so * 128, 128), 128)]
        if k == 1:
            return dec_all.at[to, pl.ds(pl.multiple_of(so * 128, 128), 128)]
        return enc_all.at[to, pl.ds(pl.multiple_of(so * 256 + (k - 2) * 128, 128), 128)]

    sources = (cot, dec, enc.at[pl.ds(0, 128)], enc.at[pl.ds(128, 128)])
    position = (ring_position(0, x, y), ring_position(1, x, y))

    def origin(k, j):
        sign = 1 - 2 * (k % 2)
        return ring_chip(k // 2, lax.rem(position[k // 2] + RING - sign * j, RING))

    def onward(k, j, src):
        sign = 1 - 2 * (k % 2)
        device = ring_device(k // 2, position[k // 2] + sign, core)
        return remote(src, slot(k, origin(k, j), core), send.at[k, j], recv.at[k, j], device)

    def across(k, j, src):
        return remote(
            src, slot(k, origin(k, j), core), sib_send.at[k, j], sib_recv.at[k, j], sibling
        )

    for k in range(4):
        onward(k, 0, sources[k]).start()
    half = pl.ds(pl.multiple_of(t * 256, 256), 256)
    rest = pl.ds(pl.multiple_of((1 - t) * 256, 256), 256)
    weights = ((wq, wq_all), (wk, wk_all), (wv, wv_all))
    swaps = [
        remote(w.at[:, rest], w_all.at[t], w_send.at[n], w_recv.at[n], partner)
        for n, (w, w_all) in enumerate(weights)
    ] + [remote(wo.at[rest, :], wo_all.at[t], w_send.at[3], w_recv.at[3], partner)]
    keeps = [
        pltpu.make_async_copy(w.at[:, half], w_all.at[t], w_own.at[n])
        for n, (w, w_all) in enumerate(weights)
    ] + [pltpu.make_async_copy(wo.at[half, :], wo_all.at[t], w_own.at[3])]
    for copy in swaps:
        copy.start()
    for k in range(4):
        across(k, 0, sources[k]).start()
        pltpu.make_async_copy(sources[k], slot(k, (x, y), core), own_sem.at[k]).start()
    for copy in keeps:
        copy.start()

    def step(j, _):
        for k in range(4):
            remote(
                sources[k],
                slot(k, origin(k, j + 1), core),
                send.at[k, j],
                recv.at[k, j],
                sibling,
            ).wait_recv()
            block = slot(k, origin(k, j + 1), core)

            @pl.when(j < RING - 2)
            def _(k=k, block=block):
                onward(k, j + 1, block).start()

            across(k, j + 1, block).start()
        return 0

    lax.fori_loop(0, RING - 1, step, 0)

    for k in range(4):
        pltpu.make_async_copy(sources[k], slot(k, (x, y), core), own_sem.at[k]).wait()

    def finish(j, _):
        for k in range(4):
            remote(
                sources[k],
                slot(k, origin(k, j), 1 - core),
                sib_send.at[k, j],
                sib_recv.at[k, j],
                sibling,
            ).wait_recv()
            across(k, j, sources[k]).wait_send()

            @pl.when(j < RING - 1)
            def _(k=k):
                onward(k, j, sources[k]).wait_send()

        return 0

    lax.fori_loop(0, RING, finish, 0)
    for copy in keeps:
        copy.wait()
    for copy in swaps:
        copy.wait_send()
    for n, (w, w_all) in enumerate(weights):
        remote(w.at[:, rest], w_all.at[1 - t], w_send.at[n], w_recv.at[n], partner).wait_recv()
    remote(wo.at[rest, :], wo_all.at[1 - t], w_send.at[3], w_recv.at[3], partner).wait_recv()


def gather_rows(cot, dec, enc, wq, wk, wv, wo):
    sds = jax.ShapeDtypeStruct
    return pl.pallas_call(
        gather_kernel,
        out_shape=[
            sds((2, 2048, 512), BF16),
            sds((2, 2048, 512), BF16),
            sds((2, 4096, 512), BF16),
            sds((2, 512, 256), BF16),
            sds((2, 512, 256), BF16),
            sds((2, 512, 256), BF16),
            sds((2, 256, 512), BF16),
        ],
        in_specs=[ANY] * 7,
        out_specs=[ANY] * 7,
        scratch_shapes=[
            DMA((4, 15)),
            DMA((4, 15)),
            DMA((4, 16)),
            DMA((4, 16)),
            DMA((4,)),
            DMA((4,)),
            DMA((4,)),
            DMA((4,)),
        ],
        compiler_params=params(1),
    )(cot, dec, enc, wq, wk, wv, wo)


def reorder_kernel(index, *refs):
    n = len(refs) // 2
    ins, outs, sem = refs[:n], refs[n : 2 * n], refs[2 * n]

    def copy(j, k):
        src = pl.ds(pl.multiple_of(index[j] * 64, 64), 64)
        dst = pl.ds(pl.multiple_of(j * 64, 64), 64)
        return pltpu.make_async_copy(ins[k].at[:, src], outs[k].at[:, dst], sem.at[k, j])

    def start(j, _):
        for k in range(n):
            copy(j, k).start()
        return 0

    def wait(j, _):
        for k in range(n):
            copy(j, k).wait()
        return 0

    lax.fori_loop(0, 32, start, 0)
    lax.fori_loop(0, 32, wait, 0)


def reorder(index, *arrays):
    n = len(arrays)
    return pl.pallas_call(
        reorder_kernel,
        out_shape=[jax.ShapeDtypeStruct(a.shape, a.dtype) for a in arrays],
        in_specs=[SMEM] + [ANY] * n,
        out_specs=[ANY] * n,
        scratch_shapes=[DMA((n, 32))],
    )(index, *arrays)


def dot(a, b):
    return jnp.dot(a, b, preferred_element_type=F32)


def dot_t(a, b):
    return lax.dot_general(a, b, (((1,), (1,)), ((), ())), preferred_element_type=F32)


def t_dot(a, b):
    return lax.dot_general(a, b, (((0,), (0,)), ((), ())), preferred_element_type=F32)


def split(a):
    high = a.astype(BF16)
    return high, (a - high.astype(F32)).astype(BF16)


def attend(q, a, k, v, bias):
    scale = 128 ** (-0.5)
    scores = dot_t(q, k) * scale + bias
    top = jnp.max(scores, axis=1, keepdims=True)
    expo = jnp.exp(scores - top)
    probs = expo / jnp.sum(expo, axis=1, keepdims=True)
    low = probs.astype(BF16)
    attended = dot(low, v).astype(BF16)
    value_grad = t_dot(low, a).astype(BF16)
    prob_grad = dot_t(a, v)
    inner = jnp.sum(probs * prob_grad, axis=1, keepdims=True)
    score_grad = probs * (prob_grad - inner) * scale
    high, rest = split(score_grad)
    query_grad = (dot(high, k) + dot(rest, k)).astype(BF16)
    key_grad = (t_dot(high, q) + t_dot(rest, q)).astype(BF16)
    return attended, query_grad, key_grad, value_grad


def ring_kernel(
    dec,
    enc,
    cot,
    wq,
    wk,
    wv,
    wo,
    bias,
    att_all,
    qg_all,
    kg_all,
    vg_all,
    sendb,
    recvb,
    fin,
    att,
    qg,
    kg,
    vg,
    send,
    recv,
    g_send,
    g_recv,
    own_sem,
):
    z = lax.axis_index("section")
    ahead = {"section": lax.rem(z + 1, DEPTH)}
    behind = {"section": lax.rem(z + DEPTH - 1, DEPTH)}
    greet([ahead, behind])

    def partial(d, h):
        j = d * 4 + h * 2
        blocks = pl.ds(pl.multiple_of(j * 64, 128), 128)
        stored = pl.ds(pl.multiple_of(j * 128, 256), 256)
        q = a = k = v = 0.0
        for f in range(2):
            q = q + dot(dec[f, blocks, :], wq[f])
            a = a + dot_t(cot[f, blocks, :], wo[f])
            rows = enc[f, stored, :]
            k = k + dot(rows, wk[f])
            v = v + dot(rows, wv[f])
        return ((0, 128, q), (128, 256, a), (256, 512, k), (512, 768, v))

    def stream(n):
        h = lax.rem(n, 2)
        way = lax.rem(h + lax.div(n, 2), 2)
        return h, 1 - 2 * way, 4 - lax.div(n, 2)

    def chain(n, t, sign):
        device = {"section": lax.rem(z + DEPTH + sign, DEPTH)}
        return remote(
            sendb.at[n, t], recvb.at[n, t + 1], send.at[n, t], recv.at[n, t], device
        )

    def zero(n, _):
        recvb[n, 0] = jnp.zeros((768, 256), BF16)
        return 0

    lax.fori_loop(0, 4, zero, 0)

    def item(w, _):
        n, t = lax.rem(w, 4), lax.div(w, 4)
        h, sign, length = stream(n)
        parts = partial(lax.rem(z + DEPTH + sign * (length - t), DEPTH), h)

        @pl.when(t > 0)
        def _():
            chain(n, t - 1, sign).wait_recv()

        for lo, hi, part in parts:
            sendb[n, t, lo:hi] = (part + recvb[n, t, lo:hi].astype(F32)).astype(BF16)
        chain(n, t, sign).start()
        return 0

    lax.fori_loop(0, 14, item, 0)

    def last(h, _):
        parts = partial(z, h)
        chain(h, 3, 1).wait_recv()
        chain(h + 2, 2, 1).wait_recv()
        for lo, hi, part in parts:
            total = part + recvb[h, 4, lo:hi].astype(F32) + recvb[h + 2, 3, lo:hi].astype(F32)
            fin[h, lo:hi] = total.astype(BF16)
        return 0

    lax.fori_loop(0, 2, last, 0)

    for h in range(2):
        for u in range(2):
            n = h * 2 + u
            for g in range(2):
                head = slice(g * 128, (g + 1) * 128)
                attended, query_grad, key_grad, value_grad = attend(
                    fin[h, u * 64 : (u + 1) * 64, head],
                    fin[h, 128 + u * 64 : 128 + (u + 1) * 64, head],
                    fin[h, 256 + u * 128 : 256 + (u + 1) * 128, head],
                    fin[h, 512 + u * 128 : 512 + (u + 1) * 128, head],
                    bias[pl.ds(z * 4 + n, 1), :],
                )
                att[n * 64 : (n + 1) * 64, head] = attended
                qg[n * 64 : (n + 1) * 64, head] = query_grad
                kg[n * 128 : (n + 1) * 128, head] = key_grad
                vg[n * 128 : (n + 1) * 128, head] = value_grad

    arrays = ((kg, kg_all, 1), (vg, vg_all, -1), (att, att_all, 1), (qg, qg_all, -1))

    def origin(n, j):
        return lax.rem(z + DEPTH - arrays[n][2] * j, DEPTH)

    def onward(n, j, src):
        device = ahead if arrays[n][2] == 1 else behind
        return remote(
            src, arrays[n][1].at[origin(n, j)], g_send.at[n, j], g_recv.at[n, j], device
        )

    for n in range(4):
        onward(n, 0, arrays[n][0]).start()
    for n in range(4):
        pltpu.make_async_copy(arrays[n][0], arrays[n][1].at[z], own_sem.at[n]).start()

    def step(j, _):
        for n in range(4):
            block = arrays[n][1].at[origin(n, j + 1)]
            remote(arrays[n][0], block, g_send.at[n, j], g_recv.at[n, j], ahead).wait_recv()

            @pl.when(j < DEPTH - 2)
            def _(n=n, block=block):
                onward(n, j + 1, block).start()

        return 0

    lax.fori_loop(0, DEPTH - 1, step, 0)

    def drain(j, _):
        for n in range(4):
            onward(n, j, arrays[n][0]).wait_send()
        return 0

    lax.fori_loop(0, DEPTH - 1, drain, 0)

    def drain_chain(w, _):
        chain(lax.rem(w, 4), lax.div(w, 4), 1).wait_send()
        return 0

    lax.fori_loop(0, 14, drain_chain, 0)
    for n in range(4):
        pltpu.make_async_copy(arrays[n][0], arrays[n][1].at[z], own_sem.at[n]).wait()


def ring_attention(dec, enc, cot, wq, wk, wv, wo, bias):
    sds = jax.ShapeDtypeStruct
    return pl.pallas_call(
        ring_kernel,
        out_shape=[
            sds((8, 256, 256), BF16),
            sds((8, 256, 256), BF16),
            sds((8, 512, 256), BF16),
            sds((8, 512, 256), BF16),
        ],
        in_specs=[VMEM] * 8,
        out_specs=[ANY] * 4,
        scratch_shapes=[
            pltpu.VMEM((4, 4, 768, 256), BF16),
            pltpu.VMEM((4, 5, 768, 256), BF16),
            pltpu.VMEM((2, 768, 256), BF16),
            pltpu.VMEM((256, 256), BF16),
            pltpu.VMEM((256, 256), BF16),
            pltpu.VMEM((512, 256), BF16),
            pltpu.VMEM((512, 256), BF16),
            DMA((4, 4)),
            DMA((4, 4)),
            DMA((4, 7)),
            DMA((4, 7)),
            DMA((4,)),
        ],
        compiler_params=params(2, 56),
    )(dec, enc, cot, wq, wk, wv, wo, bias)


def scatter_kernel(
    qg,
    att,
    kg,
    vg,
    wq,
    wk,
    wv,
    wo,
    wg,
    wog,
    dec_out,
    out_out,
    enc_out,
    wg_out,
    wog_out,
    sib_out,
    sib_in,
    chain_out,
    chain_in,
    s_send,
    s_recv,
    c_send,
    c_recv,
    w_send,
    w_recv,
):
    z, s, t, x, y, core = place()
    sibling = {"seq": s + 1 - 2 * core}
    partner = {"tensor": 1 - t}
    position = (ring_position(0, x, y), ring_position(1, x, y))
    greet(plane_neighbours(x, y, core, s))
    swaps = (
        remote(wg, wg_out, w_send.at[0], w_recv.at[0], partner),
        remote(wog, wog_out, w_send.at[1], w_recv.at[1], partner),
    )

    def partial(k, offset, c):
        cx, cy = ring_chip(k // 2, lax.rem(position[k // 2] + offset, RING))
        sd, td = seq_tensor(cx, cy, c)
        if k < 2:
            rows = pl.ds(pl.multiple_of(sd * 128, 128), 128)
            return dot_t(qg[rows, :], wq[td]) if k == 0 else dot(att[rows, :], wo[td])
        stored = pl.ds(pl.multiple_of(sd * 256 + (k - 2) * 128, 128), 128)
        return dot_t(kg[stored, :], wk[td]) + dot_t(vg[stored, :], wv[td])

    def across(k, i):
        return remote(
            sib_out.at[k, i], sib_in.at[k, i], s_send.at[k, i], s_recv.at[k, i], sibling
        )

    def give(i):
        offset = 8 + (1 - 2 * lax.rem(i, 2)) * lax.div(i + 1, 2)
        for k in range(4):
            sib_out[k, i] = partial(k, offset, 1 - core).astype(BF16)
            across(k, i).start()

    def onward(k, way, j):
        device = ring_device(k // 2, position[k // 2] + 1 - 2 * way, core)
        return remote(
            chain_out.at[k, way, j],
            chain_in.at[k, way, j + 1],
            c_send.at[k, way, j],
            c_recv.at[k, way, j],
            device,
        )

    for k in range(4):
        for way in range(2):
            chain_in[k, way, 0] = jnp.zeros((128, 512), BF16)

    lax.fori_loop(0, 3, lambda i, _: (give(i), 0)[1], 0)
    for copy in swaps:
        copy.start()

    def step(j, _):
        def ahead(i, _):
            @pl.when(i < RING)
            def _():
                give(i)

            return 0

        lax.fori_loop(2 * j + 3, 2 * j + 5, ahead, 0)

        def way_step(way, _):
            for k in range(4):
                length = 8 - way if k % 2 == 0 else 7 + way
                distance = length - j

                @pl.when(distance > 0)
                def _(k=k, distance=distance):
                    m = 8 - distance
                    i = jnp.maximum(2 * m - 1 + way, 0)
                    total = partial(k, RING + (1 - 2 * way) * distance, core)
                    across(k, i).wait_recv()

                    @pl.when(j > 0)
                    def _():
                        onward(k, way, j - 1).wait_recv()

                    total = total + sib_in[k, i].astype(F32)
                    total = total + chain_in[k, way, j].astype(F32)
                    chain_out[k, way, j] = total.astype(BF16)
                    onward(k, way, j).start()

            return 0

        lax.fori_loop(0, 2, way_step, 0)
        return 0

    lax.fori_loop(0, 8, step, 0)

    outs = (
        dec_out,
        out_out,
        enc_out.at[pl.ds(0, 128)],
        enc_out.at[pl.ds(128, 128)],
    )
    for k in range(4):
        total = partial(k, RING, core)
        across(k, 15).wait_recv()
        total = total + sib_in[k, 15].astype(F32)
        for way in range(2):
            length = 8 - way if k % 2 == 0 else 7 + way
            onward(k, way, length - 1).wait_recv()
            total = total + chain_in[k, way, length].astype(F32)
        outs[k][...] = total

    def drain(i, _):
        for k in range(4):
            across(k, i).wait_send()
        return 0

    lax.fori_loop(0, RING, drain, 0)

    def drain_chain(j, _):
        for k in range(4):
            for way in range(2):
                onward(k, way, j).wait_send()
        return 0

    lax.fori_loop(0, 7, drain_chain, 0)
    for k in range(4):
        onward(k, k % 2, 7).wait_send()
    for copy in swaps:
        copy.wait()


def scatter_rows(qg, att, kg, vg, wq, wk, wv, wo, wg, wog):
    sds = jax.ShapeDtypeStruct
    return pl.pallas_call(
        scatter_kernel,
        out_shape=[
            sds((128, 512), F32),
            sds((128, 512), F32),
            sds((256, 512), F32),
            sds((3, 512, 256), BF16),
            sds((256, 512), BF16),
        ],
        in_specs=[VMEM] * 8 + [ANY] * 2,
        out_specs=[VMEM] * 3 + [ANY] * 2,
        scratch_shapes=[
            pltpu.VMEM((4, 16, 128, 512), BF16),
            pltpu.VMEM((4, 16, 128, 512), BF16),
            pltpu.VMEM((4, 2, 8, 128, 512), BF16),
            pltpu.VMEM((4, 2, 9, 128, 512), BF16),
            DMA((4, 16)),
            DMA((4, 16)),
            DMA((4, 2, 8)),
            DMA((4, 2, 8)),
            DMA((2,)),
            DMA((2,)),
        ],
        compiler_params=params(3, 56),
    )(qg, att, kg, vg, wq, wk, wv, wo, wg, wog)


def pack(*vectors):
    flat = jnp.concatenate(vectors)
    return jnp.pad(flat, (0, 1024 - flat.shape[0])).reshape(8, 128)


def body(
    hidden,
    dec_gain,
    neigh_states,
    enc_gain,
    w_query,
    w_key,
    w_value,
    w_out,
    neighbour_ids,
    neighbour_len,
    cotangent,
):
    t = lax.axis_index("tensor")
    rows = hidden.shape[0]
    dec_rows = hidden.astype(F32)
    enc_rows = neigh_states.astype(F32)
    (squares,) = small_sums(
        [pack(jnp.sum(dec_rows * dec_rows, axis=1), jnp.sum(enc_rows * enc_rows, axis=1))],
        ("st",),
        0,
    )
    scales = lax.rsqrt(squares.reshape(-1)[:384] / WIDTH + EPS)
    dec_scale, enc_scale = scales[:rows, None], scales[rows:, None]
    dec_hat = dec_rows * dec_scale
    enc_hat = enc_rows * enc_scale
    dec_local = (dec_hat * dec_gain).astype(BF16)
    enc_local = (enc_hat * enc_gain).astype(BF16)
    cot_all, dec_all, enc_all, wq, wk, wv, wo = gather_rows(
        cotangent, dec_local, enc_local, w_query, w_key, w_value, w_out
    )
    count = neighbour_ids.shape[0]
    inverse = jnp.sum(
        jnp.where(
            neighbour_ids[None, :] == jnp.arange(count, dtype=jnp.int32)[:, None],
            jnp.arange(count, dtype=jnp.int32)[None, :],
            0,
        ),
        axis=1,
    )
    dec_all, cot_all = reorder(inverse, dec_all, cot_all)
    slots = jnp.arange(128, dtype=jnp.int32)[None, :]
    bias = jnp.where(slots < neighbour_len[:, None], 0.0, -jnp.inf).astype(F32)
    att, qg, kg, vg = ring_attention(dec_all, enc_all, cot_all, wq, wk, wv, wo, bias)
    att, qg = att.reshape(2048, 256), qg.reshape(2048, 256)
    kg, vg = kg.reshape(4096, 256), vg.reshape(4096, 256)
    att_rows, qg_rows = reorder(neighbour_ids, att[None], qg[None])

    def weight(left, right):
        return jnp.einsum("tnf,nh->tfh", left, right, preferred_element_type=F32)

    grads = (weight(dec_all, qg), weight(enc_all, kg), weight(enc_all, vg))
    out_grad = jnp.einsum("nh,tnf->thf", att, cot_all, preferred_element_type=F32)

    def mine(g):
        return jnp.where(t == 0, g[0], g[1])

    def other(g):
        return jnp.where(t == 0, g[1], g[0]).astype(BF16)

    dec_input, out_total, enc_input, wg, wog = scatter_rows(
        qg_rows[0],
        att_rows[0],
        kg,
        vg,
        wq,
        wk,
        wv,
        wo,
        jnp.stack([other(g) for g in grads]),
        other(out_grad),
    )

    def join(own, got, axis):
        got = got.astype(F32)
        return jnp.where(
            t == 0, jnp.concatenate([own, got], axis), jnp.concatenate([got, own], axis)
        )

    weight_grads = [join(mine(g), wg[n], 1) for n, g in enumerate(grads)]
    out_weight_grad = join(mine(out_grad), wog, 0)
    layer_out = (dec_rows + out_total).astype(BF16)
    dec_scaled = dec_gain * dec_input
    enc_scaled = enc_gain * enc_input
    inner, gains = small_sums(
        [
            pack(jnp.sum(dec_scaled * dec_hat, axis=1), jnp.sum(enc_scaled * enc_hat, axis=1)),
            pack(jnp.sum(dec_input * dec_hat, axis=0), jnp.sum(enc_input * enc_hat, axis=0)),
        ],
        ("st", "seq"),
        4,
    )
    inner = inner.reshape(-1)[:384] / WIDTH
    gains = gains.reshape(-1)
    hidden_grad = cotangent.astype(F32) + dec_scale * (
        dec_scaled - dec_hat * inner[:rows, None]
    )
    neighbour_grad = enc_scale * (enc_scaled - enc_hat * inner[rows:, None])
    return (
        layer_out,
        hidden_grad,
        neighbour_grad,
        gains[:512],
        gains[512:],
        weight_grads[0],
        weight_grads[1],
        weight_grads[2],
        out_weight_grad,
    )


def solution(mesh):
    features = ("section", "tensor")
    rows = P("seq", features)
    vector = P(features)
    columns = P(features, "seq")
    return jax.shard_map(
        body,
        mesh=mesh,
        in_specs=(
            rows,
            vector,
            rows,
            vector,
            columns,
            columns,
            columns,
            rows,
            P(),
            P(),
            rows,
        ),
        out_specs=(rows, rows, rows, vector, vector, columns, columns, columns, rows),
        check_vma=False,
    )
```

```python
import functools

import jax
import jax.numpy as jnp
from jax import lax
from jax.experimental import pallas as pl
from jax.experimental.pallas import tpu as pltpu
from jax.sharding import PartitionSpec as P

F32 = jnp.float32
BF16 = jnp.bfloat16
MESH = pl.DeviceIdType.MESH
EPS = 1e-05
WIDTH = 8192
ANY = pl.BlockSpec(memory_space=pl.ANY)
VMEM = pl.BlockSpec(memory_space=pltpu.VMEM)
SMEM = pl.BlockSpec(memory_space=pltpu.SMEM)
DMA = pltpu.SemaphoreType.DMA
RING = 16
DEPTH = 8


def place():
    z = lax.axis_index("section")
    s = lax.axis_index("seq")
    t = lax.axis_index("tensor")
    x = lax.div(lax.rem(s, 8), 2)
    y = lax.div(s, 8) * 2 + t
    return z, s, t, x, y, lax.rem(s, 2)


def ring_position(ring, x, y):
    return (y if ring == 0 else x) * 4 + lax.rem(x + y, 4)


def ring_chip(ring, p):
    a = lax.div(p, 4)
    b = lax.rem(lax.rem(p, 4) + 4 - a, 4)
    return (b, a) if ring == 0 else (a, b)


def seq_tensor(x, y, core):
    return lax.div(y, 2) * 8 + x * 2 + core, lax.rem(y, 2)


def ring_device(ring, p, core):
    x, y = ring_chip(ring, lax.rem(p + RING, RING))
    s, t = seq_tensor(x, y, core)
    return {"seq": s, "tensor": t}


def remote(src, dst, send_sem, recv_sem, device):
    return pltpu.make_async_remote_copy(
        src_ref=src,
        dst_ref=dst,
        send_sem=send_sem,
        recv_sem=recv_sem,
        device_id=device,
        device_id_type=MESH,
    )


def greet(devices):
    barrier = pltpu.get_barrier_semaphore()
    for device in devices:
        pl.semaphore_signal(barrier, inc=1, device_id=device, device_id_type=MESH)
    pl.semaphore_wait(barrier, len(devices))


def plane_neighbours(x, y, core, s):
    p1, p2 = ring_position(0, x, y), ring_position(1, x, y)
    return [
        ring_device(0, p1 + 1, core),
        ring_device(0, p1 - 1, core),
        ring_device(1, p2 + 1, core),
        ring_device(1, p2 - 1, core),
        {"seq": s + 1 - 2 * core},
    ]


def params(cid, mib=None):
    return pltpu.CompilerParams(
        collective_id=cid,
        has_side_effects=True,
        vmem_limit_bytes=None if mib is None else mib * 1024 * 1024,
    )


def small_kernel(groups, *refs):
    n = len(groups)
    ins, outs, slots = refs[:n], refs[n : 2 * n], refs[2 * n : 3 * n]
    send, recv = refs[3 * n], refs[3 * n + 1]
    z, s, t, _, _, _ = place()

    def peer(group, r):
        if group == "st":
            g = lax.rem(z * 2 + t + r, 16)
            return {"section": lax.div(g, 2), "tensor": lax.rem(g, 2)}, g
        g = lax.rem(s + r, 16)
        return {"seq": g}, g

    barrier = pltpu.get_barrier_semaphore()
    for group in groups:

        def hello(r, _, group=group):
            pl.semaphore_signal(
                barrier, inc=1, device_id=peer(group, r)[0], device_id_type=MESH
            )
            return 0

        lax.fori_loop(1, 16, hello, 0)
    pl.semaphore_wait(barrier, 15 * n)
    for k, group in enumerate(groups):
        mine = peer(group, 0)[1]

        def push(r, _, k=k, group=group, mine=mine):
            device, _g = peer(group, r)
            remote(
                ins[k], slots[k].at[mine], send.at[k, r], recv.at[k, mine], device
            ).start()
            return 0

        lax.fori_loop(1, 16, push, 0)
        slots[k][mine] = ins[k][...]
    for k, group in enumerate(groups):
        mine = peer(group, 0)[1]

        def take(r, _, k=k, group=group, mine=mine):
            device, g = peer(group, r)
            remote(ins[k], slots[k].at[g], send.at[k, r], recv.at[k, g], device).wait_recv()
            return 0

        lax.fori_loop(1, 16, take, 0)
        total = slots[k][0]
        for g in range(1, 16):
            total = total + slots[k][g]
        outs[k][...] = total
    for k, group in enumerate(groups):
        mine = peer(group, 0)[1]

        def drain(r, _, k=k, group=group, mine=mine):
            device, _g = peer(group, r)
            remote(
                ins[k], slots[k].at[mine], send.at[k, r], recv.at[k, mine], device
            ).wait_send()
            return 0

        lax.fori_loop(1, 16, drain, 0)


def small_sums(arrays, groups, cid):
    n = len(groups)
    return pl.pallas_call(
        functools.partial(small_kernel, groups),
        out_shape=[jax.ShapeDtypeStruct((8, 128), F32)] * n,
        in_specs=[VMEM] * n,
        out_specs=[VMEM] * n,
        scratch_shapes=[pltpu.VMEM((16, 8, 128), F32)] * n + [DMA((n, 16)), DMA((n, 16))],
        compiler_params=params(cid),
    )(*arrays)


def reorder_kernel(index, *refs):
    n = len(refs) // 2

    def move(j, _):
        src = pl.ds(pl.multiple_of(index[j] * 64, 64), 64)
        dst = pl.ds(pl.multiple_of(j * 64, 64), 64)
        for k in range(n):
            refs[n + k][dst, :] = refs[k][src, :]
        return 0

    lax.fori_loop(0, 32, move, 0)


def reorder(index, *arrays):
    n = len(arrays)
    return pl.pallas_call(
        reorder_kernel,
        out_shape=[jax.ShapeDtypeStruct(a.shape, a.dtype) for a in arrays],
        in_specs=[SMEM] + [VMEM] * n,
        out_specs=[VMEM] * n,
    )(index, *arrays)


def dot(a, b):
    return jnp.dot(a, b, preferred_element_type=F32)


def dot_t(a, b):
    return lax.dot_general(a, b, (((1,), (1,)), ((), ())), preferred_element_type=F32)


def t_dot(a, b):
    return lax.dot_general(a, b, (((0,), (0,)), ((), ())), preferred_element_type=F32)


def split(a):
    high = a.astype(BF16)
    return high, (a - high.astype(F32)).astype(BF16)


def attend(q, a, k, v, bias):
    scale = 128 ** (-0.5)
    scores = dot_t(q, k) * scale + bias
    top = jnp.max(scores, axis=1, keepdims=True)
    expo = jnp.exp(scores - top)
    probs = expo / jnp.sum(expo, axis=1, keepdims=True)
    low = probs.astype(BF16)
    attended = dot(low, v).astype(BF16)
    value_grad = t_dot(low, a).astype(BF16)
    prob_grad = dot_t(a, v)
    inner = jnp.sum(probs * prob_grad, axis=1, keepdims=True)
    score_grad = probs * (prob_grad - inner) * scale
    high, rest = split(score_grad)
    query_grad = (dot(high, k) + dot(rest, k)).astype(BF16)
    key_grad = (t_dot(high, q) + t_dot(rest, q)).astype(BF16)
    return attended, query_grad, key_grad, value_grad


def hops(k, way):
    return 8 - way if k % 2 == 0 else 7 + way


def front_kernel(
    cot,
    dec,
    enc,
    wq_own,
    wk_own,
    wv_own,
    wo_own,
    bias,
    inverse,
    cot_all,
    dec_all,
    enc_all,
    wq,
    wk,
    wv,
    wo,
    att_all,
    qg_all,
    kg_all,
    vg_all,
    cot_v,
    dec_v,
    enc_v,
    sendb,
    recvb,
    fin,
    p_send,
    p_recv,
    s_send,
    s_recv,
    own_sem,
    w_send,
    w_recv,
    w_own,
    out_sem,
    send,
    recv,
    g_send,
    g_recv,
):
    z, s, t, x, y, core = place()
    sibling = {"seq": s + 1 - 2 * core}
    partner = {"tensor": 1 - t}
    ahead = {"section": lax.rem(z + 1, DEPTH)}
    behind = {"section": lax.rem(z + DEPTH - 1, DEPTH)}
    greet(plane_neighbours(x, y, core, s) + [ahead, behind])


    def slot(k, chip, c):
        so, to = seq_tensor(chip[0], chip[1], c)
        if k == 0:
            return cot_v.at[to, pl.ds(so * 2, 2)]
        if k == 1:
            return dec_v.at[to, pl.ds(so * 2, 2)]
        return enc_v.at[to, pl.ds(pl.multiple_of(so * 256 + (k - 2) * 128, 128), 128)]

    sources = (cot, dec, enc.at[pl.ds(0, 128)], enc.at[pl.ds(128, 128)])
    position = (ring_position(0, x, y), ring_position(1, x, y))

    def origin(k, way, j):
        return ring_chip(
            k // 2, lax.rem(position[k // 2] + RING - (1 - 2 * way) * j, RING)
        )

    def onward(k, way, j, src):
        device = ring_device(k // 2, position[k // 2] + 1 - 2 * way, core)
        block = slot(k, origin(k, way, j), core)
        return remote(src, block, p_send.at[k, way, j], p_recv.at[k, way, j], device)

    def arrival(k, way, j):
        block = slot(k, origin(k, way, j + 1), core)
        return remote(block, block, p_send.at[k, way, j], p_recv.at[k, way, j], sibling), block

    def across(k, way, j, src, c):
        block = slot(k, origin(k, way, j), c)
        return remote(src, block, s_send.at[k, way, j], s_recv.at[k, way, j], sibling)

    def keep(k):
        return pltpu.make_async_copy(sources[k], slot(k, (x, y), core), own_sem.at[k])

    for k in range(4):
        for way in range(2):
            onward(k, way, 0, sources[k]).start()
    half = pl.ds(pl.multiple_of(t * 256, 256), 256)
    rest = pl.ds(pl.multiple_of((1 - t) * 256, 256), 256)
    weights = ((wq_own, wq), (wk_own, wk), (wv_own, wv))
    swaps = [
        remote(w.at[:, rest], w_all.at[t], w_send.at[n], w_recv.at[n], partner)
        for n, (w, w_all) in enumerate(weights)
    ] + [remote(wo_own.at[rest, :], wo.at[t], w_send.at[3], w_recv.at[3], partner)]
    keeps = [
        pltpu.make_async_copy(w.at[:, half], w_all.at[t], w_own.at[n])
        for n, (w, w_all) in enumerate(weights)
    ] + [pltpu.make_async_copy(wo_own.at[half, :], wo.at[t], w_own.at[3])]
    for copy in swaps:
        copy.start()
    for k in range(4):
        across(k, 0, 0, sources[k], core).start()
        keep(k).start()
    for copy in keeps:
        copy.start()

    def gather_step(j, _):
        for way in range(2):
            for k in range(4):

                @pl.when(j < hops(k, way))
                def _(k=k, way=way):
                    wait, block = arrival(k, way, j)
                    wait.wait_recv()

                    @pl.when(j + 1 < hops(k, way))
                    def _():
                        onward(k, way, j + 1, block).start()

                    across(k, way, j + 1, block, core).start()

        return 0

    lax.fori_loop(0, 8, gather_step, 0)

    def zero(n, _):
        recvb[n, 0] = jnp.zeros((768, 256), BF16)
        return 0

    lax.fori_loop(0, 4, zero, 0)

    def gather_end(j, _):
        for way in range(2):
            for k in range(4):

                @pl.when(j < hops(k, way))
                def _(k=k, way=way):
                    onward(k, way, j, sources[k]).wait_send()
                    across(k, way, j + 1, sources[k], core).wait_send()
                    across(k, way, j + 1, sources[k], 1 - core).wait_recv()

        return 0

    lax.fori_loop(0, 8, gather_end, 0)
    for k in range(4):
        across(k, 0, 0, sources[k], core).wait_send()
        across(k, 0, 0, sources[k], 1 - core).wait_recv()
        keep(k).wait()
    for copy in keeps:
        copy.wait()
    for copy in swaps:
        copy.wait_send()
    for n, (w, w_all) in enumerate(weights):
        remote(w.at[:, rest], w_all.at[1 - t], w_send.at[n], w_recv.at[n], partner).wait_recv()
    remote(wo_own.at[rest, :], wo.at[1 - t], w_send.at[3], w_recv.at[3], partner).wait_recv()
    stores = [
        pltpu.make_async_copy(src, dst, out_sem.at[n])
        for n, (src, dst) in enumerate(((cot_v, cot_all), (dec_v, dec_all), (enc_v, enc_all)))
    ]
    for copy in stores:
        copy.start()


    def partial(d, h):
        j = d * 4 + h * 2
        b0, b1 = inverse[j], inverse[j + 1]
        stored = pl.ds(pl.multiple_of(j * 128, 256), 256)
        q = a = k = v = 0.0
        for f in range(2):
            rows = jnp.concatenate([dec_v[f, b0], dec_v[f, b1]], axis=0)
            q = q + dot(rows, wq[f])
            rows = jnp.concatenate([cot_v[f, b0], cot_v[f, b1]], axis=0)
            a = a + dot_t(rows, wo[f])
            rows = enc_v[f, stored, :]
            k = k + dot(rows, wk[f])
            v = v + dot(rows, wv[f])
        return ((0, 128, q), (128, 256, a), (256, 512, k), (512, 768, v))

    def stream(n):
        h = lax.rem(n, 2)
        way = lax.rem(h + lax.div(n, 2), 2)
        return h, 1 - 2 * way, 4 - lax.div(n, 2)

    def chain(n, t, sign):
        device = {"section": lax.rem(z + DEPTH + sign, DEPTH)}
        return remote(
            sendb.at[n, t], recvb.at[n, t + 1], send.at[n, t], recv.at[n, t], device
        )

    def item(w, _):
        n, t = lax.rem(w, 4), lax.div(w, 4)
        h, sign, length = stream(n)
        parts = partial(lax.rem(z + DEPTH + sign * (length - t), DEPTH), h)

        @pl.when(t > 0)
        def _():
            chain(n, t - 1, sign).wait_recv()

        for lo, hi, part in parts:
            sendb[n, t, lo:hi] = (part + recvb[n, t, lo:hi].astype(F32)).astype(BF16)
        chain(n, t, sign).start()
        return 0

    lax.fori_loop(0, 14, item, 0)

    def last(h, _):
        parts = partial(z, h)
        chain(h, 3, 1).wait_recv()
        chain(h + 2, 2, 1).wait_recv()
        for lo, hi, part in parts:
            total = part + recvb[h, 4, lo:hi].astype(F32) + recvb[h + 2, 3, lo:hi].astype(F32)
            fin[h, lo:hi] = total.astype(BF16)
        return 0

    lax.fori_loop(0, 2, last, 0)

    for h in range(2):
        for u in range(2):
            n = h * 2 + u
            for g in range(2):
                head = slice(g * 128, (g + 1) * 128)
                attended, query_grad, key_grad, value_grad = attend(
                    fin[h, u * 64 : (u + 1) * 64, head],
                    fin[h, 128 + u * 64 : 128 + (u + 1) * 64, head],
                    fin[h, 256 + u * 128 : 256 + (u + 1) * 128, head],
                    fin[h, 512 + u * 128 : 512 + (u + 1) * 128, head],
                    bias[pl.ds(z * 4 + n, 1), :],
                )
                att_all[z, n * 64 : (n + 1) * 64, head] = attended
                qg_all[z, n * 64 : (n + 1) * 64, head] = query_grad
                kg_all[z, n * 128 : (n + 1) * 128, head] = key_grad
                vg_all[z, n * 128 : (n + 1) * 128, head] = value_grad

    arrays = ((kg_all, 1), (vg_all, -1), (att_all, 1), (qg_all, -1))

    def ring_block(n, j):
        return arrays[n][0].at[lax.rem(z + DEPTH - arrays[n][1] * j, DEPTH)]

    def ring_copy(n, j):
        device = ahead if arrays[n][1] == 1 else behind
        block = ring_block(n, j)
        return remote(block, block, g_send.at[n, j], g_recv.at[n, j], device)

    for n in range(4):
        ring_copy(n, 0).start()

    def ring_step(j, _):
        for n in range(4):
            block = ring_block(n, j + 1)
            remote(block, block, g_send.at[n, j], g_recv.at[n, j], ahead).wait_recv()

            @pl.when(j < DEPTH - 2)
            def _(n=n):
                ring_copy(n, j + 1).start()

        return 0

    lax.fori_loop(0, DEPTH - 1, ring_step, 0)

    def ring_end(j, _):
        for n in range(4):
            ring_copy(n, j).wait_send()
        return 0

    lax.fori_loop(0, DEPTH - 1, ring_end, 0)

    def chain_end(w, _):
        chain(lax.rem(w, 4), lax.div(w, 4), 1).wait_send()
        return 0

    lax.fori_loop(0, 14, chain_end, 0)
    for copy in stores:
        copy.wait()


def front(cot, dec, enc, wq, wk, wv, wo, bias, inverse):
    sds = jax.ShapeDtypeStruct
    return pl.pallas_call(
        front_kernel,
        out_shape=[
            sds((2, 32, 64, 512), BF16),
            sds((2, 32, 64, 512), BF16),
            sds((2, 4096, 512), BF16),
            sds((2, 512, 256), BF16),
            sds((2, 512, 256), BF16),
            sds((2, 512, 256), BF16),
            sds((2, 256, 512), BF16),
            sds((8, 256, 256), BF16),
            sds((8, 256, 256), BF16),
            sds((8, 512, 256), BF16),
            sds((8, 512, 256), BF16),
        ],
        in_specs=[VMEM] * 8 + [SMEM],
        out_specs=[ANY] * 3 + [VMEM] * 8,
        scratch_shapes=[
            pltpu.VMEM((2, 32, 64, 512), BF16),
            pltpu.VMEM((2, 32, 64, 512), BF16),
            pltpu.VMEM((2, 4096, 512), BF16),
            pltpu.VMEM((4, 4, 768, 256), BF16),
            pltpu.VMEM((4, 5, 768, 256), BF16),
            pltpu.VMEM((2, 768, 256), BF16),
            DMA((4, 2, 8)),
            DMA((4, 2, 8)),
            DMA((4, 2, 9)),
            DMA((4, 2, 9)),
            DMA((4,)),
            DMA((4,)),
            DMA((4,)),
            DMA((4,)),
            DMA((3,)),
            DMA((4, 4)),
            DMA((4, 4)),
            DMA((4, 7)),
            DMA((4, 7)),
        ],
        compiler_params=params(1, 60),
    )(cot, dec, enc, wq, wk, wv, wo, bias, inverse)


def scatter_kernel(
    qg,
    att,
    kg,
    vg,
    wq,
    wk,
    wv,
    wo,
    wg,
    wog,
    dec_out,
    out_out,
    enc_out,
    wg_out,
    wog_out,
    sib_out,
    sib_in,
    chain_out,
    chain_in,
    mine,
    s_send,
    s_recv,
    c_send,
    c_recv,
    w_send,
    w_recv,
):
    z, s, t, x, y, core = place()
    sibling = {"seq": s + 1 - 2 * core}
    partner = {"tensor": 1 - t}
    position = (ring_position(0, x, y), ring_position(1, x, y))
    greet(plane_neighbours(x, y, core, s))
    swaps = (
        remote(wg, wg_out, w_send.at[0], w_recv.at[0], partner),
        remote(wog, wog_out, w_send.at[1], w_recv.at[1], partner),
    )

    def both(ref, sd, size):
        return jnp.concatenate(
            [
                ref[pl.ds(pl.multiple_of((sd + c) * size, 128), size), :]
                for c in (core, 1 - core)
            ],
            axis=0,
        )

    def across(k, i):
        return remote(
            sib_out.at[k, i], sib_in.at[k, i], s_send.at[k, i], s_recv.at[k, i], sibling
        )

    def give(i):
        offset = 8 + (1 - 2 * lax.rem(i, 2)) * lax.div(i + 1, 2)
        place_of = lax.rem(i, 8)
        cx, cy = ring_chip(0, lax.rem(position[0] + offset, RING))
        sd, td = seq_tensor(cx, cy, 0)
        for k, rows, w in ((0, qg, wq), (1, att, wo)):
            total = dot(both(rows, sd, 128), w[td])
            sib_out[k, i] = total[128:].astype(BF16)
            across(k, i).start()
            mine[k, place_of] = total[:128]
        cx, cy = ring_chip(1, lax.rem(position[1] + offset, RING))
        sd, td = seq_tensor(cx, cy, 0)
        total = dot(both(kg, sd, 256), wk[td]) + dot(both(vg, sd, 256), wv[td])
        for k in (2, 3):
            lo = (k - 2) * 128
            sib_out[k, i] = total[256 + lo : 384 + lo].astype(BF16)
            across(k, i).start()
            mine[k, place_of] = total[lo : 128 + lo]

    def onward(k, way, j):
        device = ring_device(k // 2, position[k // 2] + 1 - 2 * way, core)
        return remote(
            chain_out.at[k, way, j],
            chain_in.at[k, way, j + 1],
            c_send.at[k, way, j],
            c_recv.at[k, way, j],
            device,
        )

    for k in range(4):
        for way in range(2):
            chain_in[k, way, 0] = jnp.zeros((128, 512), BF16)

    lax.fori_loop(0, 3, lambda i, _: (give(i), 0)[1], 0)
    for copy in swaps:
        copy.start()

    def step(j, _):
        def ahead(i, _):
            @pl.when(i < RING)
            def _():
                give(i)

            return 0

        lax.fori_loop(2 * j + 3, 2 * j + 5, ahead, 0)

        def way_step(way, _):
            for k in range(4):
                length = 8 - way if k % 2 == 0 else 7 + way
                distance = length - j

                @pl.when(distance > 0)
                def _(k=k, distance=distance):
                    m = 8 - distance
                    i = jnp.maximum(2 * m - 1 + way, 0)
                    across(k, i).wait_recv()

                    @pl.when(j > 0)
                    def _():
                        onward(k, way, j - 1).wait_recv()

                    total = mine[k, lax.rem(i, 8)] + sib_in[k, i].astype(F32)
                    total = total + chain_in[k, way, j].astype(F32)
                    chain_out[k, way, j] = total.astype(BF16)
                    onward(k, way, j).start()

            return 0

        lax.fori_loop(0, 2, way_step, 0)
        return 0

    lax.fori_loop(0, 8, step, 0)

    outs = (
        dec_out,
        out_out,
        enc_out.at[pl.ds(0, 128)],
        enc_out.at[pl.ds(128, 128)],
    )
    for k in range(4):
        across(k, 15).wait_recv()
        total = mine[k, 7] + sib_in[k, 15].astype(F32)
        for way in range(2):
            length = 8 - way if k % 2 == 0 else 7 + way
            onward(k, way, length - 1).wait_recv()
            total = total + chain_in[k, way, length].astype(F32)
        outs[k][...] = total

    def drain(i, _):
        for k in range(4):
            across(k, i).wait_send()
        return 0

    lax.fori_loop(0, RING, drain, 0)

    def drain_chain(j, _):
        for k in range(4):
            for way in range(2):
                onward(k, way, j).wait_send()
        return 0

    lax.fori_loop(0, 7, drain_chain, 0)
    for k in range(4):
        onward(k, k % 2, 7).wait_send()
    for copy in swaps:
        copy.wait()


def scatter_rows(qg, att, kg, vg, wq, wk, wv, wo, wg, wog):
    sds = jax.ShapeDtypeStruct
    return pl.pallas_call(
        scatter_kernel,
        out_shape=[
            sds((128, 512), F32),
            sds((128, 512), F32),
            sds((256, 512), F32),
            sds((3, 512, 256), BF16),
            sds((256, 512), BF16),
        ],
        in_specs=[VMEM] * 8 + [ANY] * 2,
        out_specs=[VMEM] * 3 + [ANY] * 2,
        scratch_shapes=[
            pltpu.VMEM((4, 16, 128, 512), BF16),
            pltpu.VMEM((4, 16, 128, 512), BF16),
            pltpu.VMEM((4, 2, 8, 128, 512), BF16),
            pltpu.VMEM((4, 2, 9, 128, 512), BF16),
            pltpu.VMEM((4, 8, 128, 512), F32),
            DMA((4, 16)),
            DMA((4, 16)),
            DMA((4, 2, 8)),
            DMA((4, 2, 8)),
            DMA((2,)),
            DMA((2,)),
        ],
        compiler_params=params(2, 60),
    )(qg, att, kg, vg, wq, wk, wv, wo, wg, wog)


def pack(*vectors):
    flat = jnp.concatenate(vectors)
    return jnp.pad(flat, (0, 1024 - flat.shape[0])).reshape(8, 128)


def body(
    hidden,
    dec_gain,
    neigh_states,
    enc_gain,
    w_query,
    w_key,
    w_value,
    w_out,
    neighbour_ids,
    neighbour_len,
    cotangent,
):
    t = lax.axis_index("tensor")
    rows = hidden.shape[0]
    dec_rows = hidden.astype(F32)
    enc_rows = neigh_states.astype(F32)
    (squares,) = small_sums(
        [pack(jnp.sum(dec_rows * dec_rows, axis=1), jnp.sum(enc_rows * enc_rows, axis=1))],
        ("st",),
        0,
    )
    scales = lax.rsqrt(squares.reshape(-1)[:384] / WIDTH + EPS)
    dec_scale, enc_scale = scales[:rows, None], scales[rows:, None]
    dec_hat = dec_rows * dec_scale
    enc_hat = enc_rows * enc_scale
    dec_local = (dec_hat * dec_gain).astype(BF16)
    enc_local = (enc_hat * enc_gain).astype(BF16)
    count = neighbour_ids.shape[0]
    inverse = jnp.sum(
        jnp.where(
            neighbour_ids[None, :] == jnp.arange(count, dtype=jnp.int32)[:, None],
            jnp.arange(count, dtype=jnp.int32)[None, :],
            0,
        ),
        axis=1,
    )
    slots = jnp.arange(128, dtype=jnp.int32)[None, :]
    bias = jnp.where(slots < neighbour_len[:, None], 0.0, -jnp.inf).astype(F32)
    cot_all, dec_all, enc_all, wq, wk, wv, wo, att, qg, kg, vg = front(
        cotangent.reshape(2, 64, 512),
        dec_local.reshape(2, 64, 512),
        enc_local,
        w_query,
        w_key,
        w_value,
        w_out,
        bias,
        inverse,
    )
    cot_all, dec_all = cot_all.reshape(2, 2048, 512), dec_all.reshape(2, 2048, 512)
    att, qg = att.reshape(2048, 256), qg.reshape(2048, 256)
    kg, vg = kg.reshape(4096, 256), vg.reshape(4096, 256)
    att, qg = reorder(neighbour_ids, att, qg)

    def weight(left, right):
        return jnp.einsum("tnf,nh->tfh", left, right, preferred_element_type=F32)

    grads = (weight(dec_all, qg), weight(enc_all, kg), weight(enc_all, vg))
    out_grad = jnp.einsum("nh,tnf->thf", att, cot_all, preferred_element_type=F32)

    def mine(g):
        return jnp.where(t == 0, g[0], g[1])

    def other(g):
        return jnp.where(t == 0, g[1], g[0]).astype(BF16)

    dec_input, out_total, enc_input, wg, wog = scatter_rows(
        qg,
        att,
        kg,
        vg,
        jnp.swapaxes(wq, 1, 2),
        jnp.swapaxes(wk, 1, 2),
        jnp.swapaxes(wv, 1, 2),
        wo,
        jnp.stack([other(g) for g in grads]),
        other(out_grad),
    )

    def join(own, got, axis):
        got = got.astype(F32)
        return jnp.where(
            t == 0, jnp.concatenate([own, got], axis), jnp.concatenate([got, own], axis)
        )

    weight_grads = [join(mine(g), wg[n], 1) for n, g in enumerate(grads)]
    out_weight_grad = join(mine(out_grad), wog, 0)
    layer_out = (dec_rows + out_total).astype(BF16)
    dec_scaled = dec_gain * dec_input
    enc_scaled = enc_gain * enc_input
    inner, gains = small_sums(
        [
            pack(jnp.sum(dec_scaled * dec_hat, axis=1), jnp.sum(enc_scaled * enc_hat, axis=1)),
            pack(jnp.sum(dec_input * dec_hat, axis=0), jnp.sum(enc_input * enc_hat, axis=0)),
        ],
        ("st", "seq"),
        3,
    )
    inner = inner.reshape(-1)[:384] / WIDTH
    gains = gains.reshape(-1)
    hidden_grad = cotangent.astype(F32) + dec_scale * (
        dec_scaled - dec_hat * inner[:rows, None]
    )
    neighbour_grad = enc_scale * (enc_scaled - enc_hat * inner[rows:, None])
    return (
        layer_out,
        hidden_grad,
        neighbour_grad,
        gains[:512],
        gains[512:],
        weight_grads[0],
        weight_grads[1],
        weight_grads[2],
        out_weight_grad,
    )


def solution(mesh):
    features = ("section", "tensor")
    rows = P("seq", features)
    vector = P(features)
    columns = P(features, "seq")
    return jax.shard_map(
        body,
        mesh=mesh,
        in_specs=(
            rows,
            vector,
            rows,
            vector,
            columns,
            columns,
            columns,
            rows,
            P(),
            P(),
            rows,
        ),
        out_specs=(rows, rows, rows, vector, vector, columns, columns, columns, rows),
        check_vma=False,
    )
```

```python
import functools

import jax
import jax.numpy as jnp
from jax import lax
from jax.experimental import pallas as pl
from jax.experimental.pallas import tpu as pltpu
from jax.sharding import PartitionSpec as P

F32 = jnp.float32
BF16 = jnp.bfloat16
MESH = pl.DeviceIdType.MESH
EPS = 1e-05
WIDTH = 8192
ANY = pl.BlockSpec(memory_space=pl.ANY)
VMEM = pl.BlockSpec(memory_space=pltpu.VMEM)
SMEM = pl.BlockSpec(memory_space=pltpu.SMEM)
DMA = pltpu.SemaphoreType.DMA
RING = 16
DEPTH = 8


def place():
    z = lax.axis_index("section")
    s = lax.axis_index("seq")
    t = lax.axis_index("tensor")
    x = lax.div(lax.rem(s, 8), 2)
    y = lax.div(s, 8) * 2 + t
    return z, s, t, x, y, lax.rem(s, 2)


def ring_position(ring, x, y):
    return (y if ring == 0 else x) * 4 + lax.rem(x + y, 4)


def ring_chip(ring, p):
    a = lax.div(p, 4)
    b = lax.rem(lax.rem(p, 4) + 4 - a, 4)
    return (b, a) if ring == 0 else (a, b)


def seq_tensor(x, y, core):
    return lax.div(y, 2) * 8 + x * 2 + core, lax.rem(y, 2)


def ring_device(ring, p, core):
    x, y = ring_chip(ring, lax.rem(p + RING, RING))
    s, t = seq_tensor(x, y, core)
    return {"seq": s, "tensor": t}


def remote(src, dst, send_sem, recv_sem, device):
    return pltpu.make_async_remote_copy(
        src_ref=src,
        dst_ref=dst,
        send_sem=send_sem,
        recv_sem=recv_sem,
        device_id=device,
        device_id_type=MESH,
    )


def greet(devices):
    barrier = pltpu.get_barrier_semaphore()
    for device in devices:
        pl.semaphore_signal(barrier, inc=1, device_id=device, device_id_type=MESH)
    pl.semaphore_wait(barrier, len(devices))


def plane_neighbours(x, y, core, s):
    p1, p2 = ring_position(0, x, y), ring_position(1, x, y)
    return [
        ring_device(0, p1 + 1, core),
        ring_device(0, p1 - 1, core),
        ring_device(1, p2 + 1, core),
        ring_device(1, p2 - 1, core),
        {"seq": s + 1 - 2 * core},
    ]


def ring_neighbours(z):
    return [
        {"section": lax.rem(z + 1, DEPTH)},
        {"section": lax.rem(z + DEPTH - 1, DEPTH)},
    ]


def params(cid, mib=None):
    return pltpu.CompilerParams(
        collective_id=cid,
        has_side_effects=True,
        vmem_limit_bytes=None if mib is None else mib * 1024 * 1024,
    )


def small_kernel(groups, *refs):
    n = len(groups)
    ins, outs, slots = refs[:n], refs[n : 2 * n], refs[2 * n : 3 * n]
    send, recv = refs[3 * n], refs[3 * n + 1]
    z, s, t, _, _, _ = place()

    def peer(group, r):
        if group == "st":
            g = lax.rem(z * 2 + t + r, 16)
            return {"section": lax.div(g, 2), "tensor": lax.rem(g, 2)}, g
        g = lax.rem(s + r, 16)
        return {"seq": g}, g

    barrier = pltpu.get_barrier_semaphore()
    for group in groups:

        def hello(r, _, group=group):
            pl.semaphore_signal(
                barrier, inc=1, device_id=peer(group, r)[0], device_id_type=MESH
            )
            return 0

        lax.fori_loop(1, 16, hello, 0)
    pl.semaphore_wait(barrier, 15 * n)
    for k, group in enumerate(groups):
        mine = peer(group, 0)[1]

        def push(r, _, k=k, group=group, mine=mine):
            device, _g = peer(group, r)
            remote(
                ins[k], slots[k].at[mine], send.at[k, r], recv.at[k, mine], device
            ).start()
            return 0

        lax.fori_loop(1, 16, push, 0)
        slots[k][mine] = ins[k][...]
    for k, group in enumerate(groups):
        mine = peer(group, 0)[1]

        def take(r, _, k=k, group=group, mine=mine):
            device, g = peer(group, r)
            remote(ins[k], slots[k].at[g], send.at[k, r], recv.at[k, g], device).wait_recv()
            return 0

        lax.fori_loop(1, 16, take, 0)
        total = slots[k][0]
        for g in range(1, 16):
            total = total + slots[k][g]
        outs[k][...] = total
    for k, group in enumerate(groups):
        mine = peer(group, 0)[1]

        def drain(r, _, k=k, group=group, mine=mine):
            device, _g = peer(group, r)
            remote(
                ins[k], slots[k].at[mine], send.at[k, r], recv.at[k, mine], device
            ).wait_send()
            return 0

        lax.fori_loop(1, 16, drain, 0)


def small_sums(arrays, groups, cid):
    n = len(groups)
    return pl.pallas_call(
        functools.partial(small_kernel, groups),
        out_shape=[jax.ShapeDtypeStruct((8, 128), F32)] * n,
        in_specs=[VMEM] * n,
        out_specs=[VMEM] * n,
        scratch_shapes=[pltpu.VMEM((16, 8, 128), F32)] * n + [DMA((n, 16)), DMA((n, 16))],
        compiler_params=params(cid),
    )(*arrays)


def dot(a, b):
    return jnp.dot(a, b, preferred_element_type=F32)


def dot_t(a, b):
    return lax.dot_general(a, b, (((1,), (1,)), ((), ())), preferred_element_type=F32)


def t_dot(a, b):
    return lax.dot_general(a, b, (((0,), (0,)), ((), ())), preferred_element_type=F32)


def split(a):
    high = a.astype(BF16)
    return high, (a - high.astype(F32)).astype(BF16)


def attend(q, a, k, v, bias):
    scale = 128 ** (-0.5)
    scores = dot_t(q, k) * scale + bias
    top = jnp.max(scores, axis=1, keepdims=True)
    expo = jnp.exp(scores - top)
    probs = expo / jnp.sum(expo, axis=1, keepdims=True)
    low = probs.astype(BF16)
    attended = dot(low, v).astype(BF16)
    value_grad = t_dot(low, a).astype(BF16)
    prob_grad = dot_t(a, v)
    inner = jnp.sum(probs * prob_grad, axis=1, keepdims=True)
    score_grad = probs * (prob_grad - inner) * scale
    high, rest = split(score_grad)
    query_grad = (dot(high, k) + dot(rest, k)).astype(BF16)
    key_grad = (t_dot(high, q) + t_dot(rest, q)).astype(BF16)
    return attended, query_grad, key_grad, value_grad


def hops(k, way):
    return 8 - way if k % 2 == 0 else 7 + way


def front_kernel(
    cot,
    dec,
    enc,
    wq_own,
    wk_own,
    wv_own,
    wo_own,
    bias,
    inverse,
    cot_all,
    dec_all,
    enc_all,
    wq,
    wk,
    wv,
    wo,
    att,
    qg,
    kg,
    vg,
    cot_v,
    dec_v,
    enc_v,
    sendb,
    recvb,
    fin,
    p_send,
    p_recv,
    s_send,
    s_recv,
    own_sem,
    w_send,
    w_recv,
    w_own,
    out_sem,
    send,
    recv,
):
    z, s, t, x, y, core = place()
    sibling = {"seq": s + 1 - 2 * core}
    partner = {"tensor": 1 - t}
    greet(plane_neighbours(x, y, core, s) + ring_neighbours(z))


    def slot(k, chip, c):
        so, to = seq_tensor(chip[0], chip[1], c)
        if k == 0:
            return cot_v.at[to, pl.ds(so * 2, 2)]
        if k == 1:
            return dec_v.at[to, pl.ds(so * 2, 2)]
        return enc_v.at[to, pl.ds(pl.multiple_of(so * 256 + (k - 2) * 128, 128), 128)]

    sources = (cot, dec, enc.at[pl.ds(0, 128)], enc.at[pl.ds(128, 128)])
    position = (ring_position(0, x, y), ring_position(1, x, y))

    def origin(k, way, j):
        return ring_chip(
            k // 2, lax.rem(position[k // 2] + RING - (1 - 2 * way) * j, RING)
        )

    def onward(k, way, j, src):
        device = ring_device(k // 2, position[k // 2] + 1 - 2 * way, core)
        block = slot(k, origin(k, way, j), core)
        return remote(src, block, p_send.at[k, way, j], p_recv.at[k, way, j], device)

    def arrival(k, way, j):
        block = slot(k, origin(k, way, j + 1), core)
        return remote(block, block, p_send.at[k, way, j], p_recv.at[k, way, j], sibling), block

    def across(k, way, j, src, c):
        block = slot(k, origin(k, way, j), c)
        return remote(src, block, s_send.at[k, way, j], s_recv.at[k, way, j], sibling)

    def keep(k):
        return pltpu.make_async_copy(sources[k], slot(k, (x, y), core), own_sem.at[k])

    for k in (0, 2, 1, 3):
        for way in range(2):
            onward(k, way, 0, sources[k]).start()
    half = pl.ds(pl.multiple_of(t * 256, 256), 256)
    rest = pl.ds(pl.multiple_of((1 - t) * 256, 256), 256)
    weights = ((wq_own, wq), (wk_own, wk), (wv_own, wv))
    swaps = [
        remote(w.at[:, rest], w_all.at[t], w_send.at[n], w_recv.at[n], partner)
        for n, (w, w_all) in enumerate(weights)
    ] + [remote(wo_own.at[rest, :], wo.at[t], w_send.at[3], w_recv.at[3], partner)]
    keeps = [
        pltpu.make_async_copy(w.at[:, half], w_all.at[t], w_own.at[n])
        for n, (w, w_all) in enumerate(weights)
    ] + [pltpu.make_async_copy(wo_own.at[half, :], wo.at[t], w_own.at[3])]
    for copy in swaps:
        copy.start()
    for k in range(4):
        across(k, 0, 0, sources[k], core).start()
        keep(k).start()
    for copy in keeps:
        copy.start()

    def gather_step(j, _):
        for k in (0, 2, 1, 3):
            for way in range(2):

                @pl.when(j < hops(k, way))
                def _(k=k, way=way):
                    wait, block = arrival(k, way, j)
                    wait.wait_recv()

                    @pl.when(j + 1 < hops(k, way))
                    def _():
                        onward(k, way, j + 1, block).start()

                    across(k, way, j + 1, block, core).start()

        return 0

    lax.fori_loop(0, 8, gather_step, 0)

    def zero(n, _):
        recvb[n, 0] = jnp.zeros((768, 256), BF16)
        return 0

    lax.fori_loop(0, 4, zero, 0)

    def gather_end(j, _):
        for way in range(2):
            for k in range(4):

                @pl.when(j < hops(k, way))
                def _(k=k, way=way):
                    onward(k, way, j, sources[k]).wait_send()
                    across(k, way, j + 1, sources[k], core).wait_send()
                    across(k, way, j + 1, sources[k], 1 - core).wait_recv()

        return 0

    lax.fori_loop(0, 8, gather_end, 0)
    for k in range(4):
        across(k, 0, 0, sources[k], core).wait_send()
        across(k, 0, 0, sources[k], 1 - core).wait_recv()
        keep(k).wait()
    for copy in keeps:
        copy.wait()
    for copy in swaps:
        copy.wait_send()
    for n, (w, w_all) in enumerate(weights):
        remote(w.at[:, rest], w_all.at[1 - t], w_send.at[n], w_recv.at[n], partner).wait_recv()
    remote(wo_own.at[rest, :], wo.at[1 - t], w_send.at[3], w_recv.at[3], partner).wait_recv()
    stores = [
        pltpu.make_async_copy(src, dst, out_sem.at[n])
        for n, (src, dst) in enumerate(((cot_v, cot_all), (dec_v, dec_all), (enc_v, enc_all)))
    ]
    for copy in stores:
        copy.start()


    def partial(d, h):
        j = d * 4 + h * 2
        b0, b1 = inverse[j], inverse[j + 1]
        stored = pl.ds(pl.multiple_of(j * 128, 256), 256)
        q = a = k = v = 0.0
        for f in range(2):
            rows = jnp.concatenate([dec_v[f, b0], dec_v[f, b1]], axis=0)
            q = q + dot(rows, wq[f])
            rows = jnp.concatenate([cot_v[f, b0], cot_v[f, b1]], axis=0)
            a = a + dot_t(rows, wo[f])
            rows = enc_v[f, stored, :]
            k = k + dot(rows, wk[f])
            v = v + dot(rows, wv[f])
        return ((0, 128, q), (128, 256, a), (256, 512, k), (512, 768, v))

    def stream(n):
        h = lax.rem(n, 2)
        way = lax.rem(h + lax.div(n, 2), 2)
        return h, 1 - 2 * way, 4 - lax.div(n, 2)

    def chain(n, t, sign):
        device = {"section": lax.rem(z + DEPTH + sign, DEPTH)}
        return remote(
            sendb.at[n, t], recvb.at[n, t + 1], send.at[n, t], recv.at[n, t], device
        )

    def item(w, _):
        n, t = lax.rem(w, 4), lax.div(w, 4)
        h, sign, length = stream(n)
        parts = partial(lax.rem(z + DEPTH + sign * (length - t), DEPTH), h)

        @pl.when(t > 0)
        def _():
            chain(n, t - 1, sign).wait_recv()

        for lo, hi, part in parts:
            sendb[n, t, lo:hi] = (part + recvb[n, t, lo:hi].astype(F32)).astype(BF16)
        chain(n, t, sign).start()
        return 0

    lax.fori_loop(0, 14, item, 0)

    def last(h, _):
        parts = partial(z, h)
        chain(h, 3, 1).wait_recv()
        chain(h + 2, 2, 1).wait_recv()
        for lo, hi, part in parts:
            total = part + recvb[h, 4, lo:hi].astype(F32) + recvb[h + 2, 3, lo:hi].astype(F32)
            fin[h, lo:hi] = total.astype(BF16)
        return 0

    lax.fori_loop(0, 2, last, 0)

    for h in range(2):
        for u in range(2):
            n = h * 2 + u
            for g in range(2):
                head = slice(g * 128, (g + 1) * 128)
                attended, query_grad, key_grad, value_grad = attend(
                    fin[h, u * 64 : (u + 1) * 64, head],
                    fin[h, 128 + u * 64 : 128 + (u + 1) * 64, head],
                    fin[h, 256 + u * 128 : 256 + (u + 1) * 128, head],
                    fin[h, 512 + u * 128 : 512 + (u + 1) * 128, head],
                    bias[pl.ds(z * 4 + n, 1), :],
                )
                att[n, :, head] = attended
                qg[n, :, head] = query_grad
                kg[n * 128 : (n + 1) * 128, head] = key_grad
                vg[n * 128 : (n + 1) * 128, head] = value_grad

    def chain_end(w, _):
        chain(lax.rem(w, 4), lax.div(w, 4), 1).wait_send()
        return 0

    lax.fori_loop(0, 14, chain_end, 0)
    for copy in stores:
        copy.wait()


def front(cot, dec, enc, wq, wk, wv, wo, bias, inverse):
    sds = jax.ShapeDtypeStruct
    return pl.pallas_call(
        front_kernel,
        out_shape=[
            sds((2, 32, 64, 512), BF16),
            sds((2, 32, 64, 512), BF16),
            sds((2, 4096, 512), BF16),
            sds((2, 512, 256), BF16),
            sds((2, 512, 256), BF16),
            sds((2, 512, 256), BF16),
            sds((2, 256, 512), BF16),
            sds((4, 64, 256), BF16),
            sds((4, 64, 256), BF16),
            sds((512, 256), BF16),
            sds((512, 256), BF16),
        ],
        in_specs=[VMEM] * 8 + [SMEM],
        out_specs=[ANY] * 3 + [VMEM] * 8,
        scratch_shapes=[
            pltpu.VMEM((2, 32, 64, 512), BF16),
            pltpu.VMEM((2, 32, 64, 512), BF16),
            pltpu.VMEM((2, 4096, 512), BF16),
            pltpu.VMEM((4, 4, 768, 256), BF16),
            pltpu.VMEM((4, 5, 768, 256), BF16),
            pltpu.VMEM((2, 768, 256), BF16),
            DMA((4, 2, 8)),
            DMA((4, 2, 8)),
            DMA((4, 2, 9)),
            DMA((4, 2, 9)),
            DMA((4,)),
            DMA((4,)),
            DMA((4,)),
            DMA((4,)),
            DMA((3,)),
            DMA((4, 4)),
            DMA((4, 4)),
        ],
        compiler_params=params(1, 60),
    )(cot, dec, enc, wq, wk, wv, wo, bias, inverse)


def back_kernel(
    att_own,
    qg_own,
    kg_own,
    vg_own,
    wq,
    wk,
    wv,
    wo,
    cot_hbm,
    dec_hbm,
    enc_hbm,
    ids,
    dec_out,
    out_out,
    enc_out,
    grads,
    grads_in,
    att_all,
    qg_all,
    kg_all,
    vg_all,
    att,
    qg,
    cot,
    dec,
    enc,
    sib_out,
    sib_in,
    chain_out,
    chain_in,
    mine,
    acc,
    grads_out,
    g_send,
    g_recv,
    own_sem,
    x_sem,
    s_send,
    s_recv,
    c_send,
    c_recv,
    w_send,
    w_recv,
):
    z, s, t, x, y, core = place()
    sibling = {"seq": s + 1 - 2 * core}
    partner = {"tensor": 1 - t}
    position = (ring_position(0, x, y), ring_position(1, x, y))
    loads = [
        pltpu.make_async_copy(src, dst, x_sem.at[n])
        for n, (src, dst) in enumerate(((cot_hbm, cot), (dec_hbm, dec), (enc_hbm, enc)))
    ]
    owns = (att_own, qg_own, kg_own, vg_own)
    alls = (att_all, qg_all, kg_all, vg_all)
    greet(plane_neighbours(x, y, core, s) + ring_neighbours(z))


    def ring_block(n, place_z):
        if n < 2:
            return alls[n].at[pl.ds(place_z * 4, 4)]
        return alls[n].at[pl.ds(pl.multiple_of(place_z * 512, 512), 512)]

    def ring_hops(n, way):
        return 4 if n % 2 == way else 3

    def ring_copy(n, way, j, src=None):
        sign = 1 - 2 * way
        block = ring_block(n, lax.rem(z + DEPTH - sign * j, DEPTH))
        device = {"section": lax.rem(z + DEPTH + sign, DEPTH)}
        return remote(
            block if src is None else src, block, g_send.at[n, way, j], g_recv.at[n, way, j], device
        )

    def ring_first(ns):
        for n in ns:
            for way in range(2):
                ring_copy(n, way, 0, owns[n]).start()

    def ring_step(ns, j):
        for n in ns:
            for way in range(2):

                @pl.when(j < ring_hops(n, way))
                def _(n=n, way=way):
                    sign = 1 - 2 * way
                    block = ring_block(n, lax.rem(z + DEPTH - sign * (j + 1), DEPTH))
                    remote(
                        block,
                        block,
                        g_send.at[n, way, j],
                        g_recv.at[n, way, j],
                        ring_neighbours(z)[0],
                    ).wait_recv()

                    @pl.when(j + 1 < ring_hops(n, way))
                    def _():
                        ring_copy(n, way, j + 1).start()

    def keep(n):
        return pltpu.make_async_copy(owns[n], ring_block(n, z), own_sem.at[n])

    ring_first((0, 1))
    for n in range(4):
        keep(n).start()
    for copy in loads:
        copy.start()
    for k in range(4):
        for way in range(2):
            for sub in range(2):
                chain_in[k, way, sub, 0] = jnp.zeros((64, 512), BF16)

    def first_steps(j, _):
        ring_step((0, 1), j)

        @pl.when(j == 2)
        def _():
            ring_first((2, 3))

        return 0

    lax.fori_loop(0, 4, first_steps, 0)
    for n in range(4):
        keep(n).wait()

    def token_order(b, _):
        rows = pl.ds(pl.multiple_of(b * 64, 64), 64)
        att[rows, :] = att_all[ids[b]]
        qg[rows, :] = qg_all[ids[b]]
        return 0

    lax.fori_loop(0, 32, token_order, 0)


    def dest(ring, offset):
        cx, cy = ring_chip(ring, lax.rem(position[ring] + offset, RING))
        return seq_tensor(cx, cy, 0)

    def both(ref, base, stride):
        return jnp.concatenate(
            [
                ref[pl.ds(pl.multiple_of(base + c * stride, 128), 128), :]
                for c in (core, 1 - core)
            ],
            axis=0,
        )

    def product(k, offset):
        sd, td = dest(k % 2, offset)
        if k == 0:
            return dot(both(qg, sd * 128, 128), wq[td])
        if k == 1:
            return dot(both(att, sd * 128, 128), wo[td])
        base = sd * 256 + (k - 2) * 128
        return dot(both(kg_all, base, 256), wk[td]) + dot(both(vg_all, base, 256), wv[td])

    def across(k, i):
        return remote(
            sib_out.at[k, lax.rem(i, 4)],
            sib_in.at[k, i],
            s_send.at[k, i],
            s_recv.at[k, i],
            sibling,
        )

    def give(ks, i):
        half = lax.div(i, 2)
        offset = 8 - half + lax.rem(i, 2) * (2 * half + 1)
        for k in ks:
            total = product(k, offset)

            @pl.when(i >= 4)
            def _(k=k):
                across(k, i - 4).wait_send()

            sib_out[k, lax.rem(i, 4)] = total[128:].astype(BF16)
            across(k, i).start()
            mine[k % 2, lax.rem(i, 4)] = total[:128]

    def onward(k, way, sub, j):
        device = ring_device(k % 2, position[k % 2] + 1 - 2 * way, core)
        return remote(
            chain_out.at[k, way, sub, lax.rem(j, 2)],
            chain_in.at[k, way, sub, j + 1],
            c_send.at[k, way, sub, j],
            c_recv.at[k, way, sub, j],
            device,
        )

    def chain_step(ks, j):
        for sub in range(2):
            part = slice(sub * 64, (sub + 1) * 64)
            for way in range(2):
                for k in ks:

                    @pl.when(j < 8 - way)
                    def _(k=k, way=way, sub=sub, part=part):
                        i = 2 * j + way
                        if sub == 0:
                            across(k, i).wait_recv()

                        @pl.when(j > 0)
                        def _():
                            onward(k, way, sub, j - 1).wait_recv()

                        @pl.when(j > 1)
                        def _():
                            onward(k, way, sub, j - 2).wait_send()

                        total = mine[k % 2, lax.rem(i, 4), part] + sib_in[k, i, part].astype(F32)
                        total = total + chain_in[k, way, sub, j].astype(F32)
                        chain_out[k, way, sub, lax.rem(j, 2)] = total.astype(BF16)
                        onward(k, way, sub, j).start()

    def weight_swap(n):
        return remote(
            grads_out.at[n], grads_in.at[n], w_send.at[n], w_recv.at[n], partner
        )

    def weight_step(pairs, rows, j):
        f = 1 - t + lax.div(j, 4) * (2 * t - 1)
        here = pl.ds(pl.multiple_of(lax.rem(j, 4) * rows, rows), rows)
        for a, (n, left, right) in enumerate(pairs):

            @pl.when(lax.rem(j, 4) == 0)
            def _(a=a):
                acc[a] = jnp.zeros((256, 512), F32)

            acc[a] += t_dot(left[here, :], right[f, here, :])

            @pl.when(j == 3)
            def _(a=a, n=n):
                grads_out[n] = acc[a].astype(BF16)
                weight_swap(n).start()

            @pl.when(j == 7)
            def _(a=a, n=n):
                grads[n] = acc[a]

    def scatter(ks, filler):
        give(ks, 0)
        give(ks, 1)

        def step(j, _):
            chain_step(ks, j)

            @pl.when(j < 7)
            def _():
                lax.fori_loop(2 * j + 2, 2 * j + 4, lambda i, _: (give(ks, i), 0)[1], 0)

            filler(j)
            return 0

        lax.fori_loop(0, 8, step, 0)
        outs = {
            0: dec_out,
            1: out_out,
            2: enc_out.at[pl.ds(0, 128)],
            3: enc_out.at[pl.ds(128, 128)],
        }
        for k in ks:
            across(k, 15).wait_recv()
            for sub in range(2):
                part = pl.ds(sub * 64, 64)
                total = mine[k % 2, 3, part] + sib_in[k, 15, part].astype(F32)
                for way in range(2):
                    onward(k, way, sub, 7 - way).wait_recv()
                    total = total + chain_in[k, way, sub, 8 - way].astype(F32)
                outs[k][part, :] = total
        for k in ks:
            for i in range(12, 16):
                across(k, i).wait_send()
            for way in range(2):
                for sub in range(2):
                    onward(k, way, sub, 6 - way).wait_send()
                    onward(k, way, sub, 7 - way).wait_send()

    def token_filler(j):
        @pl.when(j == 0)
        def _():
            loads[0].wait()
            loads[1].wait()

        weight_step(((0, qg, dec), (3, att, cot)), 512, j)

        @pl.when(lax.rem(j, 2) == 1)
        def _():
            ring_step((2, 3), lax.div(j, 2))

    scatter((0, 1), token_filler)
    loads[2].wait()
    scatter((2, 3), lambda j: weight_step(((1, kg_all, enc), (2, vg_all, enc)), 1024, j))

    for n in range(4):
        for way in range(2):
            for j in range(ring_hops(n, way)):
                ring_copy(n, way, j).wait_send()
    for n in range(4):
        weight_swap(n).wait()


def back(*args):
    sds = jax.ShapeDtypeStruct
    return pl.pallas_call(
        back_kernel,
        out_shape=[
            sds((128, 512), F32),
            sds((128, 512), F32),
            sds((256, 512), F32),
            sds((4, 256, 512), F32),
            sds((4, 256, 512), BF16),
        ],
        in_specs=[VMEM] * 8 + [ANY] * 3 + [SMEM],
        out_specs=[VMEM] * 5,
        scratch_shapes=[
            pltpu.VMEM((32, 64, 256), BF16),
            pltpu.VMEM((32, 64, 256), BF16),
            pltpu.VMEM((4096, 256), BF16),
            pltpu.VMEM((4096, 256), BF16),
            pltpu.VMEM((2048, 256), BF16),
            pltpu.VMEM((2048, 256), BF16),
            pltpu.VMEM((2, 2048, 512), BF16),
            pltpu.VMEM((2, 2048, 512), BF16),
            pltpu.VMEM((2, 4096, 512), BF16),
            pltpu.VMEM((4, 4, 128, 512), BF16),
            pltpu.VMEM((4, 16, 128, 512), BF16),
            pltpu.VMEM((4, 2, 2, 2, 64, 512), BF16),
            pltpu.VMEM((4, 2, 2, 9, 64, 512), BF16),
            pltpu.VMEM((2, 4, 128, 512), F32),
            pltpu.VMEM((2, 256, 512), F32),
            pltpu.VMEM((4, 256, 512), BF16),
            DMA((4, 2, 4)),
            DMA((4, 2, 4)),
            DMA((4,)),
            DMA((3,)),
            DMA((4, 16)),
            DMA((4, 16)),
            DMA((4, 2, 2, 8)),
            DMA((4, 2, 2, 8)),
            DMA((4,)),
            DMA((4,)),
        ],
        compiler_params=params(2, 62),
    )(*args)


def pack(*vectors):
    flat = jnp.concatenate(vectors)
    return jnp.pad(flat, (0, 1024 - flat.shape[0])).reshape(8, 128)


def body(
    hidden,
    dec_gain,
    neigh_states,
    enc_gain,
    w_query,
    w_key,
    w_value,
    w_out,
    neighbour_ids,
    neighbour_len,
    cotangent,
):
    t = lax.axis_index("tensor")
    rows = hidden.shape[0]
    dec_rows = hidden.astype(F32)
    enc_rows = neigh_states.astype(F32)
    (squares,) = small_sums(
        [pack(jnp.sum(dec_rows * dec_rows, axis=1), jnp.sum(enc_rows * enc_rows, axis=1))],
        ("st",),
        0,
    )
    scales = lax.rsqrt(squares.reshape(-1)[:384] / WIDTH + EPS)
    dec_scale, enc_scale = scales[:rows, None], scales[rows:, None]
    dec_hat = dec_rows * dec_scale
    enc_hat = enc_rows * enc_scale
    dec_local = (dec_hat * dec_gain).astype(BF16)
    enc_local = (enc_hat * enc_gain).astype(BF16)
    count = neighbour_ids.shape[0]
    inverse = jnp.sum(
        jnp.where(
            neighbour_ids[None, :] == jnp.arange(count, dtype=jnp.int32)[:, None],
            jnp.arange(count, dtype=jnp.int32)[None, :],
            0,
        ),
        axis=1,
    )
    slots = jnp.arange(128, dtype=jnp.int32)[None, :]
    bias = jnp.where(slots < neighbour_len[:, None], 0.0, -jnp.inf).astype(F32)
    cot_all, dec_all, enc_all, wq, wk, wv, wo, att, qg, kg, vg = front(
        cotangent.reshape(2, 64, 512),
        dec_local.reshape(2, 64, 512),
        enc_local,
        w_query,
        w_key,
        w_value,
        w_out,
        bias,
        inverse,
    )
    dec_input, out_total, enc_input, own, got = back(
        att,
        qg,
        kg,
        vg,
        jnp.swapaxes(wq, 1, 2),
        jnp.swapaxes(wk, 1, 2),
        jnp.swapaxes(wv, 1, 2),
        wo,
        cot_all.reshape(2, 2048, 512),
        dec_all.reshape(2, 2048, 512),
        enc_all,
        neighbour_ids,
    )
    got = got.astype(F32)
    joined = jnp.where(
        t == 0, jnp.concatenate([own, got], 1), jnp.concatenate([got, own], 1)
    )
    weight_grads = [joined[n].T for n in range(3)]
    out_weight_grad = joined[3]
    layer_out = (dec_rows + out_total).astype(BF16)
    dec_scaled = dec_gain * dec_input
    enc_scaled = enc_gain * enc_input
    inner, gains = small_sums(
        [
            pack(jnp.sum(dec_scaled * dec_hat, axis=1), jnp.sum(enc_scaled * enc_hat, axis=1)),
            pack(jnp.sum(dec_input * dec_hat, axis=0), jnp.sum(enc_input * enc_hat, axis=0)),
        ],
        ("st", "seq"),
        3,
    )
    inner = inner.reshape(-1)[:384] / WIDTH
    gains = gains.reshape(-1)
    hidden_grad = cotangent.astype(F32) + dec_scale * (
        dec_scaled - dec_hat * inner[:rows, None]
    )
    neighbour_grad = enc_scale * (enc_scaled - enc_hat * inner[rows:, None])
    return (
        layer_out,
        hidden_grad,
        neighbour_grad,
        gains[:512],
        gains[512:],
        weight_grads[0],
        weight_grads[1],
        weight_grads[2],
        out_weight_grad,
    )


def solution(mesh):
    features = ("section", "tensor")
    rows = P("seq", features)
    vector = P(features)
    columns = P(features, "seq")
    return jax.shard_map(
        body,
        mesh=mesh,
        in_specs=(
            rows,
            vector,
            rows,
            vector,
            columns,
            columns,
            columns,
            rows,
            P(),
            P(),
            rows,
        ),
        out_specs=(rows, rows, rows, vector, vector, columns, columns, columns, rows),
        check_vma=False,
    )
```

```python
import functools

import jax
import jax.numpy as jnp
from jax import lax
from jax.experimental import pallas as pl
from jax.experimental.pallas import tpu as pltpu
from jax.sharding import PartitionSpec as P

F32 = jnp.float32
BF16 = jnp.bfloat16
MESH = pl.DeviceIdType.MESH
EPS = 1e-05
WIDTH = 8192
ANY = pl.BlockSpec(memory_space=pl.ANY)
VMEM = pl.BlockSpec(memory_space=pltpu.VMEM)
SMEM = pl.BlockSpec(memory_space=pltpu.SMEM)
DMA = pltpu.SemaphoreType.DMA
RING = 16
DEPTH = 8


def place():
    z = lax.axis_index("section")
    s = lax.axis_index("seq")
    t = lax.axis_index("tensor")
    x = lax.div(lax.rem(s, 8), 2)
    y = lax.div(s, 8) * 2 + t
    return z, s, t, x, y, lax.rem(s, 2)


def ring_position(ring, x, y):
    return (y if ring == 0 else x) * 4 + lax.rem(x + y, 4)


def ring_chip(ring, p):
    a = lax.div(p, 4)
    b = lax.rem(lax.rem(p, 4) + 4 - a, 4)
    return (b, a) if ring == 0 else (a, b)


def seq_tensor(x, y, core):
    return lax.div(y, 2) * 8 + x * 2 + core, lax.rem(y, 2)


def ring_device(ring, p, core):
    x, y = ring_chip(ring, lax.rem(p + RING, RING))
    s, t = seq_tensor(x, y, core)
    return {"seq": s, "tensor": t}


def remote(src, dst, send_sem, recv_sem, device):
    return pltpu.make_async_remote_copy(
        src_ref=src,
        dst_ref=dst,
        send_sem=send_sem,
        recv_sem=recv_sem,
        device_id=device,
        device_id_type=MESH,
    )


def greet(devices):
    barrier = pltpu.get_barrier_semaphore()
    for device in devices:
        pl.semaphore_signal(barrier, inc=1, device_id=device, device_id_type=MESH)
    pl.semaphore_wait(barrier, len(devices))


def plane_neighbours(x, y, core, s):
    p1, p2 = ring_position(0, x, y), ring_position(1, x, y)
    return [
        ring_device(0, p1 + 1, core),
        ring_device(0, p1 - 1, core),
        ring_device(1, p2 + 1, core),
        ring_device(1, p2 - 1, core),
        {"seq": s + 1 - 2 * core},
    ]


def ring_neighbours(z):
    return [
        {"section": lax.rem(z + 1, DEPTH)},
        {"section": lax.rem(z + DEPTH - 1, DEPTH)},
    ]


def params(cid, mib=None):
    return pltpu.CompilerParams(
        collective_id=cid,
        has_side_effects=True,
        vmem_limit_bytes=None if mib is None else mib * 1024 * 1024,
    )


def small_kernel(groups, *refs):
    n = len(groups)
    ins, outs, slots = refs[:n], refs[n : 2 * n], refs[2 * n : 3 * n]
    send, recv = refs[3 * n], refs[3 * n + 1]
    z, s, t, _, _, _ = place()

    def peer(group, r):
        if group == "st":
            g = lax.rem(z * 2 + t + r, 16)
            return {"section": lax.div(g, 2), "tensor": lax.rem(g, 2)}, g
        g = lax.rem(s + r, 16)
        return {"seq": g}, g

    barrier = pltpu.get_barrier_semaphore()
    for group in groups:

        def hello(r, _, group=group):
            pl.semaphore_signal(
                barrier, inc=1, device_id=peer(group, r)[0], device_id_type=MESH
            )
            return 0

        lax.fori_loop(1, 16, hello, 0)
    pl.semaphore_wait(barrier, 15 * n)
    for k, group in enumerate(groups):
        mine = peer(group, 0)[1]

        def push(r, _, k=k, group=group, mine=mine):
            device, _g = peer(group, r)
            remote(
                ins[k], slots[k].at[mine], send.at[k, r], recv.at[k, mine], device
            ).start()
            return 0

        lax.fori_loop(1, 16, push, 0)
        slots[k][mine] = ins[k][...]
    for k, group in enumerate(groups):
        mine = peer(group, 0)[1]

        def take(r, _, k=k, group=group, mine=mine):
            device, g = peer(group, r)
            remote(ins[k], slots[k].at[g], send.at[k, r], recv.at[k, g], device).wait_recv()
            return 0

        lax.fori_loop(1, 16, take, 0)
        total = slots[k][0]
        for g in range(1, 16):
            total = total + slots[k][g]
        outs[k][...] = total
    for k, group in enumerate(groups):
        mine = peer(group, 0)[1]

        def drain(r, _, k=k, group=group, mine=mine):
            device, _g = peer(group, r)
            remote(
                ins[k], slots[k].at[mine], send.at[k, r], recv.at[k, mine], device
            ).wait_send()
            return 0

        lax.fori_loop(1, 16, drain, 0)


def small_sums(arrays, groups, cid):
    n = len(groups)
    return pl.pallas_call(
        functools.partial(small_kernel, groups),
        out_shape=[jax.ShapeDtypeStruct((8, 128), F32)] * n,
        in_specs=[VMEM] * n,
        out_specs=[VMEM] * n,
        scratch_shapes=[pltpu.VMEM((16, 8, 128), F32)] * n + [DMA((n, 16)), DMA((n, 16))],
        compiler_params=params(cid),
    )(*arrays)


def dot(a, b):
    return jnp.dot(a, b, preferred_element_type=F32)


def dot_t(a, b):
    return lax.dot_general(a, b, (((1,), (1,)), ((), ())), preferred_element_type=F32)


def t_dot(a, b):
    return lax.dot_general(a, b, (((0,), (0,)), ((), ())), preferred_element_type=F32)


def split(a):
    high = a.astype(BF16)
    return high, (a - high.astype(F32)).astype(BF16)


def attend(q, a, k, v, bias):
    scale = 128 ** (-0.5)
    scores = dot_t(q, k) * scale + bias
    top = jnp.max(scores, axis=1, keepdims=True)
    expo = jnp.exp(scores - top)
    probs = expo / jnp.sum(expo, axis=1, keepdims=True)
    low = probs.astype(BF16)
    attended = dot(low, v).astype(BF16)
    value_grad = t_dot(low, a).astype(BF16)
    prob_grad = dot_t(a, v)
    inner = jnp.sum(probs * prob_grad, axis=1, keepdims=True)
    score_grad = probs * (prob_grad - inner) * scale
    high, rest = split(score_grad)
    query_grad = (dot(high, k) + dot(rest, k)).astype(BF16)
    key_grad = (t_dot(high, q) + t_dot(rest, q)).astype(BF16)
    return attended, query_grad, key_grad, value_grad


def front_kernel(
    cot,
    hidden,
    neigh,
    dec_gain,
    enc_gain,
    wq_own,
    wk_own,
    wv_own,
    wo_own,
    bias,
    inverse,
    cot_all,
    dec_all,
    enc_all,
    wq_t,
    wk_t,
    wv_t,
    wo,
    att,
    qg,
    kg,
    vg,
    squares,
    cot_v,
    dec_v,
    enc_v,
    wq,
    wk,
    wv,
    dec,
    enc,
    stat,
    stats,
    kv_send,
    kv_recv,
    qa_send,
    qa_recv,
    kv_fin,
    qa_fin,
    st_send,
    st_recv,
    p_send,
    p_recv,
    s_send,
    s_recv,
    own_sem,
    w_send,
    w_recv,
    w_own,
    out_sem,
    kv_ssem,
    kv_rsem,
    qa_ssem,
    qa_rsem,
):
    z, s, t, x, y, core = place()
    sibling = {"seq": s + 1 - 2 * core}
    partner = {"tensor": 1 - t}
    group = z * 2 + t

    def peer(r):
        g = lax.rem(group + r, 16)
        return {"section": lax.div(g, 2), "tensor": lax.rem(g, 2)}, g

    barrier = pltpu.get_barrier_semaphore()
    near = plane_neighbours(x, y, core, s)
    for device in near:
        pl.semaphore_signal(barrier, inc=1, device_id=device, device_id_type=MESH)

    def hello(r, _):
        pl.semaphore_signal(barrier, inc=1, device_id=peer(r)[0], device_id_type=MESH)
        return 0

    lax.fori_loop(1, 16, hello, 0)
    dec_rows = hidden[...].reshape(128, 512).astype(F32)
    enc_rows = neigh[...].astype(F32)
    sums = jnp.concatenate(
        [
            jnp.sum(dec_rows * dec_rows, axis=1, keepdims=True),
            jnp.sum(enc_rows * enc_rows, axis=1, keepdims=True),
        ],
        axis=0,
    )
    stat[...] = jnp.broadcast_to(sums, (384, 128)).T[:8]
    pl.semaphore_wait(barrier, len(near) + 15)


    def slot(k, sub, chip, c):
        so, to = seq_tensor(chip[0], chip[1], c)
        if k == 0:
            return cot_v.at[to, so * 2 + sub]
        if k == 1:
            return dec_v.at[to, so * 2 + sub]
        return enc_v.at[to, pl.ds(pl.multiple_of(so * 256 + (k - 2) * 128 + sub * 64, 64), 64)]

    def source(k, sub):
        if k == 0:
            return cot.at[sub]
        if k == 1:
            return dec.at[sub]
        return enc.at[pl.ds((k - 2) * 128 + sub * 64, 64)]

    position = (ring_position(0, x, y), ring_position(1, x, y))

    def origin(k, way, j):
        return ring_chip(k % 2, lax.rem(position[k % 2] + RING - (1 - 2 * way) * j, RING))

    def onward(k, way, sub, j, src):
        device = ring_device(k % 2, position[k % 2] + 1 - 2 * way, core)
        block = slot(k, sub, origin(k, way, j), core)
        return remote(
            src, block, p_send.at[k, way, sub, j], p_recv.at[k, way, sub, j], device
        )

    def across(k, way, sub, j, src, c):
        block = slot(k, sub, origin(k, way, j), c)
        return remote(
            src, block, s_send.at[k, way, sub, j], s_recv.at[k, way, sub, j], sibling
        )

    def keep(k, sub):
        return pltpu.make_async_copy(
            source(k, sub), slot(k, sub, (x, y), core), own_sem.at[k, sub]
        )

    def begin(ks):
        for sub in range(2):
            for way in range(2):
                for k in ks:
                    onward(k, way, sub, 0, source(k, sub)).start()
        for k in ks:
            for sub in range(2):
                across(k, 0, sub, 0, source(k, sub), core).start()
                keep(k, sub).start()

    def gather_step(ks, j):
        for sub in range(2):
            for way in range(2):
                for k in ks:

                    @pl.when(j < 8 - way)
                    def _(k=k, way=way, sub=sub):
                        block = slot(k, sub, origin(k, way, j + 1), core)
                        remote(
                            block,
                            block,
                            p_send.at[k, way, sub, j],
                            p_recv.at[k, way, sub, j],
                            sibling,
                        ).wait_recv()

                        @pl.when(j < 7 - way)
                        def _():
                            onward(k, way, sub, j + 1, block).start()

                        across(k, way, sub, j + 1, block, core).start()

    def gather_end(ks):
        def one(j, _):
            for k in ks:
                for sub in range(2):
                    for way in range(2):

                        @pl.when(j < 8 - way)
                        def _(k=k, way=way, sub=sub):
                            src = source(k, sub)
                            onward(k, way, sub, j, src).wait_send()
                            across(k, way, sub, j + 1, src, core).wait_send()
                            across(k, way, sub, j + 1, src, 1 - core).wait_recv()

            return 0

        lax.fori_loop(0, 8, one, 0)
        for k in ks:
            for sub in range(2):
                across(k, 0, sub, 0, source(k, sub), core).wait_send()
                across(k, 0, sub, 0, source(k, sub), 1 - core).wait_recv()
                keep(k, sub).wait()


    def tell(r):
        device, g = peer(r)
        return remote(stat, stats.at[group], st_send.at[r], st_recv.at[group], device)

    lax.fori_loop(1, 16, lambda r, _: (tell(r).start(), 0)[1], 0)
    half = pl.ds(pl.multiple_of(t * 256, 256), 256)
    rest = pl.ds(pl.multiple_of((1 - t) * 256, 256), 256)
    weights = ((wk_own, wk), (wv_own, wv), (wq_own, wq))
    swaps = [
        remote(w.at[:, rest], w_all.at[t], w_send.at[n], w_recv.at[n], partner)
        for n, (w, w_all) in enumerate(weights)
    ] + [remote(wo_own.at[rest, :], wo.at[t], w_send.at[3], w_recv.at[3], partner)]
    keeps = [
        pltpu.make_async_copy(w.at[:, half], w_all.at[t], w_own.at[n])
        for n, (w, w_all) in enumerate(weights)
    ] + [pltpu.make_async_copy(wo_own.at[half, :], wo.at[t], w_own.at[3])]
    begin((0,))
    for copy in keeps:
        copy.start()
    stats[group] = stat[...]

    def hear(r, _):
        device, g = peer(r)
        remote(stat, stats.at[g], st_send.at[r], st_recv.at[g], device).wait_recv()
        return 0

    lax.fori_loop(1, 16, hear, 0)
    total = stats[0]
    for g in range(1, 16):
        total = total + stats[g]
    squares[...] = total
    scale = lax.rsqrt(total[:1] / WIDTH + EPS)
    scale = jnp.broadcast_to(scale, (128, 384)).T[:, :1]
    enc[...] = (neigh[...].astype(F32) * scale[128:] * enc_gain[...]).astype(BF16)
    begin((2, 3))
    rows = hidden[...].reshape(128, 512).astype(F32)
    dec[...] = (rows * scale[:128] * dec_gain[...]).astype(BF16).reshape(2, 64, 512)
    for copy in swaps:
        copy.start()

    def enc_step(j, _):
        gather_step((2, 3), j)

        @pl.when(j == 4)
        def _():
            begin((1,))

        @pl.when(j >= 6)
        def _():
            gather_step((0, 1), j - 6)

        return 0

    lax.fori_loop(0, 8, enc_step, 0)

    def zero(n, _):
        kv_recv[n, 0] = jnp.zeros((512, 256), BF16)
        qa_recv[n, 0] = jnp.zeros((256, 256), BF16)
        return 0

    lax.fori_loop(0, 4, zero, 0)
    for n, copy in enumerate(keeps):
        copy.wait()
        swaps[n].wait_send()
    for n, (w, w_all) in enumerate(weights):
        remote(w.at[:, rest], w_all.at[1 - t], w_send.at[n], w_recv.at[n], partner).wait_recv()
    remote(wo_own.at[rest, :], wo.at[1 - t], w_send.at[3], w_recv.at[3], partner).wait_recv()
    gather_end((2, 3))
    stores = [
        pltpu.make_async_copy(src, dst, out_sem.at[n])
        for n, (src, dst) in enumerate(((cot_v, cot_all), (dec_v, dec_all), (enc_v, enc_all)))
    ]
    stores[2].start()


    def pair_part(d, h):
        stored = pl.ds(pl.multiple_of(d * 512 + h * 256, 256), 256)
        first, second = enc_v[0, stored, :], enc_v[1, stored, :]
        k = dot(first, wk[0]) + dot(second, wk[1])
        v = dot(first, wv[0]) + dot(second, wv[1])
        return ((0, 256, k), (256, 512, v))

    def query_part(d, h):
        j = d * 4 + h * 2
        b0, b1 = inverse[j], inverse[j + 1]
        q = a = 0.0
        for f in range(2):
            q = q + dot(jnp.concatenate([dec_v[f, b0], dec_v[f, b1]], axis=0), wq[f])
            a = a + dot_t(jnp.concatenate([cot_v[f, b0], cot_v[f, b1]], axis=0), wo[f])
        return ((0, 128, q), (128, 256, a))

    pairs = (kv_send, kv_recv, kv_ssem, kv_rsem, kv_fin, pair_part)
    queries = (qa_send, qa_recv, qa_ssem, qa_rsem, qa_fin, query_part)

    def chain(which, n, j, sign):
        sendb, recvb, ssem, rsem = which[:4]
        device = {"section": lax.rem(z + DEPTH + sign, DEPTH)}
        return remote(
            sendb.at[n, j], recvb.at[n, j + 1], ssem.at[n, j], rsem.at[n, j], device
        )

    def item(which, w):
        n, j = lax.rem(w, 4), lax.div(w, 4)
        h = lax.rem(n, 2)
        sign = 1 - 2 * lax.rem(h + lax.div(n, 2), 2)
        length = 4 - lax.div(n, 2)
        parts = which[5](lax.rem(z + DEPTH + sign * (length - j), DEPTH), h)

        @pl.when(j > 0)
        def _():
            chain(which, n, j - 1, sign).wait_recv()

        for lo, hi, part in parts:
            which[0][n, j, lo:hi] = (part + which[1][n, j, lo:hi].astype(F32)).astype(BF16)
        chain(which, n, j, sign).start()

    def last(which):
        def one(h, _):
            parts = which[5](z, h)
            chain(which, h, 3, 1).wait_recv()
            chain(which, h + 2, 2, 1).wait_recv()
            for lo, hi, part in parts:
                total = part + which[1][h, 4, lo:hi].astype(F32)
                total = total + which[1][h + 2, 3, lo:hi].astype(F32)
                which[4][h, lo:hi] = total.astype(BF16)
            return 0

        lax.fori_loop(0, 2, one, 0)

    def pair_item(w, _):
        item(pairs, w)

        @pl.when((lax.rem(w, 2) == 1) & (w < 12))
        def _():
            gather_step((0, 1), lax.div(w, 2) + 2)

        for n, (src, dst) in enumerate(((wq, wq_t), (wk, wk_t), (wv, wv_t))):

            @pl.when(w == 4 + 2 * n)
            def _(src=src, dst=dst):
                for f in range(2):
                    dst[f] = src[f].T

        return 0

    lax.fori_loop(0, 14, pair_item, 0)
    gather_end((0, 1))
    stores[0].start()
    stores[1].start()
    lax.fori_loop(0, 14, lambda w, _: (item(queries, w), 0)[1], 0)
    last(pairs)
    last(queries)

    for h in range(2):
        for u in range(2):
            n = h * 2 + u
            for g in range(2):
                head = slice(g * 128, (g + 1) * 128)
                attended, query_grad, key_grad, value_grad = attend(
                    qa_fin[h, u * 64 : (u + 1) * 64, head],
                    qa_fin[h, 128 + u * 64 : 128 + (u + 1) * 64, head],
                    kv_fin[h, u * 128 : (u + 1) * 128, head],
                    kv_fin[h, 256 + u * 128 : 256 + (u + 1) * 128, head],
                    bias[pl.ds(z * 4 + n, 1), :],
                )
                att[n, :, head] = attended
                qg[n, :, head] = query_grad
                kg[n * 128 : (n + 1) * 128, head] = key_grad
                vg[n * 128 : (n + 1) * 128, head] = value_grad

    def chain_end(w, _):
        chain(pairs, lax.rem(w, 4), lax.div(w, 4), 1).wait_send()
        chain(queries, lax.rem(w, 4), lax.div(w, 4), 1).wait_send()
        return 0

    lax.fori_loop(0, 14, chain_end, 0)
    lax.fori_loop(1, 16, lambda r, _: (tell(r).wait_send(), 0)[1], 0)
    for copy in stores:
        copy.wait()


def front(*args):
    sds = jax.ShapeDtypeStruct
    return pl.pallas_call(
        front_kernel,
        out_shape=[
            sds((2, 32, 64, 512), BF16),
            sds((2, 32, 64, 512), BF16),
            sds((2, 4096, 512), BF16),
            sds((2, 256, 512), BF16),
            sds((2, 256, 512), BF16),
            sds((2, 256, 512), BF16),
            sds((2, 256, 512), BF16),
            sds((4, 64, 256), BF16),
            sds((4, 64, 256), BF16),
            sds((512, 256), BF16),
            sds((512, 256), BF16),
            sds((8, 384), F32),
        ],
        in_specs=[VMEM] * 10 + [SMEM],
        out_specs=[ANY] * 3 + [VMEM] * 9,
        scratch_shapes=[
            pltpu.VMEM((2, 32, 64, 512), BF16),
            pltpu.VMEM((2, 32, 64, 512), BF16),
            pltpu.VMEM((2, 4096, 512), BF16),
            pltpu.VMEM((2, 512, 256), BF16),
            pltpu.VMEM((2, 512, 256), BF16),
            pltpu.VMEM((2, 512, 256), BF16),
            pltpu.VMEM((2, 64, 512), BF16),
            pltpu.VMEM((256, 512), BF16),
            pltpu.VMEM((8, 384), F32),
            pltpu.VMEM((16, 8, 384), F32),
            pltpu.VMEM((4, 4, 512, 256), BF16),
            pltpu.VMEM((4, 5, 512, 256), BF16),
            pltpu.VMEM((4, 4, 256, 256), BF16),
            pltpu.VMEM((4, 5, 256, 256), BF16),
            pltpu.VMEM((2, 512, 256), BF16),
            pltpu.VMEM((2, 256, 256), BF16),
            DMA((16,)),
            DMA((16,)),
            DMA((4, 2, 2, 8)),
            DMA((4, 2, 2, 8)),
            DMA((4, 2, 2, 9)),
            DMA((4, 2, 2, 9)),
            DMA((4, 2)),
            DMA((4,)),
            DMA((4,)),
            DMA((4,)),
            DMA((3,)),
            DMA((4, 4)),
            DMA((4, 4)),
            DMA((4, 4)),
            DMA((4, 4)),
        ],
        compiler_params=params(1, 60),
    )(*args)


def back_kernel(
    att_own,
    qg_own,
    kg_own,
    vg_own,
    wq,
    wk,
    wv,
    wo,
    cot_hbm,
    dec_hbm,
    enc_hbm,
    ids,
    dec_out,
    out_out,
    enc_out,
    grads,
    grads_in,
    att_all,
    qg_all,
    kg_all,
    vg_all,
    att,
    qg,
    cot,
    dec,
    enc,
    sib_out,
    sib_in,
    chain_out,
    chain_in,
    mine,
    acc,
    grads_out,
    g_send,
    g_recv,
    own_sem,
    x_sem,
    s_send,
    s_recv,
    c_send,
    c_recv,
    w_send,
    w_recv,
):
    z, s, t, x, y, core = place()
    sibling = {"seq": s + 1 - 2 * core}
    partner = {"tensor": 1 - t}
    position = (ring_position(0, x, y), ring_position(1, x, y))
    loads = [
        pltpu.make_async_copy(src, dst, x_sem.at[n])
        for n, (src, dst) in enumerate(((cot_hbm, cot), (dec_hbm, dec), (enc_hbm, enc)))
    ]
    owns = (att_own, qg_own, kg_own, vg_own)
    alls = (att_all, qg_all, kg_all, vg_all)
    greet(plane_neighbours(x, y, core, s) + ring_neighbours(z))


    def ring_block(n, place_z):
        if n < 2:
            return alls[n].at[pl.ds(place_z * 4, 4)]
        return alls[n].at[pl.ds(pl.multiple_of(place_z * 512, 512), 512)]

    def ring_hops(n, way):
        return 4 if n % 2 == way else 3

    def ring_copy(n, way, j, src=None):
        sign = 1 - 2 * way
        block = ring_block(n, lax.rem(z + DEPTH - sign * j, DEPTH))
        device = {"section": lax.rem(z + DEPTH + sign, DEPTH)}
        return remote(
            block if src is None else src, block, g_send.at[n, way, j], g_recv.at[n, way, j], device
        )

    def ring_first(ns):
        for n in ns:
            for way in range(2):
                ring_copy(n, way, 0, owns[n]).start()

    def ring_step(ns, j):
        for n in ns:
            for way in range(2):

                @pl.when(j < ring_hops(n, way))
                def _(n=n, way=way):
                    sign = 1 - 2 * way
                    block = ring_block(n, lax.rem(z + DEPTH - sign * (j + 1), DEPTH))
                    remote(
                        block,
                        block,
                        g_send.at[n, way, j],
                        g_recv.at[n, way, j],
                        ring_neighbours(z)[0],
                    ).wait_recv()

                    @pl.when(j + 1 < ring_hops(n, way))
                    def _():
                        ring_copy(n, way, j + 1).start()

    def keep(n):
        return pltpu.make_async_copy(owns[n], ring_block(n, z), own_sem.at[n])

    ring_first((0, 1))
    for n in range(4):
        keep(n).start()
    for copy in loads:
        copy.start()
    for k in range(4):
        for way in range(2):
            for sub in range(2):
                chain_in[k, way, sub, 0] = jnp.zeros((64, 512), BF16)

    def first_steps(j, _):
        ring_step((0, 1), j)

        @pl.when(j == 2)
        def _():
            ring_first((2, 3))

        return 0

    lax.fori_loop(0, 4, first_steps, 0)
    for n in range(4):
        keep(n).wait()

    def token_order(b, _):
        rows = pl.ds(pl.multiple_of(b * 64, 64), 64)
        att[rows, :] = att_all[ids[b]]
        qg[rows, :] = qg_all[ids[b]]
        return 0

    lax.fori_loop(0, 32, token_order, 0)


    def dest(ring, offset):
        cx, cy = ring_chip(ring, lax.rem(position[ring] + offset, RING))
        return seq_tensor(cx, cy, 0)

    def both(ref, base, stride):
        return jnp.concatenate(
            [
                ref[pl.ds(pl.multiple_of(base + c * stride, 128), 128), :]
                for c in (core, 1 - core)
            ],
            axis=0,
        )

    def product(k, offset):
        sd, td = dest(k % 2, offset)
        if k == 0:
            return dot(both(qg, sd * 128, 128), wq[td])
        if k == 1:
            return dot(both(att, sd * 128, 128), wo[td])
        base = sd * 256 + (k - 2) * 128
        return dot(both(kg_all, base, 256), wk[td]) + dot(both(vg_all, base, 256), wv[td])

    def across(k, i):
        return remote(
            sib_out.at[k, lax.rem(i, 4)],
            sib_in.at[k, i],
            s_send.at[k, i],
            s_recv.at[k, i],
            sibling,
        )

    def give(ks, i):
        half = lax.div(i, 2)
        offset = 8 - half + lax.rem(i, 2) * (2 * half + 1)
        for k in ks:
            total = product(k, offset)

            @pl.when(i >= 4)
            def _(k=k):
                across(k, i - 4).wait_send()

            sib_out[k, lax.rem(i, 4)] = total[128:].astype(BF16)
            across(k, i).start()
            mine[k % 2, lax.rem(i, 4)] = total[:128]

    def onward(k, way, sub, j):
        device = ring_device(k % 2, position[k % 2] + 1 - 2 * way, core)
        return remote(
            chain_out.at[k, way, sub, lax.rem(j, 2)],
            chain_in.at[k, way, sub, j + 1],
            c_send.at[k, way, sub, j],
            c_recv.at[k, way, sub, j],
            device,
        )

    def chain_step(ks, j):
        for sub in range(2):
            part = slice(sub * 64, (sub + 1) * 64)
            for way in range(2):
                for k in ks:

                    @pl.when(j < 8 - way)
                    def _(k=k, way=way, sub=sub, part=part):
                        i = 2 * j + way
                        if sub == 0:
                            across(k, i).wait_recv()

                        @pl.when(j > 0)
                        def _():
                            onward(k, way, sub, j - 1).wait_recv()

                        @pl.when(j > 1)
                        def _():
                            onward(k, way, sub, j - 2).wait_send()

                        total = mine[k % 2, lax.rem(i, 4), part] + sib_in[k, i, part].astype(F32)
                        total = total + chain_in[k, way, sub, j].astype(F32)
                        chain_out[k, way, sub, lax.rem(j, 2)] = total.astype(BF16)
                        onward(k, way, sub, j).start()

    def weight_swap(n):
        return remote(
            grads_out.at[n], grads_in.at[n], w_send.at[n], w_recv.at[n], partner
        )

    def weight_step(pairs, rows, j):
        f = 1 - t + lax.div(j, 4) * (2 * t - 1)
        here = pl.ds(pl.multiple_of(lax.rem(j, 4) * rows, rows), rows)
        for a, (n, left, right) in enumerate(pairs):

            @pl.when(lax.rem(j, 4) == 0)
            def _(a=a):
                acc[a] = jnp.zeros((256, 512), F32)

            acc[a] += t_dot(left[here, :], right[f, here, :])

            @pl.when(j == 3)
            def _(a=a, n=n):
                grads_out[n] = acc[a].astype(BF16)
                weight_swap(n).start()

            @pl.when(j == 7)
            def _(a=a, n=n):
                grads[n] = acc[a]

    def scatter(ks, filler):
        give(ks, 0)
        give(ks, 1)

        def step(j, _):
            chain_step(ks, j)

            @pl.when(j < 7)
            def _():
                lax.fori_loop(2 * j + 2, 2 * j + 4, lambda i, _: (give(ks, i), 0)[1], 0)

            filler(j)
            return 0

        lax.fori_loop(0, 8, step, 0)
        outs = {
            0: dec_out,
            1: out_out,
            2: enc_out.at[pl.ds(0, 128)],
            3: enc_out.at[pl.ds(128, 128)],
        }
        for k in ks:
            across(k, 15).wait_recv()
            for sub in range(2):
                part = pl.ds(sub * 64, 64)
                total = mine[k % 2, 3, part] + sib_in[k, 15, part].astype(F32)
                for way in range(2):
                    onward(k, way, sub, 7 - way).wait_recv()
                    total = total + chain_in[k, way, sub, 8 - way].astype(F32)
                outs[k][part, :] = total
        for k in ks:
            for i in range(12, 16):
                across(k, i).wait_send()
            for way in range(2):
                for sub in range(2):
                    onward(k, way, sub, 6 - way).wait_send()
                    onward(k, way, sub, 7 - way).wait_send()

    def token_filler(j):
        @pl.when(j == 0)
        def _():
            loads[0].wait()
            loads[1].wait()

        weight_step(((0, qg, dec), (3, att, cot)), 512, j)

        @pl.when(lax.rem(j, 2) == 1)
        def _():
            ring_step((2, 3), lax.div(j, 2))

    scatter((0, 1), token_filler)
    loads[2].wait()
    scatter((2, 3), lambda j: weight_step(((1, kg_all, enc), (2, vg_all, enc)), 1024, j))

    for n in range(4):
        for way in range(2):
            for j in range(ring_hops(n, way)):
                ring_copy(n, way, j).wait_send()
    for n in range(4):
        weight_swap(n).wait()


def back(*args):
    sds = jax.ShapeDtypeStruct
    return pl.pallas_call(
        back_kernel,
        out_shape=[
            sds((128, 512), F32),
            sds((128, 512), F32),
            sds((256, 512), F32),
            sds((4, 256, 512), F32),
            sds((4, 256, 512), BF16),
        ],
        in_specs=[VMEM] * 8 + [ANY] * 3 + [SMEM],
        out_specs=[VMEM] * 5,
        scratch_shapes=[
            pltpu.VMEM((32, 64, 256), BF16),
            pltpu.VMEM((32, 64, 256), BF16),
            pltpu.VMEM((4096, 256), BF16),
            pltpu.VMEM((4096, 256), BF16),
            pltpu.VMEM((2048, 256), BF16),
            pltpu.VMEM((2048, 256), BF16),
            pltpu.VMEM((2, 2048, 512), BF16),
            pltpu.VMEM((2, 2048, 512), BF16),
            pltpu.VMEM((2, 4096, 512), BF16),
            pltpu.VMEM((4, 4, 128, 512), BF16),
            pltpu.VMEM((4, 16, 128, 512), BF16),
            pltpu.VMEM((4, 2, 2, 2, 64, 512), BF16),
            pltpu.VMEM((4, 2, 2, 9, 64, 512), BF16),
            pltpu.VMEM((2, 4, 128, 512), F32),
            pltpu.VMEM((2, 256, 512), F32),
            pltpu.VMEM((4, 256, 512), BF16),
            DMA((4, 2, 4)),
            DMA((4, 2, 4)),
            DMA((4,)),
            DMA((3,)),
            DMA((4, 16)),
            DMA((4, 16)),
            DMA((4, 2, 2, 8)),
            DMA((4, 2, 2, 8)),
            DMA((4,)),
            DMA((4,)),
        ],
        compiler_params=params(2, 62),
    )(*args)


def pack(*vectors):
    flat = jnp.concatenate(vectors)
    return jnp.pad(flat, (0, 1024 - flat.shape[0])).reshape(8, 128)


def body(
    hidden,
    dec_gain,
    neigh_states,
    enc_gain,
    w_query,
    w_key,
    w_value,
    w_out,
    neighbour_ids,
    neighbour_len,
    cotangent,
):
    t = lax.axis_index("tensor")
    rows = hidden.shape[0]
    dec_rows = hidden.astype(F32)
    enc_rows = neigh_states.astype(F32)
    count = neighbour_ids.shape[0]
    inverse = jnp.sum(
        jnp.where(
            neighbour_ids[None, :] == jnp.arange(count, dtype=jnp.int32)[:, None],
            jnp.arange(count, dtype=jnp.int32)[None, :],
            0,
        ),
        axis=1,
    )
    slots = jnp.arange(128, dtype=jnp.int32)[None, :]
    bias = jnp.where(slots < neighbour_len[:, None], 0.0, -jnp.inf).astype(F32)
    cot_all, dec_all, enc_all, wq, wk, wv, wo, att, qg, kg, vg, squares = front(
        cotangent.reshape(2, 64, 512),
        hidden.reshape(2, 64, 512),
        neigh_states,
        dec_gain[None],
        enc_gain[None],
        w_query,
        w_key,
        w_value,
        w_out,
        bias,
        inverse,
    )
    dec_input, out_total, enc_input, own, got = back(
        att,
        qg,
        kg,
        vg,
        wq,
        wk,
        wv,
        wo,
        cot_all.reshape(2, 2048, 512),
        dec_all.reshape(2, 2048, 512),
        enc_all,
        neighbour_ids,
    )
    scales = lax.rsqrt(squares[0] / WIDTH + EPS)
    dec_scale, enc_scale = scales[:rows, None], scales[rows:, None]
    dec_hat = dec_rows * dec_scale
    enc_hat = enc_rows * enc_scale
    got = got.astype(F32)
    joined = jnp.where(
        t == 0, jnp.concatenate([own, got], 1), jnp.concatenate([got, own], 1)
    )
    weight_grads = [joined[n].T for n in range(3)]
    out_weight_grad = joined[3]
    layer_out = (dec_rows + out_total).astype(BF16)
    dec_scaled = dec_gain * dec_input
    enc_scaled = enc_gain * enc_input
    inner, gains = small_sums(
        [
            pack(jnp.sum(dec_scaled * dec_hat, axis=1), jnp.sum(enc_scaled * enc_hat, axis=1)),
            pack(jnp.sum(dec_input * dec_hat, axis=0), jnp.sum(enc_input * enc_hat, axis=0)),
        ],
        ("st", "seq"),
        3,
    )
    inner = inner.reshape(-1)[:384] / WIDTH
    gains = gains.reshape(-1)
    hidden_grad = cotangent.astype(F32) + dec_scale * (
        dec_scaled - dec_hat * inner[:rows, None]
    )
    neighbour_grad = enc_scale * (enc_scaled - enc_hat * inner[rows:, None])
    return (
        layer_out,
        hidden_grad,
        neighbour_grad,
        gains[:512],
        gains[512:],
        weight_grads[0],
        weight_grads[1],
        weight_grads[2],
        out_weight_grad,
    )


def solution(mesh):
    features = ("section", "tensor")
    rows = P("seq", features)
    vector = P(features)
    columns = P(features, "seq")
    return jax.shard_map(
        body,
        mesh=mesh,
        in_specs=(
            rows,
            vector,
            rows,
            vector,
            columns,
            columns,
            columns,
            rows,
            P(),
            P(),
            rows,
        ),
        out_specs=(rows, rows, rows, vector, vector, columns, columns, columns, rows),
        check_vma=False,
    )
```

```python
import functools

import jax
import jax.numpy as jnp
from jax import lax
from jax.experimental import pallas as pl
from jax.experimental.pallas import tpu as pltpu
from jax.sharding import PartitionSpec as P

F32 = jnp.float32
BF16 = jnp.bfloat16
MESH = pl.DeviceIdType.MESH
EPS = 1e-05
WIDTH = 8192
ANY = pl.BlockSpec(memory_space=pl.ANY)
VMEM = pl.BlockSpec(memory_space=pltpu.VMEM)
SMEM = pl.BlockSpec(memory_space=pltpu.SMEM)
DMA = pltpu.SemaphoreType.DMA
RING = 16
DEPTH = 8


def place():
    z = lax.axis_index("section")
    s = lax.axis_index("seq")
    t = lax.axis_index("tensor")
    x = lax.div(lax.rem(s, 8), 2)
    y = lax.div(s, 8) * 2 + t
    return z, s, t, x, y, lax.rem(s, 2)


def ring_position(ring, x, y):
    return (y if ring == 0 else x) * 4 + lax.rem(x + y, 4)


def ring_chip(ring, p):
    a = lax.div(p, 4)
    b = lax.rem(lax.rem(p, 4) + 4 - a, 4)
    return (b, a) if ring == 0 else (a, b)


def seq_tensor(x, y, core):
    return lax.div(y, 2) * 8 + x * 2 + core, lax.rem(y, 2)


def ring_device(ring, p, core):
    x, y = ring_chip(ring, lax.rem(p + RING, RING))
    s, t = seq_tensor(x, y, core)
    return {"seq": s, "tensor": t}


def remote(src, dst, send_sem, recv_sem, device):
    return pltpu.make_async_remote_copy(
        src_ref=src,
        dst_ref=dst,
        send_sem=send_sem,
        recv_sem=recv_sem,
        device_id=device,
        device_id_type=MESH,
    )


def greet(devices):
    barrier = pltpu.get_barrier_semaphore()
    for device in devices:
        pl.semaphore_signal(barrier, inc=1, device_id=device, device_id_type=MESH)
    pl.semaphore_wait(barrier, len(devices))


def plane_neighbours(x, y, core, s):
    p1, p2 = ring_position(0, x, y), ring_position(1, x, y)
    return [
        ring_device(0, p1 + 1, core),
        ring_device(0, p1 - 1, core),
        ring_device(1, p2 + 1, core),
        ring_device(1, p2 - 1, core),
        {"seq": s + 1 - 2 * core},
    ]


def ring_neighbours(z):
    return [
        {"section": lax.rem(z + 1, DEPTH)},
        {"section": lax.rem(z + DEPTH - 1, DEPTH)},
    ]


def params(cid, mib=None):
    return pltpu.CompilerParams(
        collective_id=cid,
        has_side_effects=True,
        vmem_limit_bytes=None if mib is None else mib * 1024 * 1024,
    )


def dot(a, b):
    return jnp.dot(a, b, preferred_element_type=F32)


def dot_t(a, b):
    return lax.dot_general(a, b, (((1,), (1,)), ((), ())), preferred_element_type=F32)


def t_dot(a, b):
    return lax.dot_general(a, b, (((0,), (0,)), ((), ())), preferred_element_type=F32)


def split(a):
    high = a.astype(BF16)
    return high, (a - high.astype(F32)).astype(BF16)


def attend(units):
    scale = 128 ** (-0.5)
    scores = [dot_t(q, k) * scale + bias for q, a, k, v, bias in units]
    prob_grads = [dot_t(a, v) for q, a, k, v, bias in units]
    tops = [jnp.max(u, axis=1, keepdims=True) for u in scores]
    expos = [jnp.exp(u - top) for u, top in zip(scores, tops)]
    sums = [jnp.sum(u, axis=1, keepdims=True) for u in expos]
    probs = [u / total for u, total in zip(expos, sums)]
    lows = [u.astype(BF16) for u in probs]
    inners = [jnp.sum(u * g, axis=1, keepdims=True) for u, g in zip(probs, prob_grads)]
    score_grads = [u * (g - n) * scale for u, g, n in zip(probs, prob_grads, inners)]
    splits = [split(u) for u in score_grads]
    attended = [dot(low, u[3]).astype(BF16) for low, u in zip(lows, units)]
    query_grads = [
        (dot(high, u[2]) + dot(rest, u[2])).astype(BF16) for (high, rest), u in zip(splits, units)
    ]
    key_grads = [
        (t_dot(high, u[0]) + t_dot(rest, u[0])).astype(BF16)
        for (high, rest), u in zip(splits, units)
    ]
    value_grads = [t_dot(low, u[1]).astype(BF16) for low, u in zip(lows, units)]
    return list(zip(attended, query_grads, key_grads, value_grads))


def front_kernel(
    cot,
    hidden,
    neigh,
    dec_gain,
    enc_gain,
    wq_own,
    wk_own,
    wv_own,
    wo_own,
    bias,
    inverse,
    cot_all,
    dec_all,
    enc_all,
    wq,
    wk,
    wv,
    wo,
    att,
    qg,
    kg,
    vg,
    squares,
    cot_v,
    dec_v,
    enc_v,
    dec,
    enc,
    stat,
    stats,
    kv_send,
    kv_recv,
    qa_send,
    qa_recv,
    kv_fin,
    qa_fin,
    st_send,
    st_recv,
    p_send,
    p_recv,
    s_send,
    s_recv,
    own_sem,
    w_send,
    w_recv,
    w_own,
    out_sem,
    kv_ssem,
    kv_rsem,
    qa_ssem,
    qa_rsem,
):
    z, s, t, x, y, core = place()
    sibling = {"seq": s + 1 - 2 * core}
    partner = {"tensor": 1 - t}
    group = z * 2 + t

    def peer(r):
        g = lax.rem(group + r, 16)
        return {"section": lax.div(g, 2), "tensor": lax.rem(g, 2)}, g

    barrier = pltpu.get_barrier_semaphore()
    near = plane_neighbours(x, y, core, s)
    for device in near:
        pl.semaphore_signal(barrier, inc=1, device_id=device, device_id_type=MESH)

    def hello(r, _):
        pl.semaphore_signal(barrier, inc=1, device_id=peer(r)[0], device_id_type=MESH)
        return 0

    lax.fori_loop(1, 16, hello, 0)
    dec_rows = hidden[...].reshape(128, 512).astype(F32)
    enc_rows = neigh[...].astype(F32)
    sums = jnp.concatenate(
        [
            jnp.sum(dec_rows * dec_rows, axis=1, keepdims=True),
            jnp.sum(enc_rows * enc_rows, axis=1, keepdims=True),
        ],
        axis=0,
    )
    sums = jnp.broadcast_to(sums, (384, 128)).T[:1]
    stat[...] = jnp.zeros((8, 128), F32)
    for n in range(3):
        stat[n : n + 1] = sums[:, n * 128 : (n + 1) * 128]
    pl.semaphore_wait(barrier, len(near) + 15)


    def slot(k, sub, so, to, c):
        so = so + c
        if k == 0:
            return cot_v.at[to, so * 2 + sub]
        if k == 1:
            return dec_v.at[to, so * 2 + sub]
        return enc_v.at[to, pl.ds(pl.multiple_of(so * 256 + (k - 2) * 128 + sub * 64, 64), 64)]

    def source(k, sub):
        if k == 0:
            return cot.at[sub]
        if k == 1:
            return dec.at[sub]
        return enc.at[pl.ds((k - 2) * 128 + sub * 64, 64)]

    position = (ring_position(0, x, y), ring_position(1, x, y))
    own_so, own_to = seq_tensor(x, y, 0)
    nexts = [
        [ring_device(ring, position[ring] + 1 - 2 * way, core) for way in range(2)]
        for ring in range(2)
    ]

    def origins(j):
        return [
            [
                seq_tensor(
                    *ring_chip(
                        ring, lax.rem(position[ring] + RING - (1 - 2 * way) * j, RING)
                    ),
                    0,
                )
                for way in range(2)
            ]
            for ring in range(2)
        ]

    def onward(k, way, sub, j, src, dst):
        return remote(
            src, dst, p_send.at[k, way, sub, j], p_recv.at[k, way, sub, j], nexts[k % 2][way]
        )

    def across(k, way, sub, j, src, dst):
        return remote(src, dst, s_send.at[k, way, sub, j], s_recv.at[k, way, sub, j], sibling)

    def keep(k, sub):
        return pltpu.make_async_copy(
            source(k, sub), slot(k, sub, own_so, own_to, core), own_sem.at[k, sub]
        )

    def begin(ks):
        for sub in range(2):
            for way in range(2):
                for k in ks:
                    dst = slot(k, sub, own_so, own_to, core)
                    onward(k, way, sub, 0, source(k, sub), dst).start()
        for k in ks:
            for sub in range(2):
                dst = slot(k, sub, own_so, own_to, core)
                across(k, 0, sub, 0, source(k, sub), dst).start()
                keep(k, sub).start()

    def gather_step(ks, j):
        froms = origins(j + 1)
        for sub in range(2):
            for way in range(2):
                for k in ks:

                    @pl.when(j < 8 - way)
                    def _(k=k, way=way, sub=sub):
                        block = slot(k, sub, *froms[k % 2][way], core)
                        onward(k, way, sub, j, block, block).wait_recv()

                        @pl.when(j < 7 - way)
                        def _():
                            onward(k, way, sub, j + 1, block, block).start()

                        across(k, way, sub, j + 1, block, block).start()

    def gather_end(ks):
        def one(j, _):
            froms = origins(j + 1)
            for k in ks:
                for sub in range(2):
                    for way in range(2):

                        @pl.when(j < 8 - way)
                        def _(k=k, way=way, sub=sub):
                            src = source(k, sub)
                            block = slot(k, sub, *froms[k % 2][way], 1 - core)
                            onward(k, way, sub, j, src, src).wait_send()
                            across(k, way, sub, j + 1, src, src).wait_send()
                            across(k, way, sub, j + 1, block, block).wait_recv()

            return 0

        lax.fori_loop(0, 8, one, 0)
        for k in ks:
            for sub in range(2):
                src = source(k, sub)
                block = slot(k, sub, own_so, own_to, 1 - core)
                across(k, 0, sub, 0, src, src).wait_send()
                across(k, 0, sub, 0, block, block).wait_recv()
                keep(k, sub).wait()


    def tell(r):
        device, g = peer(r)
        return remote(stat, stats.at[group], st_send.at[r], st_recv.at[group], device)

    lax.fori_loop(1, 16, lambda r, _: (tell(r).start(), 0)[1], 0)
    half = pl.ds(pl.multiple_of(t * 256, 256), 256)
    rest = pl.ds(pl.multiple_of((1 - t) * 256, 256), 256)
    weights = ((wk_own, wk), (wv_own, wv), (wq_own, wq))
    swaps = [
        remote(w.at[:, rest], w_all.at[t], w_send.at[n], w_recv.at[n], partner)
        for n, (w, w_all) in enumerate(weights)
    ] + [remote(wo_own.at[rest, :], wo.at[t], w_send.at[3], w_recv.at[3], partner)]
    keeps = [
        pltpu.make_async_copy(w.at[:, half], w_all.at[t], w_own.at[n])
        for n, (w, w_all) in enumerate(weights)
    ] + [pltpu.make_async_copy(wo_own.at[half, :], wo.at[t], w_own.at[3])]
    for copy in swaps[:2]:
        copy.start()
    for copy in keeps:
        copy.start()
    stats[group] = stat[...]

    def hear(r, _):
        device, g = peer(r)
        remote(stat, stats.at[g], st_send.at[r], st_recv.at[g], device).wait_recv()
        return 0

    lax.fori_loop(1, 16, hear, 0)
    total = stats[0]
    for g in range(1, 16):
        total = total + stats[g]
    squares[...] = total
    scale = lax.rsqrt(total / WIDTH + EPS)
    scales = [jnp.broadcast_to(scale[n : n + 1], (128, 128)).T[:, :1] for n in range(3)]
    for n in range(2):
        rows = neigh[n * 128 : (n + 1) * 128].astype(F32)
        normed = rows * scales[n + 1] * enc_gain[...]
        enc[n * 128 : (n + 1) * 128] = normed.astype(BF16)
    begin((2, 3))
    rows = hidden[...].reshape(128, 512).astype(F32)
    dec[...] = (rows * scales[0] * dec_gain[...]).astype(BF16).reshape(2, 64, 512)

    def enc_step(j, _):
        gather_step((2, 3), j)

        @pl.when(j == 4)
        def _():
            begin((0, 1))

        @pl.when(j >= 6)
        def _():
            gather_step((0, 1), j - 6)

        return 0

    lax.fori_loop(0, 8, enc_step, 0)

    def zero(n, _):
        kv_recv[n, 0] = jnp.zeros((512, 256), BF16)
        qa_recv[n, 0] = jnp.zeros((256, 256), BF16)
        return 0

    lax.fori_loop(0, 4, zero, 0)
    for copy in swaps[2:]:
        copy.start()
    for copy in keeps:
        copy.wait()

    def swapped(n):
        swaps[n].wait_send()
        if n < 3:
            w, w_all = weights[n]
            dst = w_all.at[1 - t]
            remote(w.at[:, rest], dst, w_send.at[n], w_recv.at[n], partner).wait_recv()
        else:
            dst = wo.at[1 - t]
            remote(wo_own.at[rest, :], dst, w_send.at[n], w_recv.at[n], partner).wait_recv()

    swapped(0)
    swapped(1)
    gather_end((2, 3))
    stores = [
        pltpu.make_async_copy(src, dst, out_sem.at[n])
        for n, (src, dst) in enumerate(((cot_v, cot_all), (dec_v, dec_all), (enc_v, enc_all)))
    ]
    stores[2].start()


    def pair_part(d, h):
        stored = pl.ds(pl.multiple_of(d * 512 + h * 256, 256), 256)
        first, second = enc_v[0, stored, :], enc_v[1, stored, :]
        k = dot(first, wk[0]) + dot(second, wk[1])
        v = dot(first, wv[0]) + dot(second, wv[1])
        return ((0, 256, k), (256, 512, v))

    def query_part(d, h):
        j = d * 4 + h * 2
        b0, b1 = inverse[j], inverse[j + 1]
        q = a = 0.0
        for f in range(2):
            q = q + dot(jnp.concatenate([dec_v[f, b0], dec_v[f, b1]], axis=0), wq[f])
            a = a + dot_t(jnp.concatenate([cot_v[f, b0], cot_v[f, b1]], axis=0), wo[f])
        return ((0, 128, q), (128, 256, a))

    pairs = (kv_send, kv_recv, kv_ssem, kv_rsem, kv_fin, pair_part)
    queries = (qa_send, qa_recv, qa_ssem, qa_rsem, qa_fin, query_part)

    def chain(which, n, j, sign):
        sendb, recvb, ssem, rsem = which[:4]
        device = {"section": lax.rem(z + DEPTH + sign, DEPTH)}
        return remote(
            sendb.at[n, j], recvb.at[n, j + 1], ssem.at[n, j], rsem.at[n, j], device
        )

    def item(which, w):
        n, j = lax.rem(w, 4), lax.div(w, 4)
        h = lax.rem(n, 2)
        sign = 1 - 2 * lax.rem(h + lax.div(n, 2), 2)
        length = 4 - lax.div(n, 2)
        parts = which[5](lax.rem(z + DEPTH + sign * (length - j), DEPTH), h)

        @pl.when(j > 0)
        def _():
            chain(which, n, j - 1, sign).wait_recv()

        for lo, hi, part in parts:
            which[0][n, j, lo:hi] = (part + which[1][n, j, lo:hi].astype(F32)).astype(BF16)
        chain(which, n, j, sign).start()

    def last(which):
        def one(h, _):
            parts = which[5](z, h)
            chain(which, h, 3, 1).wait_recv()
            chain(which, h + 2, 2, 1).wait_recv()
            for lo, hi, part in parts:
                total = part + which[1][h, 4, lo:hi].astype(F32)
                total = total + which[1][h + 2, 3, lo:hi].astype(F32)
                which[4][h, lo:hi] = total.astype(BF16)
            return 0

        lax.fori_loop(0, 2, one, 0)

    def pair_item(w, _):
        item(pairs, w)

        @pl.when((lax.rem(w, 2) == 1) & (w < 12))
        def _():
            gather_step((0, 1), lax.div(w, 2) + 2)

        return 0

    lax.fori_loop(0, 14, pair_item, 0)
    gather_end((0, 1))
    swapped(2)
    swapped(3)
    stores[0].start()
    stores[1].start()
    lax.fori_loop(0, 14, lambda w, _: (item(queries, w), 0)[1], 0)
    last(pairs)
    last(queries)

    for h in range(2):
        places = [(u, slice(g * 128, (g + 1) * 128)) for u in range(2) for g in range(2)]
        results = attend(
            [
                (
                    qa_fin[h, u * 64 : (u + 1) * 64, head],
                    qa_fin[h, 128 + u * 64 : 128 + (u + 1) * 64, head],
                    kv_fin[h, u * 128 : (u + 1) * 128, head],
                    kv_fin[h, 256 + u * 128 : 256 + (u + 1) * 128, head],
                    bias[pl.ds(z * 4 + h * 2 + u, 1), :],
                )
                for u, head in places
            ]
        )
        for (u, head), (attended, query_grad, key_grad, value_grad) in zip(places, results):
            n = h * 2 + u
            att[n, :, head] = attended
            qg[n, :, head] = query_grad
            kg[n * 128 : (n + 1) * 128, head] = key_grad
            vg[n * 128 : (n + 1) * 128, head] = value_grad

    def chain_end(w, _):
        chain(pairs, lax.rem(w, 4), lax.div(w, 4), 1).wait_send()
        chain(queries, lax.rem(w, 4), lax.div(w, 4), 1).wait_send()
        return 0

    lax.fori_loop(0, 14, chain_end, 0)
    lax.fori_loop(1, 16, lambda r, _: (tell(r).wait_send(), 0)[1], 0)
    for copy in stores:
        copy.wait()


def front(*args):
    sds = jax.ShapeDtypeStruct
    return pl.pallas_call(
        front_kernel,
        out_shape=[
            sds((2, 32, 64, 512), BF16),
            sds((2, 32, 64, 512), BF16),
            sds((2, 4096, 512), BF16),
            sds((2, 512, 256), BF16),
            sds((2, 512, 256), BF16),
            sds((2, 512, 256), BF16),
            sds((2, 256, 512), BF16),
            sds((4, 64, 256), BF16),
            sds((4, 64, 256), BF16),
            sds((512, 256), BF16),
            sds((512, 256), BF16),
            sds((8, 128), F32),
        ],
        in_specs=[VMEM] * 10 + [SMEM],
        out_specs=[ANY] * 3 + [VMEM] * 9,
        scratch_shapes=[
            pltpu.VMEM((2, 32, 64, 512), BF16),
            pltpu.VMEM((2, 32, 64, 512), BF16),
            pltpu.VMEM((2, 4096, 512), BF16),
            pltpu.VMEM((2, 64, 512), BF16),
            pltpu.VMEM((256, 512), BF16),
            pltpu.VMEM((8, 128), F32),
            pltpu.VMEM((16, 8, 128), F32),
            pltpu.VMEM((4, 4, 512, 256), BF16),
            pltpu.VMEM((4, 5, 512, 256), BF16),
            pltpu.VMEM((4, 4, 256, 256), BF16),
            pltpu.VMEM((4, 5, 256, 256), BF16),
            pltpu.VMEM((2, 512, 256), BF16),
            pltpu.VMEM((2, 256, 256), BF16),
            DMA((16,)),
            DMA((16,)),
            DMA((4, 2, 2, 8)),
            DMA((4, 2, 2, 8)),
            DMA((4, 2, 2, 9)),
            DMA((4, 2, 2, 9)),
            DMA((4, 2)),
            DMA((4,)),
            DMA((4,)),
            DMA((4,)),
            DMA((3,)),
            DMA((4, 4)),
            DMA((4, 4)),
            DMA((4, 4)),
            DMA((4, 4)),
        ],
        compiler_params=params(1, 60),
    )(*args)


def back_kernel(
    att_own,
    qg_own,
    kg_own,
    vg_own,
    wq,
    wk,
    wv,
    wo,
    cot_hbm,
    dec_hbm,
    enc_hbm,
    ids,
    hidden,
    neigh,
    dec_gain,
    enc_gain,
    squares,
    dec_out,
    out_out,
    enc_out,
    grads,
    grads_in,
    inner_out,
    gain_out,
    att_all,
    qg_all,
    kg_all,
    vg_all,
    att,
    qg,
    cot,
    dec,
    enc,
    sib_out,
    sib_in,
    chain_out,
    chain_in,
    mine,
    acc,
    pair_acc,
    grads_out,
    inner,
    gains,
    inners,
    gainses,
    e_send,
    e_recv,
    g_send,
    g_recv,
    own_sem,
    x_sem,
    s_send,
    s_recv,
    c_send,
    c_recv,
    w_send,
    w_recv,
):
    z, s, t, x, y, core = place()
    sibling = {"seq": s + 1 - 2 * core}
    partner = {"tensor": 1 - t}
    position = (ring_position(0, x, y), ring_position(1, x, y))
    loads = [
        pltpu.make_async_copy(src, dst, x_sem.at[n])
        for n, (src, dst) in enumerate(((cot_hbm, cot), (dec_hbm, dec), (enc_hbm, enc)))
    ]
    nexts = [
        [ring_device(ring, position[ring] + 1 - 2 * way, core) for way in range(2)]
        for ring in range(2)
    ]
    owns = (att_own, qg_own, kg_own, vg_own)
    alls = (att_all, qg_all, kg_all, vg_all)
    group = z * 2 + t
    sums = ((inner, inners, inner_out, group), (gains, gainses, gain_out, s))

    def peer(n, r):
        g = lax.rem(sums[n][3] + r, 16)
        return ({"section": lax.div(g, 2), "tensor": lax.rem(g, 2)} if n == 0 else {"seq": g}), g

    barrier = pltpu.get_barrier_semaphore()
    near = plane_neighbours(x, y, core, s)
    for device in near:
        pl.semaphore_signal(barrier, inc=1, device_id=device, device_id_type=MESH)

    def hello(r, _):
        for n in range(2):
            pl.semaphore_signal(barrier, inc=1, device_id=peer(n, r)[0], device_id_type=MESH)
        return 0

    lax.fori_loop(1, 16, hello, 0)
    pl.semaphore_wait(barrier, len(near) + 30)


    def ring_block(n, place_z):
        if n < 2:
            return alls[n].at[pl.ds(place_z * 4, 4)]
        return alls[n].at[pl.ds(pl.multiple_of(place_z * 512, 512), 512)]

    def ring_hops(n, way):
        return 4 if n % 2 == way else 3

    def ring_copy(n, way, j, src=None):
        sign = 1 - 2 * way
        block = ring_block(n, lax.rem(z + DEPTH - sign * j, DEPTH))
        device = {"section": lax.rem(z + DEPTH + sign, DEPTH)}
        return remote(
            block if src is None else src, block, g_send.at[n, way, j], g_recv.at[n, way, j], device
        )

    def ring_first(ns):
        for n in ns:
            for way in range(2):
                ring_copy(n, way, 0, owns[n]).start()

    def ring_step(ns, j):
        for n in ns:
            for way in range(2):

                @pl.when(j < ring_hops(n, way))
                def _(n=n, way=way):
                    sign = 1 - 2 * way
                    block = ring_block(n, lax.rem(z + DEPTH - sign * (j + 1), DEPTH))
                    remote(
                        block,
                        block,
                        g_send.at[n, way, j],
                        g_recv.at[n, way, j],
                        ring_neighbours(z)[0],
                    ).wait_recv()

                    @pl.when(j + 1 < ring_hops(n, way))
                    def _():
                        ring_copy(n, way, j + 1).start()

    def keep(n):
        return pltpu.make_async_copy(owns[n], ring_block(n, z), own_sem.at[n])

    ring_first((0, 1))
    for n in range(4):
        keep(n).start()
    for copy in loads:
        copy.start()
    for k in range(4):
        for way in range(2):
            for sub in range(2):
                chain_in[k, way, sub, 0] = jnp.zeros((64, 512), BF16)

    def first_steps(j, _):
        ring_step((0, 1), j)

        @pl.when(j == 2)
        def _():
            ring_first((2, 3))

        return 0

    lax.fori_loop(0, 4, first_steps, 0)
    for n in range(4):
        keep(n).wait()

    def token_order(b, _):
        rows = pl.ds(pl.multiple_of(b * 64, 64), 64)
        att[rows, :] = att_all[ids[b]]
        qg[rows, :] = qg_all[ids[b]]
        return 0

    lax.fori_loop(0, 32, token_order, 0)


    def dest(ring, offset):
        cx, cy = ring_chip(ring, lax.rem(position[ring] + offset, RING))
        return seq_tensor(cx, cy, 0)

    def both(ref, base, stride):
        return jnp.concatenate(
            [
                ref[pl.ds(pl.multiple_of(base + c * stride, 128), 128), :]
                for c in (core, 1 - core)
            ],
            axis=0,
        )

    def product(k, offset):
        sd, td = dest(k % 2, offset)
        if k == 0:
            return dot_t(both(qg, sd * 128, 128), wq[td])
        if k == 1:
            return dot(both(att, sd * 128, 128), wo[td])
        base = sd * 256 + (k - 2) * 128
        return dot_t(both(kg_all, base, 256), wk[td]) + dot_t(both(vg_all, base, 256), wv[td])

    def across(k, i, four=0):
        return remote(
            sib_out.at[k, four],
            sib_in.at[k, i],
            s_send.at[k, i],
            s_recv.at[k, i],
            sibling,
        )

    def give(ks, i):
        half = lax.div(i, 2)
        four = lax.rem(i, 4)
        offset = 8 - half + (i - 2 * half) * (2 * half + 1)
        for k in ks:
            total = product(k, offset)

            @pl.when(i >= 4)
            def _(k=k):
                across(k, i - 4, four).wait_send()

            sib_out[k, four] = total[128:].astype(BF16)
            across(k, i, four).start()
            mine[k % 2, four] = total[:128]

    def onward(k, way, sub, j, two):
        return remote(
            chain_out.at[k, way, sub, two],
            chain_in.at[k, way, sub, j + 1],
            c_send.at[k, way, sub, j],
            c_recv.at[k, way, sub, j],
            nexts[k % 2][way],
        )

    def chain_step(ks, j):
        two = lax.rem(j, 2)
        for sub in range(2):
            part = slice(sub * 64, (sub + 1) * 64)
            for way in range(2):
                for k in ks:

                    @pl.when(j < 8 - way)
                    def _(k=k, way=way, sub=sub, part=part):
                        i = 2 * j + way
                        four = 2 * two + way
                        if sub == 0:
                            across(k, i).wait_recv()

                        @pl.when(j > 0)
                        def _():
                            onward(k, way, sub, j - 1, two).wait_recv()

                        @pl.when(j > 1)
                        def _():
                            onward(k, way, sub, j - 2, two).wait_send()

                        total = mine[k % 2, four, part] + sib_in[k, i, part].astype(F32)
                        total = total + chain_in[k, way, sub, j].astype(F32)
                        chain_out[k, way, sub, two] = total.astype(BF16)
                        onward(k, way, sub, j, two).start()

    def weight_swap(n):
        return remote(
            grads_out.at[n], grads_in.at[n], w_send.at[n, 0], w_recv.at[n, 0], partner
        )

    def pair_swap(j):
        n, m = 1 + lax.div(j, 4), lax.rem(j, 4)
        rows = pl.ds(pl.multiple_of(m * 64, 64), 64)
        return remote(
            grads_out.at[n, rows], grads_in.at[n, rows], w_send.at[n, m], w_recv.at[n, m], partner
        )

    def weight_step(pairs, rows, j):
        f = 1 - t + lax.div(j, 4) * (2 * t - 1)
        here = pl.ds(pl.multiple_of(lax.rem(j, 4) * rows, rows), rows)
        for a, (n, left, right) in enumerate(pairs):

            @pl.when(lax.rem(j, 4) == 0)
            def _(a=a):
                acc[a] = jnp.zeros((256, 512), F32)

            acc[a] += t_dot(left[here, :], right[f, here, :])

            @pl.when(j == 3)
            def _(a=a, n=n):
                grads_out[n] = acc[a].astype(BF16)
                weight_swap(n).start()

            @pl.when(j == 7)
            def _(a=a, n=n):
                grads[n] = acc[a]

    def pair_weights(place_z):
        rows = pl.ds(pl.multiple_of(place_z * 512, 512), 512)
        for a, left in enumerate((kg_all, vg_all)):
            block = left[rows, :]
            for f in range(2):
                pair_acc[a, f] += t_dot(block, enc[f, rows, :])

    def scatter(ks, filler):
        give(ks, 0)
        give(ks, 1)

        def step(j, _):
            chain_step(ks, j)

            @pl.when(j < 7)
            def _():
                lax.fori_loop(2 * j + 2, 2 * j + 4, lambda i, _: (give(ks, i), 0)[1], 0)

            filler(j)
            return 0

        lax.fori_loop(0, 8, step, 0)
        outs = {
            0: dec_out,
            1: out_out,
            2: enc_out.at[pl.ds(0, 128)],
            3: enc_out.at[pl.ds(128, 128)],
        }
        for k in ks:
            across(k, 15).wait_recv()
            for sub in range(2):
                part = pl.ds(sub * 64, 64)
                total = mine[k % 2, 3, part] + sib_in[k, 15, part].astype(F32)
                for way in range(2):
                    onward(k, way, sub, 7 - way, 0).wait_recv()
                    total = total + chain_in[k, way, sub, 8 - way].astype(F32)
                outs[k][part, :] = total
        for k in ks:
            for i in range(12, 16):
                across(k, i).wait_send()
            for way in range(2):
                for sub in range(2):
                    onward(k, way, sub, 6 - way, 0).wait_send()
                    onward(k, way, sub, 7 - way, 1).wait_send()

    def token_filler(j):
        @pl.when(j == 0)
        def _():
            loads[0].wait()
            loads[1].wait()
            loads[2].wait()

        weight_step(((0, qg, dec), (3, att, cot)), 512, j)

        @pl.when(lax.rem(j, 2) == 0)
        def _():
            distance = lax.div(j, 2)
            pair_weights(lax.rem(z + distance, DEPTH))

            @pl.when(j > 0)
            def _():
                pair_weights(lax.rem(z + DEPTH - distance, DEPTH))

        @pl.when(lax.rem(j, 2) == 1)
        def _():
            ring_step((2, 3), lax.div(j, 2))

    pair_acc[...] = jnp.zeros((2, 2, 256, 512), F32)
    inner[...] = jnp.zeros((8, 128), F32)
    gains[...] = jnp.zeros((8, 128), F32)
    scale = lax.rsqrt(squares[...] / WIDTH + EPS)
    scales = [jnp.broadcast_to(scale[n : n + 1], (128, 128)).T[:, :1] for n in range(3)]
    scatter((0, 1), token_filler)

    def sum_rows(n):
        part = slice(max(n - 1, 0) * 128, max(n - 1, 0) * 128 + 128)
        upstream = dec_out[...] if n == 0 else enc_out[part, :]
        unit = (hidden if n == 0 else neigh)[part, :].astype(F32) * scales[n]
        product_of = upstream * unit
        gain = (dec_gain if n == 0 else enc_gain)[...]
        column = jnp.sum(product_of * gain, axis=1, keepdims=True)
        inner[n : n + 1] = jnp.broadcast_to(column, (128, 128)).T[:1]
        row = jnp.sum(product_of, axis=0, keepdims=True)
        first = 0 if n == 0 else 4
        for m in range(4):
            gains[first + m : first + m + 1] += row[:, m * 128 : (m + 1) * 128]

    def pair_filler(j):
        @pl.when(j == 0)
        def _():
            pair_weights(lax.rem(z + 4, DEPTH))
            for a in range(2):
                grads_out[1 + a] = pair_acc[a, 1 - t].astype(BF16)
                grads[1 + a] = pair_acc[a, t]

        pair_swap(j).start()

        @pl.when(j == 1)
        def _():
            sum_rows(0)

    scatter((2, 3), pair_filler)


    sum_rows(1)
    sum_rows(2)

    def tell(n, r):
        src, slots, _out, own = sums[n]
        return remote(src, slots.at[own], e_send.at[n, r], e_recv.at[n, own], peer(n, r)[0])

    def tell_all(r, _):
        for n in range(2):
            tell(n, r).start()
        return 0

    def hear_all(r, _):
        for n in range(2):
            src, slots, _out, own = sums[n]
            device, g = peer(n, r)
            remote(src, slots.at[g], e_send.at[n, r], e_recv.at[n, g], device).wait_recv()
        return 0

    def told_all(r, _):
        for n in range(2):
            tell(n, r).wait_send()
        return 0

    lax.fori_loop(1, 16, tell_all, 0)
    for src, slots, _out, own in sums:
        slots[own] = src[...]

    for n in range(4):
        for way in range(2):
            for j in range(ring_hops(n, way)):
                ring_copy(n, way, j).wait_send()
    weight_swap(0).wait()
    weight_swap(3).wait()
    lax.fori_loop(0, 8, lambda j, _: (pair_swap(j).wait(), 0)[1], 0)
    lax.fori_loop(1, 16, hear_all, 0)
    for src, slots, out, own in sums:
        total = slots[0]
        for g in range(1, 16):
            total = total + slots[g]
        out[...] = total
    lax.fori_loop(1, 16, told_all, 0)


def back(*args):
    sds = jax.ShapeDtypeStruct
    return pl.pallas_call(
        back_kernel,
        out_shape=[
            sds((128, 512), F32),
            sds((128, 512), F32),
            sds((256, 512), F32),
            sds((4, 256, 512), F32),
            sds((4, 256, 512), BF16),
            sds((8, 128), F32),
            sds((8, 128), F32),
        ],
        in_specs=[VMEM] * 8 + [ANY] * 3 + [SMEM] + [VMEM] * 5,
        out_specs=[VMEM] * 7,
        scratch_shapes=[
            pltpu.VMEM((32, 64, 256), BF16),
            pltpu.VMEM((32, 64, 256), BF16),
            pltpu.VMEM((4096, 256), BF16),
            pltpu.VMEM((4096, 256), BF16),
            pltpu.VMEM((2048, 256), BF16),
            pltpu.VMEM((2048, 256), BF16),
            pltpu.VMEM((2, 2048, 512), BF16),
            pltpu.VMEM((2, 2048, 512), BF16),
            pltpu.VMEM((2, 4096, 512), BF16),
            pltpu.VMEM((4, 4, 128, 512), BF16),
            pltpu.VMEM((4, 16, 128, 512), BF16),
            pltpu.VMEM((4, 2, 2, 2, 64, 512), BF16),
            pltpu.VMEM((4, 2, 2, 9, 64, 512), BF16),
            pltpu.VMEM((2, 4, 128, 512), F32),
            pltpu.VMEM((2, 256, 512), F32),
            pltpu.VMEM((2, 2, 256, 512), F32),
            pltpu.VMEM((4, 256, 512), BF16),
            pltpu.VMEM((8, 128), F32),
            pltpu.VMEM((8, 128), F32),
            pltpu.VMEM((16, 8, 128), F32),
            pltpu.VMEM((16, 8, 128), F32),
            DMA((2, 16)),
            DMA((2, 16)),
            DMA((4, 2, 4)),
            DMA((4, 2, 4)),
            DMA((4,)),
            DMA((3,)),
            DMA((4, 16)),
            DMA((4, 16)),
            DMA((4, 2, 2, 8)),
            DMA((4, 2, 2, 8)),
            DMA((4, 4)),
            DMA((4, 4)),
        ],
        compiler_params=params(2, 63),
    )(*args)


def body(
    hidden,
    dec_gain,
    neigh_states,
    enc_gain,
    w_query,
    w_key,
    w_value,
    w_out,
    neighbour_ids,
    neighbour_len,
    cotangent,
):
    t = lax.axis_index("tensor")
    rows = hidden.shape[0]
    dec_rows = hidden.astype(F32)
    enc_rows = neigh_states.astype(F32)
    count = neighbour_ids.shape[0]
    inverse = jnp.sum(
        jnp.where(
            neighbour_ids[None, :] == jnp.arange(count, dtype=jnp.int32)[:, None],
            jnp.arange(count, dtype=jnp.int32)[None, :],
            0,
        ),
        axis=1,
    )
    slots = jnp.arange(128, dtype=jnp.int32)[None, :]
    bias = jnp.where(slots < neighbour_len[:, None], 0.0, -jnp.inf).astype(F32)
    cot_all, dec_all, enc_all, wq, wk, wv, wo, att, qg, kg, vg, squares = front(
        cotangent.reshape(2, 64, 512),
        hidden.reshape(2, 64, 512),
        neigh_states,
        dec_gain[None],
        enc_gain[None],
        w_query,
        w_key,
        w_value,
        w_out,
        bias,
        inverse,
    )
    dec_input, out_total, enc_input, own, got, inner, gains = back(
        att,
        qg,
        kg,
        vg,
        wq,
        wk,
        wv,
        wo,
        cot_all.reshape(2, 2048, 512),
        dec_all.reshape(2, 2048, 512),
        enc_all,
        neighbour_ids,
        hidden,
        neigh_states,
        dec_gain[None],
        enc_gain[None],
        squares,
    )
    scales = lax.rsqrt(squares.reshape(-1)[:384] / WIDTH + EPS)
    dec_scale, enc_scale = scales[:rows, None], scales[rows:, None]
    dec_hat = dec_rows * dec_scale
    enc_hat = enc_rows * enc_scale
    got = got.astype(F32)
    joined = jnp.where(
        t == 0, jnp.concatenate([own, got], 1), jnp.concatenate([got, own], 1)
    )
    weight_grads = [joined[n].T for n in range(3)]
    out_weight_grad = joined[3]
    layer_out = (dec_rows + out_total).astype(BF16)
    dec_scaled = dec_gain * dec_input
    enc_scaled = enc_gain * enc_input
    inner = inner.reshape(-1)[:384] / WIDTH
    gains = gains.reshape(-1)
    hidden_grad = cotangent.astype(F32) + dec_scale * (
        dec_scaled - dec_hat * inner[:rows, None]
    )
    neighbour_grad = enc_scale * (enc_scaled - enc_hat * inner[rows:, None])
    return (
        layer_out,
        hidden_grad,
        neighbour_grad,
        gains[:512],
        gains[512:],
        weight_grads[0],
        weight_grads[1],
        weight_grads[2],
        out_weight_grad,
    )


def solution(mesh):
    features = ("section", "tensor")
    rows = P("seq", features)
    vector = P(features)
    columns = P(features, "seq")
    return jax.shard_map(
        body,
        mesh=mesh,
        in_specs=(
            rows,
            vector,
            rows,
            vector,
            columns,
            columns,
            columns,
            rows,
            P(),
            P(),
            rows,
        ),
        out_specs=(rows, rows, rows, vector, vector, columns, columns, columns, rows),
        check_vma=False,
    )
```

```python
import functools

import jax
import jax.numpy as jnp
from jax import lax
from jax.experimental import pallas as pl
from jax.experimental.pallas import tpu as pltpu
from jax.sharding import PartitionSpec as P

F32 = jnp.float32
BF16 = jnp.bfloat16
MESH = pl.DeviceIdType.MESH
EPS = 1e-05
WIDTH = 8192
ANY = pl.BlockSpec(memory_space=pl.ANY)
VMEM = pl.BlockSpec(memory_space=pltpu.VMEM)
SMEM = pl.BlockSpec(memory_space=pltpu.SMEM)
DMA = pltpu.SemaphoreType.DMA
RING = 16
DEPTH = 8


def place():
    z = lax.axis_index("section")
    s = lax.axis_index("seq")
    t = lax.axis_index("tensor")
    x = lax.div(lax.rem(s, 8), 2)
    y = lax.div(s, 8) * 2 + t
    return z, s, t, x, y, lax.rem(s, 2)


def ring_position(ring, x, y):
    return (y if ring == 0 else x) * 4 + lax.rem(x + y, 4)


def ring_chip(ring, p):
    a = lax.div(p, 4)
    b = lax.rem(lax.rem(p, 4) + 4 - a, 4)
    return (b, a) if ring == 0 else (a, b)


def seq_tensor(x, y, core):
    return lax.div(y, 2) * 8 + x * 2 + core, lax.rem(y, 2)


def ring_device(ring, p, core):
    x, y = ring_chip(ring, lax.rem(p + RING, RING))
    s, t = seq_tensor(x, y, core)
    return {"seq": s, "tensor": t}


def remote(src, dst, send_sem, recv_sem, device):
    return pltpu.make_async_remote_copy(
        src_ref=src,
        dst_ref=dst,
        send_sem=send_sem,
        recv_sem=recv_sem,
        device_id=device,
        device_id_type=MESH,
    )


def greet(devices):
    barrier = pltpu.get_barrier_semaphore()
    for device in devices:
        pl.semaphore_signal(barrier, inc=1, device_id=device, device_id_type=MESH)
    pl.semaphore_wait(barrier, len(devices))


def plane_neighbours(x, y, core, s):
    p1, p2 = ring_position(0, x, y), ring_position(1, x, y)
    return [
        ring_device(0, p1 + 1, core),
        ring_device(0, p1 - 1, core),
        ring_device(1, p2 + 1, core),
        ring_device(1, p2 - 1, core),
        {"seq": s + 1 - 2 * core},
    ]


def ring_neighbours(z):
    return [
        {"section": lax.rem(z + 1, DEPTH)},
        {"section": lax.rem(z + DEPTH - 1, DEPTH)},
    ]


def params(cid, mib=None):
    return pltpu.CompilerParams(
        collective_id=cid,
        has_side_effects=True,
        vmem_limit_bytes=None if mib is None else mib * 1024 * 1024,
    )


def dot(a, b):
    return jnp.dot(a, b, preferred_element_type=F32)


def dot_t(a, b):
    return lax.dot_general(a, b, (((1,), (1,)), ((), ())), preferred_element_type=F32)


def t_dot(a, b):
    return lax.dot_general(a, b, (((0,), (0,)), ((), ())), preferred_element_type=F32)


def split(a):
    high = a.astype(BF16)
    return high, (a - high.astype(F32)).astype(BF16)


def attend(units):
    scale = 128 ** (-0.5)
    scores = [dot_t(q, k) * scale + bias for q, a, k, v, bias in units]
    prob_grads = [dot_t(a, v) for q, a, k, v, bias in units]
    tops = [jnp.max(u, axis=1, keepdims=True) for u in scores]
    expos = [jnp.exp(u - top) for u, top in zip(scores, tops)]
    sums = [jnp.sum(u, axis=1, keepdims=True) for u in expos]
    probs = [u / total for u, total in zip(expos, sums)]
    lows = [u.astype(BF16) for u in probs]
    inners = [jnp.sum(u * g, axis=1, keepdims=True) for u, g in zip(probs, prob_grads)]
    score_grads = [u * (g - n) * scale for u, g, n in zip(probs, prob_grads, inners)]
    splits = [split(u) for u in score_grads]
    attended = [dot(low, u[3]).astype(BF16) for low, u in zip(lows, units)]
    query_grads = [
        (dot(high, u[2]) + dot(rest, u[2])).astype(BF16) for (high, rest), u in zip(splits, units)
    ]
    key_grads = [
        (t_dot(high, u[0]) + t_dot(rest, u[0])).astype(BF16)
        for (high, rest), u in zip(splits, units)
    ]
    value_grads = [t_dot(low, u[1]).astype(BF16) for low, u in zip(lows, units)]
    return list(zip(attended, query_grads, key_grads, value_grads))


def front_kernel(
    cot,
    hidden,
    neigh,
    dec_gain,
    enc_gain,
    wq_own,
    wk_own,
    wv_own,
    wo_own,
    bias,
    inverse,
    cot_all,
    dec_all,
    enc_all,
    wq_out,
    wk_out,
    wv_out,
    wo_out,
    att,
    qg,
    kg,
    vg,
    squares,
    cot_v,
    dec_v,
    enc_v,
    wq,
    wk,
    wv,
    wo,
    dec,
    enc,
    stat,
    stats,
    kv_send,
    kv_recv,
    qa_send,
    qa_recv,
    kv_fin,
    qa_fin,
    st_send,
    st_recv,
    p_send,
    p_recv,
    s_send,
    s_recv,
    own_sem,
    w_send,
    w_recv,
    w_own,
    out_sem,
    kv_ssem,
    kv_rsem,
    qa_ssem,
    qa_rsem,
):
    z, s, t, x, y, core = place()
    sibling = {"seq": s + 1 - 2 * core}
    partner = {"tensor": 1 - t}
    group = z * 2 + t

    def peer(r):
        g = lax.rem(group + r, 16)
        return {"section": lax.div(g, 2), "tensor": lax.rem(g, 2)}, g

    barrier = pltpu.get_barrier_semaphore()
    near = plane_neighbours(x, y, core, s)
    for device in near:
        pl.semaphore_signal(barrier, inc=1, device_id=device, device_id_type=MESH)

    def hello(r, _):
        pl.semaphore_signal(barrier, inc=1, device_id=peer(r)[0], device_id_type=MESH)
        return 0

    lax.fori_loop(1, 16, hello, 0)
    dec_rows = hidden[...].reshape(128, 512).astype(F32)
    enc_rows = neigh[...].astype(F32)
    sums = jnp.concatenate(
        [
            jnp.sum(dec_rows * dec_rows, axis=1, keepdims=True),
            jnp.sum(enc_rows * enc_rows, axis=1, keepdims=True),
        ],
        axis=0,
    )
    sums = jnp.broadcast_to(sums, (384, 128)).T[:1]
    stat[...] = jnp.zeros((8, 128), F32)
    for n in range(3):
        stat[n : n + 1] = sums[:, n * 128 : (n + 1) * 128]
    pl.semaphore_wait(barrier, len(near) + 15)


    def slot(k, sub, so, to, c):
        so = so + c
        if k == 0:
            return cot_v.at[to, so * 2 + sub]
        if k == 1:
            return dec_v.at[to, so * 2 + sub]
        return enc_v.at[to, pl.ds(pl.multiple_of(so * 256 + (k - 2) * 128 + sub * 64, 64), 64)]

    def source(k, sub):
        if k == 0:
            return cot.at[sub]
        if k == 1:
            return dec.at[sub]
        return enc.at[pl.ds((k - 2) * 128 + sub * 64, 64)]

    position = (ring_position(0, x, y), ring_position(1, x, y))
    own_so, own_to = seq_tensor(x, y, 0)
    nexts = [
        [ring_device(ring, position[ring] + 1 - 2 * way, core) for way in range(2)]
        for ring in range(2)
    ]

    def origins(j):
        return [
            [
                seq_tensor(
                    *ring_chip(
                        ring, lax.rem(position[ring] + RING - (1 - 2 * way) * j, RING)
                    ),
                    0,
                )
                for way in range(2)
            ]
            for ring in range(2)
        ]

    def onward(k, way, sub, j, src, dst):
        return remote(
            src, dst, p_send.at[k, way, sub, j], p_recv.at[k, way, sub, j], nexts[k % 2][way]
        )

    def across(k, way, sub, j, src, dst):
        return remote(src, dst, s_send.at[k, way, sub, j], s_recv.at[k, way, sub, j], sibling)

    def keep(k, sub):
        return pltpu.make_async_copy(
            source(k, sub), slot(k, sub, own_so, own_to, core), own_sem.at[k, sub]
        )

    def begin(ks):
        for sub in range(2):
            for way in range(2):
                for k in ks:
                    dst = slot(k, sub, own_so, own_to, core)
                    onward(k, way, sub, 0, source(k, sub), dst).start()
        for k in ks:
            for sub in range(2):
                dst = slot(k, sub, own_so, own_to, core)
                across(k, 0, sub, 0, source(k, sub), dst).start()
                keep(k, sub).start()

    def gather_step(ks, j):
        froms = origins(j + 1)
        for sub in range(2):
            for way in range(2):
                for k in ks:

                    @pl.when(j < 8 - way)
                    def _(k=k, way=way, sub=sub):
                        block = slot(k, sub, *froms[k % 2][way], core)
                        onward(k, way, sub, j, block, block).wait_recv()

                        @pl.when(j < 7 - way)
                        def _():
                            onward(k, way, sub, j + 1, block, block).start()

                        across(k, way, sub, j + 1, block, block).start()

    def gather_end(ks):
        def one(j, _):
            froms = origins(j + 1)
            for k in ks:
                for sub in range(2):
                    for way in range(2):

                        @pl.when(j < 8 - way)
                        def _(k=k, way=way, sub=sub):
                            src = source(k, sub)
                            block = slot(k, sub, *froms[k % 2][way], 1 - core)
                            onward(k, way, sub, j, src, src).wait_send()
                            across(k, way, sub, j + 1, src, src).wait_send()
                            across(k, way, sub, j + 1, block, block).wait_recv()

            return 0

        lax.fori_loop(0, 8, one, 0)
        for k in ks:
            for sub in range(2):
                src = source(k, sub)
                block = slot(k, sub, own_so, own_to, 1 - core)
                across(k, 0, sub, 0, src, src).wait_send()
                across(k, 0, sub, 0, block, block).wait_recv()
                keep(k, sub).wait()


    def tell(r):
        device, g = peer(r)
        return remote(stat, stats.at[group], st_send.at[r], st_recv.at[group], device)

    lax.fori_loop(1, 16, lambda r, _: (tell(r).start(), 0)[1], 0)
    half = pl.ds(pl.multiple_of(t * 256, 256), 256)
    rest = pl.ds(pl.multiple_of((1 - t) * 256, 256), 256)
    weights = ((wk_own, wk), (wv_own, wv), (wq_own, wq))
    swaps = [
        remote(w.at[:, rest], w_all.at[t], w_send.at[n], w_recv.at[n], partner)
        for n, (w, w_all) in enumerate(weights)
    ] + [remote(wo_own.at[rest, :], wo.at[t], w_send.at[3], w_recv.at[3], partner)]
    keeps = [
        pltpu.make_async_copy(w.at[:, half], w_all.at[t], w_own.at[n])
        for n, (w, w_all) in enumerate(weights)
    ] + [pltpu.make_async_copy(wo_own.at[half, :], wo.at[t], w_own.at[3])]
    for copy in swaps[:2]:
        copy.start()
    for copy in keeps:
        copy.start()
    stats[group] = stat[...]

    def hear(r, _):
        device, g = peer(r)
        remote(stat, stats.at[g], st_send.at[r], st_recv.at[g], device).wait_recv()
        return 0

    lax.fori_loop(1, 16, hear, 0)
    total = stats[0]
    for g in range(1, 16):
        total = total + stats[g]
    squares[...] = total
    scale = lax.rsqrt(total / WIDTH + EPS)
    scales = [jnp.broadcast_to(scale[n : n + 1], (128, 128)).T[:, :1] for n in range(3)]
    for n in range(2):
        rows = neigh[n * 128 : (n + 1) * 128].astype(F32)
        normed = rows * scales[n + 1] * enc_gain[...]
        enc[n * 128 : (n + 1) * 128] = normed.astype(BF16)
    begin((2, 3))
    rows = hidden[...].reshape(128, 512).astype(F32)
    dec[...] = (rows * scales[0] * dec_gain[...]).astype(BF16).reshape(2, 64, 512)

    def enc_step(j, _):
        gather_step((2, 3), j)

        @pl.when(j == 4)
        def _():
            begin((0, 1))

        @pl.when(j >= 6)
        def _():
            gather_step((0, 1), j - 6)

        return 0

    lax.fori_loop(0, 8, enc_step, 0)

    def zero(n, _):
        kv_recv[n, 0] = jnp.zeros((512, 256), BF16)
        qa_recv[n, 0] = jnp.zeros((256, 256), BF16)
        return 0

    lax.fori_loop(0, 4, zero, 0)
    for copy in swaps[2:]:
        copy.start()
    for copy in keeps:
        copy.wait()

    def swapped(n):
        swaps[n].wait_send()
        if n < 3:
            w, w_all = weights[n]
            dst = w_all.at[1 - t]
            remote(w.at[:, rest], dst, w_send.at[n], w_recv.at[n], partner).wait_recv()
        else:
            dst = wo.at[1 - t]
            remote(wo_own.at[rest, :], dst, w_send.at[n], w_recv.at[n], partner).wait_recv()

    swapped(0)
    swapped(1)
    gather_end((2, 3))
    stores = [
        pltpu.make_async_copy(src, dst, out_sem.at[n])
        for n, (src, dst) in enumerate(
            (
                (cot_v, cot_all),
                (dec_v, dec_all),
                (enc_v, enc_all),
                (wk, wk_out),
                (wv, wv_out),
                (wq, wq_out),
                (wo, wo_out),
            )
        )
    ]
    for copy in stores[2:5]:
        copy.start()


    def pair_part(d, h):
        stored = pl.ds(pl.multiple_of(d * 512 + h * 256, 256), 256)
        first, second = enc_v[0, stored, :], enc_v[1, stored, :]
        k = dot(first, wk[0]) + dot(second, wk[1])
        v = dot(first, wv[0]) + dot(second, wv[1])
        return ((0, 256, k), (256, 512, v))

    def query_part(d, h):
        j = d * 4 + h * 2
        b0, b1 = inverse[j], inverse[j + 1]
        q = a = 0.0
        for f in range(2):
            q = q + dot(jnp.concatenate([dec_v[f, b0], dec_v[f, b1]], axis=0), wq[f])
            a = a + dot_t(jnp.concatenate([cot_v[f, b0], cot_v[f, b1]], axis=0), wo[f])
        return ((0, 128, q), (128, 256, a))

    pairs = (kv_send, kv_recv, kv_ssem, kv_rsem, kv_fin, pair_part)
    queries = (qa_send, qa_recv, qa_ssem, qa_rsem, qa_fin, query_part)

    def chain(which, n, j, sign):
        sendb, recvb, ssem, rsem = which[:4]
        device = {"section": lax.rem(z + DEPTH + sign, DEPTH)}
        return remote(
            sendb.at[n, j], recvb.at[n, j + 1], ssem.at[n, j], rsem.at[n, j], device
        )

    def item(which, w):
        n, j = lax.rem(w, 4), lax.div(w, 4)
        h = lax.rem(n, 2)
        sign = 1 - 2 * lax.rem(h + lax.div(n, 2), 2)
        length = 4 - lax.div(n, 2)
        parts = which[5](lax.rem(z + DEPTH + sign * (length - j), DEPTH), h)

        @pl.when(j > 0)
        def _():
            chain(which, n, j - 1, sign).wait_recv()

        for lo, hi, part in parts:
            which[0][n, j, lo:hi] = (part + which[1][n, j, lo:hi].astype(F32)).astype(BF16)
        chain(which, n, j, sign).start()

    def last(which):
        def one(h, _):
            parts = which[5](z, h)
            chain(which, h, 3, 1).wait_recv()
            chain(which, h + 2, 2, 1).wait_recv()
            for lo, hi, part in parts:
                total = part + which[1][h, 4, lo:hi].astype(F32)
                total = total + which[1][h + 2, 3, lo:hi].astype(F32)
                which[4][h, lo:hi] = total.astype(BF16)
            return 0

        lax.fori_loop(0, 2, one, 0)

    def pair_item(w, _):
        item(pairs, w)

        @pl.when((lax.rem(w, 2) == 1) & (w > 2))
        def _():
            gather_step((0, 1), lax.div(w, 2) + 1)

        return 0

    lax.fori_loop(0, 14, pair_item, 0)
    gather_end((0, 1))
    swapped(2)
    swapped(3)
    for copy in stores[:2] + stores[5:]:
        copy.start()

    def query_item(w, _):
        item(queries, w)

        @pl.when(w == 7)
        def _():
            last(pairs)

        return 0

    lax.fori_loop(0, 14, query_item, 0)
    last(queries)

    for h in range(2):
        places = [(u, slice(g * 128, (g + 1) * 128)) for u in range(2) for g in range(2)]
        results = attend(
            [
                (
                    qa_fin[h, u * 64 : (u + 1) * 64, head],
                    qa_fin[h, 128 + u * 64 : 128 + (u + 1) * 64, head],
                    kv_fin[h, u * 128 : (u + 1) * 128, head],
                    kv_fin[h, 256 + u * 128 : 256 + (u + 1) * 128, head],
                    bias[pl.ds(z * 4 + h * 2 + u, 1), :],
                )
                for u, head in places
            ]
        )
        for (u, head), (attended, query_grad, key_grad, value_grad) in zip(places, results):
            n = h * 2 + u
            att[n, :, head] = attended
            qg[n, :, head] = query_grad
            kg[n * 128 : (n + 1) * 128, head] = key_grad
            vg[n * 128 : (n + 1) * 128, head] = value_grad

    def chain_end(w, _):
        chain(pairs, lax.rem(w, 4), lax.div(w, 4), 1).wait_send()
        chain(queries, lax.rem(w, 4), lax.div(w, 4), 1).wait_send()
        return 0

    lax.fori_loop(0, 14, chain_end, 0)
    lax.fori_loop(1, 16, lambda r, _: (tell(r).wait_send(), 0)[1], 0)
    for copy in stores:
        copy.wait()


def front(*args):
    sds = jax.ShapeDtypeStruct
    return pl.pallas_call(
        front_kernel,
        out_shape=[
            sds((2, 32, 64, 512), BF16),
            sds((2, 32, 64, 512), BF16),
            sds((2, 4096, 512), BF16),
            sds((2, 512, 256), BF16),
            sds((2, 512, 256), BF16),
            sds((2, 512, 256), BF16),
            sds((2, 256, 512), BF16),
            sds((4, 64, 256), BF16),
            sds((4, 64, 256), BF16),
            sds((512, 256), BF16),
            sds((512, 256), BF16),
            sds((8, 128), F32),
        ],
        in_specs=[VMEM] * 5 + [ANY] * 4 + [VMEM, SMEM],
        out_specs=[ANY] * 7 + [VMEM] * 5,
        scratch_shapes=[
            pltpu.VMEM((2, 32, 64, 512), BF16),
            pltpu.VMEM((2, 32, 64, 512), BF16),
            pltpu.VMEM((2, 4096, 512), BF16),
            pltpu.VMEM((2, 512, 256), BF16),
            pltpu.VMEM((2, 512, 256), BF16),
            pltpu.VMEM((2, 512, 256), BF16),
            pltpu.VMEM((2, 256, 512), BF16),
            pltpu.VMEM((2, 64, 512), BF16),
            pltpu.VMEM((256, 512), BF16),
            pltpu.VMEM((8, 128), F32),
            pltpu.VMEM((16, 8, 128), F32),
            pltpu.VMEM((4, 4, 512, 256), BF16),
            pltpu.VMEM((4, 5, 512, 256), BF16),
            pltpu.VMEM((4, 4, 256, 256), BF16),
            pltpu.VMEM((4, 5, 256, 256), BF16),
            pltpu.VMEM((2, 512, 256), BF16),
            pltpu.VMEM((2, 256, 256), BF16),
            DMA((16,)),
            DMA((16,)),
            DMA((4, 2, 2, 8)),
            DMA((4, 2, 2, 8)),
            DMA((4, 2, 2, 9)),
            DMA((4, 2, 2, 9)),
            DMA((4, 2)),
            DMA((4,)),
            DMA((4,)),
            DMA((4,)),
            DMA((7,)),
            DMA((4, 4)),
            DMA((4, 4)),
            DMA((4, 4)),
            DMA((4, 4)),
        ],
        compiler_params=params(1, 60),
    )(*args)


def back_kernel(
    att_own,
    qg_own,
    kg_own,
    vg_own,
    wq_hbm,
    wk_hbm,
    wv_hbm,
    wo_hbm,
    cot_hbm,
    dec_hbm,
    enc_hbm,
    ids,
    hidden,
    neigh,
    dec_gain,
    enc_gain,
    squares,
    dec_out,
    out_out,
    enc_out,
    grads,
    out_grad,
    grads_in,
    out_grad_in,
    inner_out,
    gain_out,
    att_all,
    qg_all,
    kg_all,
    vg_all,
    att,
    qg,
    cot,
    dec,
    enc,
    wq,
    wk,
    wv,
    wo,
    sib_out,
    sib_in,
    chain_out,
    chain_in,
    mine,
    acc,
    out_acc,
    pair_acc,
    grads_out,
    out_grad_out,
    inner,
    gains,
    inners,
    gainses,
    e_send,
    e_recv,
    g_send,
    g_recv,
    own_sem,
    x_sem,
    s_send,
    s_recv,
    c_send,
    c_recv,
    w_send,
    w_recv,
    o_sem,
):
    z, s, t, x, y, core = place()
    sibling = {"seq": s + 1 - 2 * core}
    partner = {"tensor": 1 - t}
    position = (ring_position(0, x, y), ring_position(1, x, y))
    loads = [
        pltpu.make_async_copy(src, dst, x_sem.at[n])
        for n, (src, dst) in enumerate(
            (
                (cot_hbm, cot),
                (dec_hbm, dec),
                (enc_hbm, enc),
                (wq_hbm, wq),
                (wk_hbm, wk),
                (wv_hbm, wv),
                (wo_hbm, wo),
            )
        )
    ]
    nexts = [
        [ring_device(ring, position[ring] + 1 - 2 * way, core) for way in range(2)]
        for ring in range(2)
    ]
    owns = (att_own, qg_own, kg_own, vg_own)
    alls = (att_all, qg_all, kg_all, vg_all)
    group = z * 2 + t
    sums = ((inner, inners, inner_out, group), (gains, gainses, gain_out, s))

    def peer(n, r):
        g = lax.rem(sums[n][3] + r, 16)
        return ({"section": lax.div(g, 2), "tensor": lax.rem(g, 2)} if n == 0 else {"seq": g}), g

    barrier = pltpu.get_barrier_semaphore()
    near = plane_neighbours(x, y, core, s)
    for device in near:
        pl.semaphore_signal(barrier, inc=1, device_id=device, device_id_type=MESH)

    def hello(r, _):
        for n in range(2):
            pl.semaphore_signal(barrier, inc=1, device_id=peer(n, r)[0], device_id_type=MESH)
        return 0

    lax.fori_loop(1, 16, hello, 0)
    pl.semaphore_wait(barrier, len(near) + 30)


    def ring_block(n, place_z):
        if n < 2:
            return alls[n].at[pl.ds(place_z * 4, 4)]
        return alls[n].at[pl.ds(pl.multiple_of(place_z * 512, 512), 512)]

    def ring_hops(n, way):
        return 4 if n % 2 == way else 3

    def ring_copy(n, way, j, src=None):
        sign = 1 - 2 * way
        block = ring_block(n, lax.rem(z + DEPTH - sign * j, DEPTH))
        device = {"section": lax.rem(z + DEPTH + sign, DEPTH)}
        return remote(
            block if src is None else src, block, g_send.at[n, way, j], g_recv.at[n, way, j], device
        )

    def ring_first(ns):
        for n in ns:
            for way in range(2):
                ring_copy(n, way, 0, owns[n]).start()

    def ring_step(ns, j):
        for n in ns:
            for way in range(2):

                @pl.when(j < ring_hops(n, way))
                def _(n=n, way=way):
                    sign = 1 - 2 * way
                    block = ring_block(n, lax.rem(z + DEPTH - sign * (j + 1), DEPTH))
                    remote(
                        block,
                        block,
                        g_send.at[n, way, j],
                        g_recv.at[n, way, j],
                        ring_neighbours(z)[0],
                    ).wait_recv()

                    @pl.when(j + 1 < ring_hops(n, way))
                    def _():
                        ring_copy(n, way, j + 1).start()

    def keep(n):
        return pltpu.make_async_copy(owns[n], ring_block(n, z), own_sem.at[n])

    ring_first((0, 1))
    for n in range(4):
        keep(n).start()
    for copy in loads[2:] + loads[:2]:
        copy.start()
    for k in range(4):
        for way in range(2):
            for sub in range(2):
                chain_in[k, way, sub, 0] = jnp.zeros((64, 512), BF16)

    def pair_weights(place_z):
        rows = pl.ds(pl.multiple_of(place_z * 512, 512), 512)
        block = jnp.concatenate([kg_all[rows, :], vg_all[rows, :]], axis=1)
        for f in range(2):
            pair_acc[f] += t_dot(enc[f, rows, :], block)

    pair_acc[...] = jnp.zeros((2, 512, 512), F32)

    def first_steps(j, _):
        ring_step((0, 1), j)

        @pl.when(j == 1)
        def _():
            loads[2].wait()
            keep(2).wait()
            keep(3).wait()
            pair_weights(z)

        @pl.when(j == 2)
        def _():
            ring_first((2, 3))

        return 0

    lax.fori_loop(0, 4, first_steps, 0)
    keep(0).wait()
    keep(1).wait()
    for copy in loads[3:]:
        copy.wait()

    def token_order(b, _):
        rows = pl.ds(pl.multiple_of(b * 64, 64), 64)
        att[rows, :] = att_all[ids[b]]
        qg[rows, :] = qg_all[ids[b]]
        return 0

    lax.fori_loop(0, 32, token_order, 0)


    def dest(ring, offset):
        cx, cy = ring_chip(ring, lax.rem(position[ring] + offset, RING))
        return seq_tensor(cx, cy, 0)

    def both(ref, base, stride):
        return jnp.concatenate(
            [
                ref[pl.ds(pl.multiple_of(base + c * stride, 128), 128), :]
                for c in (core, 1 - core)
            ],
            axis=0,
        )

    def product(k, offset):
        sd, td = dest(k % 2, offset)
        if k == 0:
            return dot_t(both(qg, sd * 128, 128), wq[td])
        if k == 1:
            return dot(both(att, sd * 128, 128), wo[td])
        base = sd * 256 + (k - 2) * 128
        return dot_t(both(kg_all, base, 256), wk[td]) + dot_t(both(vg_all, base, 256), wv[td])

    def across(k, i, four=0):
        return remote(
            sib_out.at[k, four],
            sib_in.at[k, i],
            s_send.at[k, i],
            s_recv.at[k, i],
            sibling,
        )

    def give(ks, i):
        half = lax.div(i, 2)
        four = lax.rem(i, 4)
        offset = 8 - half + (i - 2 * half) * (2 * half + 1)
        for k in ks:
            total = product(k, offset)

            @pl.when(i >= 4)
            def _(k=k):
                across(k, i - 4, four).wait_send()

            sib_out[k, four] = total[128:].astype(BF16)
            across(k, i, four).start()
            mine[k % 2, four] = total[:128]

    def onward(k, way, sub, j, two):
        return remote(
            chain_out.at[k, way, sub, two],
            chain_in.at[k, way, sub, j + 1],
            c_send.at[k, way, sub, j],
            c_recv.at[k, way, sub, j],
            nexts[k % 2][way],
        )

    def chain_step(ks, j):
        two = lax.rem(j, 2)
        for sub in range(2):
            part = slice(sub * 64, (sub + 1) * 64)
            for way in range(2):
                for k in ks:

                    @pl.when(j < 8 - way)
                    def _(k=k, way=way, sub=sub, part=part):
                        i = 2 * j + way
                        four = 2 * two + way
                        if sub == 0:
                            across(k, i).wait_recv()

                        @pl.when(j > 0)
                        def _():
                            onward(k, way, sub, j - 1, two).wait_recv()

                        @pl.when(j > 1)
                        def _():
                            onward(k, way, sub, j - 2, two).wait_send()

                        total = mine[k % 2, four, part] + sib_in[k, i, part].astype(F32)
                        total = total + chain_in[k, way, sub, j].astype(F32)
                        chain_out[k, way, sub, two] = total.astype(BF16)
                        onward(k, way, sub, j, two).start()

    def own_store(n):
        if n == 0:
            src, dst = acc, grads.at[0]
        elif n == 3:
            src, dst = out_acc, out_grad
        else:
            src, dst = pair_acc.at[t, :, pl.ds((n - 1) * 256, 256)], grads.at[n]
        return pltpu.make_async_copy(src, dst, o_sem.at[n])

    def query_swap():
        return remote(
            grads_out.at[0], grads_in.at[0], w_send.at[0, 0], w_recv.at[0, 0], partner
        )

    def out_swap():
        return remote(out_grad_out, out_grad_in, w_send.at[3, 0], w_recv.at[3, 0], partner)

    def pair_swap(j):
        n, m = 1 + lax.div(j, 4), lax.rem(j, 4)
        rows = pl.ds(pl.multiple_of(m * 128, 128), 128)
        return remote(
            grads_out.at[n, rows], grads_in.at[n, rows], w_send.at[n, m], w_recv.at[n, m], partner
        )

    def weight_step(j):
        f = 1 - t + lax.div(j, 4) * (2 * t - 1)
        here = pl.ds(pl.multiple_of(lax.rem(j, 4) * 512, 512), 512)

        @pl.when(lax.rem(j, 4) == 0)
        def _():
            acc[...] = jnp.zeros((512, 256), F32)
            out_acc[...] = jnp.zeros((256, 512), F32)

        acc[...] += t_dot(dec[f, here, :], qg[here, :])
        out_acc[...] += t_dot(att[here, :], cot[f, here, :])

        @pl.when(j == 3)
        def _():
            grads_out[0] = acc[...].astype(BF16)
            out_grad_out[...] = out_acc[...].astype(BF16)
            query_swap().start()
            out_swap().start()

        @pl.when(j == 7)
        def _():
            own_store(0).start()
            own_store(3).start()

    def scatter(ks, filler):
        give(ks, 0)
        give(ks, 1)

        def step(j, _):
            chain_step(ks, j)

            @pl.when(j < 7)
            def _():
                lax.fori_loop(2 * j + 2, 2 * j + 4, lambda i, _: (give(ks, i), 0)[1], 0)

            filler(j)
            return 0

        lax.fori_loop(0, 8, step, 0)
        outs = {
            0: dec_out,
            1: out_out,
            2: enc_out.at[pl.ds(0, 128)],
            3: enc_out.at[pl.ds(128, 128)],
        }
        for k in ks:
            across(k, 15).wait_recv()
            for sub in range(2):
                part = pl.ds(sub * 64, 64)
                total = mine[k % 2, 3, part] + sib_in[k, 15, part].astype(F32)
                for way in range(2):
                    onward(k, way, sub, 7 - way, 0).wait_recv()
                    total = total + chain_in[k, way, sub, 8 - way].astype(F32)
                outs[k][part, :] = total
        for k in ks:
            for i in range(12, 16):
                across(k, i).wait_send()
            for way in range(2):
                for sub in range(2):
                    onward(k, way, sub, 6 - way, 0).wait_send()
                    onward(k, way, sub, 7 - way, 1).wait_send()

    def token_filler(j):
        @pl.when(j == 0)
        def _():
            loads[0].wait()
            loads[1].wait()

        weight_step(j)

        @pl.when((lax.rem(j, 2) == 0) & (j > 0))
        def _():
            distance = lax.div(j, 2)
            pair_weights(lax.rem(z + distance, DEPTH))
            pair_weights(lax.rem(z + DEPTH - distance, DEPTH))

        @pl.when(lax.rem(j, 2) == 1)
        def _():
            ring_step((2, 3), lax.div(j, 2))

    inner[...] = jnp.zeros((8, 128), F32)
    gains[...] = jnp.zeros((8, 128), F32)
    scale = lax.rsqrt(squares[...] / WIDTH + EPS)
    scales = [jnp.broadcast_to(scale[n : n + 1], (128, 128)).T[:, :1] for n in range(3)]
    scatter((0, 1), token_filler)

    def sum_rows(n):
        part = slice(max(n - 1, 0) * 128, max(n - 1, 0) * 128 + 128)
        upstream = dec_out[...] if n == 0 else enc_out[part, :]
        unit = (hidden if n == 0 else neigh)[part, :].astype(F32) * scales[n]
        product_of = upstream * unit
        gain = (dec_gain if n == 0 else enc_gain)[...]
        column = jnp.sum(product_of * gain, axis=1, keepdims=True)
        inner[n : n + 1] = jnp.broadcast_to(column, (128, 128)).T[:1]
        row = jnp.sum(product_of, axis=0, keepdims=True)
        first = 0 if n == 0 else 4
        for m in range(4):
            gains[first + m : first + m + 1] += row[:, m * 128 : (m + 1) * 128]

    def pair_filler(j):
        @pl.when(j == 0)
        def _():
            pair_weights(lax.rem(z + 4, DEPTH))
            for a in range(2):
                half = slice(a * 256, (a + 1) * 256)
                grads_out[1 + a] = pair_acc[1 - t, :, half].astype(BF16)
                own_store(1 + a).start()

        pair_swap(j).start()

        @pl.when(j == 1)
        def _():
            sum_rows(0)

    scatter((2, 3), pair_filler)


    sum_rows(1)
    sum_rows(2)

    def tell(n, r):
        src, slots, _out, own = sums[n]
        return remote(src, slots.at[own], e_send.at[n, r], e_recv.at[n, own], peer(n, r)[0])

    def tell_all(r, _):
        for n in range(2):
            tell(n, r).start()
        return 0

    def hear_all(r, _):
        for n in range(2):
            src, slots, _out, own = sums[n]
            device, g = peer(n, r)
            remote(src, slots.at[g], e_send.at[n, r], e_recv.at[n, g], device).wait_recv()
        return 0

    def told_all(r, _):
        for n in range(2):
            tell(n, r).wait_send()
        return 0

    lax.fori_loop(1, 16, tell_all, 0)
    for src, slots, _out, own in sums:
        slots[own] = src[...]

    for n in range(4):
        for way in range(2):
            for j in range(ring_hops(n, way)):
                ring_copy(n, way, j).wait_send()
    query_swap().wait()
    out_swap().wait()
    for n in range(4):
        own_store(n).wait()
    lax.fori_loop(0, 8, lambda j, _: (pair_swap(j).wait(), 0)[1], 0)
    lax.fori_loop(1, 16, hear_all, 0)
    for src, slots, out, own in sums:
        total = slots[0]
        for g in range(1, 16):
            total = total + slots[g]
        out[...] = total
    lax.fori_loop(1, 16, told_all, 0)


def back(*args):
    sds = jax.ShapeDtypeStruct
    return pl.pallas_call(
        back_kernel,
        out_shape=[
            sds((128, 512), F32),
            sds((128, 512), F32),
            sds((256, 512), F32),
            sds((3, 512, 256), F32),
            sds((256, 512), F32),
            sds((3, 512, 256), BF16),
            sds((256, 512), BF16),
            sds((8, 128), F32),
            sds((8, 128), F32),
        ],
        in_specs=[VMEM] * 4 + [ANY] * 7 + [SMEM] + [VMEM] * 5,
        out_specs=[VMEM] * 3 + [ANY] * 4 + [VMEM] * 2,
        scratch_shapes=[
            pltpu.VMEM((32, 64, 256), BF16),
            pltpu.VMEM((32, 64, 256), BF16),
            pltpu.VMEM((4096, 256), BF16),
            pltpu.VMEM((4096, 256), BF16),
            pltpu.VMEM((2048, 256), BF16),
            pltpu.VMEM((2048, 256), BF16),
            pltpu.VMEM((2, 2048, 512), BF16),
            pltpu.VMEM((2, 2048, 512), BF16),
            pltpu.VMEM((2, 4096, 512), BF16),
            pltpu.VMEM((2, 512, 256), BF16),
            pltpu.VMEM((2, 512, 256), BF16),
            pltpu.VMEM((2, 512, 256), BF16),
            pltpu.VMEM((2, 256, 512), BF16),
            pltpu.VMEM((4, 4, 128, 512), BF16),
            pltpu.VMEM((4, 16, 128, 512), BF16),
            pltpu.VMEM((4, 2, 2, 2, 64, 512), BF16),
            pltpu.VMEM((4, 2, 2, 9, 64, 512), BF16),
            pltpu.VMEM((2, 4, 128, 512), F32),
            pltpu.VMEM((512, 256), F32),
            pltpu.VMEM((256, 512), F32),
            pltpu.VMEM((2, 512, 512), F32),
            pltpu.VMEM((3, 512, 256), BF16),
            pltpu.VMEM((256, 512), BF16),
            pltpu.VMEM((8, 128), F32),
            pltpu.VMEM((8, 128), F32),
            pltpu.VMEM((16, 8, 128), F32),
            pltpu.VMEM((16, 8, 128), F32),
            DMA((2, 16)),
            DMA((2, 16)),
            DMA((4, 2, 4)),
            DMA((4, 2, 4)),
            DMA((4,)),
            DMA((7,)),
            DMA((4, 16)),
            DMA((4, 16)),
            DMA((4, 2, 2, 8)),
            DMA((4, 2, 2, 8)),
            DMA((4, 4)),
            DMA((4, 4)),
            DMA((4,)),
        ],
        compiler_params=params(2, 63),
    )(*args)


def body(
    hidden,
    dec_gain,
    neigh_states,
    enc_gain,
    w_query,
    w_key,
    w_value,
    w_out,
    neighbour_ids,
    neighbour_len,
    cotangent,
):
    t = lax.axis_index("tensor")
    rows = hidden.shape[0]
    dec_rows = hidden.astype(F32)
    enc_rows = neigh_states.astype(F32)
    count = neighbour_ids.shape[0]
    inverse = jnp.sum(
        jnp.where(
            neighbour_ids[None, :] == jnp.arange(count, dtype=jnp.int32)[:, None],
            jnp.arange(count, dtype=jnp.int32)[None, :],
            0,
        ),
        axis=1,
    )
    slots = jnp.arange(128, dtype=jnp.int32)[None, :]
    bias = jnp.where(slots < neighbour_len[:, None], 0.0, -jnp.inf).astype(F32)
    cot_all, dec_all, enc_all, wq, wk, wv, wo, att, qg, kg, vg, squares = front(
        cotangent.reshape(2, 64, 512),
        hidden.reshape(2, 64, 512),
        neigh_states,
        dec_gain[None],
        enc_gain[None],
        w_query,
        w_key,
        w_value,
        w_out,
        bias,
        inverse,
    )
    dec_input, out_total, enc_input, own, out_own, got, out_got, inner, gains = back(
        att,
        qg,
        kg,
        vg,
        wq,
        wk,
        wv,
        wo,
        cot_all.reshape(2, 2048, 512),
        dec_all.reshape(2, 2048, 512),
        enc_all,
        neighbour_ids,
        hidden,
        neigh_states,
        dec_gain[None],
        enc_gain[None],
        squares,
    )
    scales = lax.rsqrt(squares.reshape(-1)[:384] / WIDTH + EPS)
    dec_scale, enc_scale = scales[:rows, None], scales[rows:, None]
    dec_hat = dec_rows * dec_scale
    enc_hat = enc_rows * enc_scale

    def join(mine, theirs, axis):
        theirs = theirs.astype(F32)
        return jnp.where(
            t == 0,
            jnp.concatenate([mine, theirs], axis),
            jnp.concatenate([theirs, mine], axis),
        )

    weight_grads = [join(own[n], got[n], 1) for n in range(3)]
    out_weight_grad = join(out_own, out_got, 0)
    layer_out = (dec_rows + out_total).astype(BF16)
    dec_scaled = dec_gain * dec_input
    enc_scaled = enc_gain * enc_input
    inner = inner.reshape(-1)[:384] / WIDTH
    gains = gains.reshape(-1)
    hidden_grad = cotangent.astype(F32) + dec_scale * (
        dec_scaled - dec_hat * inner[:rows, None]
    )
    neighbour_grad = enc_scale * (enc_scaled - enc_hat * inner[rows:, None])
    return (
        layer_out,
        hidden_grad,
        neighbour_grad,
        gains[:512],
        gains[512:],
        weight_grads[0],
        weight_grads[1],
        weight_grads[2],
        out_weight_grad,
    )


def solution(mesh):
    features = ("section", "tensor")
    rows = P("seq", features)
    vector = P(features)
    columns = P(features, "seq")
    return jax.shard_map(
        body,
        mesh=mesh,
        in_specs=(
            rows,
            vector,
            rows,
            vector,
            columns,
            columns,
            columns,
            rows,
            P(),
            P(),
            rows,
        ),
        out_specs=(rows, rows, rows, vector, vector, columns, columns, columns, rows),
        check_vma=False,
    )
```

```python
import functools

import jax
import jax.numpy as jnp
from jax import lax
from jax.experimental import pallas as pl
from jax.experimental.pallas import tpu as pltpu
from jax.sharding import PartitionSpec as P

F32 = jnp.float32
BF16 = jnp.bfloat16
MESH = pl.DeviceIdType.MESH
EPS = 1e-05
WIDTH = 8192
ANY = pl.BlockSpec(memory_space=pl.ANY)
VMEM = pl.BlockSpec(memory_space=pltpu.VMEM)
SMEM = pl.BlockSpec(memory_space=pltpu.SMEM)
DMA = pltpu.SemaphoreType.DMA
RING = 16
DEPTH = 8


def place():
    z = lax.axis_index("section")
    s = lax.axis_index("seq")
    t = lax.axis_index("tensor")
    x = lax.div(lax.rem(s, 8), 2)
    y = lax.div(s, 8) * 2 + t
    return z, s, t, x, y, lax.rem(s, 2)


def ring_position(ring, x, y):
    return (y if ring == 0 else x) * 4 + lax.rem(x + y, 4)


def ring_chip(ring, p):
    a = lax.div(p, 4)
    b = lax.rem(lax.rem(p, 4) + 4 - a, 4)
    return (b, a) if ring == 0 else (a, b)


def seq_tensor(x, y, core):
    return lax.div(y, 2) * 8 + x * 2 + core, lax.rem(y, 2)


def ring_device(ring, p, core):
    x, y = ring_chip(ring, lax.rem(p + RING, RING))
    s, t = seq_tensor(x, y, core)
    return {"seq": s, "tensor": t}


def remote(src, dst, send_sem, recv_sem, device):
    return pltpu.make_async_remote_copy(
        src_ref=src,
        dst_ref=dst,
        send_sem=send_sem,
        recv_sem=recv_sem,
        device_id=device,
        device_id_type=MESH,
    )


def greet(devices):
    barrier = pltpu.get_barrier_semaphore()
    for device in devices:
        pl.semaphore_signal(barrier, inc=1, device_id=device, device_id_type=MESH)
    pl.semaphore_wait(barrier, len(devices))


def plane_neighbours(x, y, core, s):
    p1, p2 = ring_position(0, x, y), ring_position(1, x, y)
    return [
        ring_device(0, p1 + 1, core),
        ring_device(0, p1 - 1, core),
        ring_device(1, p2 + 1, core),
        ring_device(1, p2 - 1, core),
        {"seq": s + 1 - 2 * core},
    ]


def ring_neighbours(z):
    return [
        {"section": lax.rem(z + 1, DEPTH)},
        {"section": lax.rem(z + DEPTH - 1, DEPTH)},
    ]


def params(cid, mib=None):
    return pltpu.CompilerParams(
        collective_id=cid,
        has_side_effects=True,
        vmem_limit_bytes=None if mib is None else mib * 1024 * 1024,
    )


def dot(a, b):
    return jnp.dot(a, b, preferred_element_type=F32)


def dot_t(a, b):
    return lax.dot_general(a, b, (((1,), (1,)), ((), ())), preferred_element_type=F32)


def t_dot(a, b):
    return lax.dot_general(a, b, (((0,), (0,)), ((), ())), preferred_element_type=F32)


def split(a):
    high = a.astype(BF16)
    return high, (a - high.astype(F32)).astype(BF16)


def attend(units):
    scale = 128 ** (-0.5)
    scores = [dot_t(q, k) * scale + bias for q, a, k, v, bias in units]
    prob_grads = [dot_t(a, v) for q, a, k, v, bias in units]
    tops = [jnp.max(u, axis=1, keepdims=True) for u in scores]
    expos = [jnp.exp(u - top) for u, top in zip(scores, tops)]
    sums = [jnp.sum(u, axis=1, keepdims=True) for u in expos]
    probs = [u / total for u, total in zip(expos, sums)]
    lows = [u.astype(BF16) for u in probs]
    inners = [jnp.sum(u * g, axis=1, keepdims=True) for u, g in zip(probs, prob_grads)]
    score_grads = [u * (g - n) * scale for u, g, n in zip(probs, prob_grads, inners)]
    splits = [split(u) for u in score_grads]
    attended = [dot(low, u[3]).astype(BF16) for low, u in zip(lows, units)]
    query_grads = [
        (dot(high, u[2]) + dot(rest, u[2])).astype(BF16) for (high, rest), u in zip(splits, units)
    ]
    key_grads = [
        (t_dot(high, u[0]) + t_dot(rest, u[0])).astype(BF16)
        for (high, rest), u in zip(splits, units)
    ]
    value_grads = [t_dot(low, u[1]).astype(BF16) for low, u in zip(lows, units)]
    return list(zip(attended, query_grads, key_grads, value_grads))


def front_kernel(
    cot,
    hidden,
    neigh,
    dec_gain,
    enc_gain,
    wq_own,
    wk_own,
    wv_own,
    wo_own,
    bias,
    inverse,
    cot_all,
    dec_all,
    enc_all,
    wq_out,
    wk_out,
    wv_out,
    wo_out,
    att,
    qg,
    kg,
    vg,
    squares,
    cot_v,
    dec_v,
    enc_v,
    wq,
    wk,
    wv,
    wo,
    dec,
    enc,
    stat,
    stats,
    kv_send,
    kv_recv,
    qa_send,
    qa_recv,
    kv_fin,
    qa_fin,
    st_send,
    st_recv,
    p_send,
    p_recv,
    s_send,
    s_recv,
    own_sem,
    w_send,
    w_recv,
    w_own,
    out_sem,
    kv_ssem,
    kv_rsem,
    qa_ssem,
    qa_rsem,
):
    z, s, t, x, y, core = place()
    sibling = {"seq": s + 1 - 2 * core}
    partner = {"tensor": 1 - t}
    group = z * 2 + t

    def peer(r):
        g = lax.rem(group + r, 16)
        return {"section": lax.div(g, 2), "tensor": lax.rem(g, 2)}, g

    barrier = pltpu.get_barrier_semaphore()
    near = plane_neighbours(x, y, core, s)
    for device in near:
        pl.semaphore_signal(barrier, inc=1, device_id=device, device_id_type=MESH)

    def hello(r, _):
        pl.semaphore_signal(barrier, inc=1, device_id=peer(r)[0], device_id_type=MESH)
        return 0

    lax.fori_loop(1, 16, hello, 0)
    dec_rows = hidden[...].reshape(128, 512).astype(F32)
    enc_rows = neigh[...].astype(F32)
    sums = jnp.concatenate(
        [
            jnp.sum(dec_rows * dec_rows, axis=1, keepdims=True),
            jnp.sum(enc_rows * enc_rows, axis=1, keepdims=True),
        ],
        axis=0,
    )
    sums = jnp.broadcast_to(sums, (384, 128)).T[:1]
    stat[...] = jnp.zeros((8, 128), F32)
    for n in range(3):
        stat[n : n + 1] = sums[:, n * 128 : (n + 1) * 128]
    pl.semaphore_wait(barrier, len(near) + 15)


    def slot(k, sub, so, to, c):
        so = so + c
        if k == 0:
            return cot_v.at[to, so * 2 + sub]
        if k == 1:
            return dec_v.at[to, so * 2 + sub]
        return enc_v.at[to, pl.ds(pl.multiple_of(so * 256 + (k - 2) * 128 + sub * 64, 64), 64)]

    def source(k, sub):
        if k == 0:
            return cot.at[sub]
        if k == 1:
            return dec.at[sub]
        return enc.at[pl.ds((k - 2) * 128 + sub * 64, 64)]

    position = (ring_position(0, x, y), ring_position(1, x, y))
    own_so, own_to = seq_tensor(x, y, 0)
    nexts = [
        [ring_device(ring, position[ring] + 1 - 2 * way, core) for way in range(2)]
        for ring in range(2)
    ]

    def origins(j):
        return [
            [
                seq_tensor(
                    *ring_chip(
                        ring, lax.rem(position[ring] + RING - (1 - 2 * way) * j, RING)
                    ),
                    0,
                )
                for way in range(2)
            ]
            for ring in range(2)
        ]

    def onward(k, way, sub, j, src, dst):
        return remote(
            src, dst, p_send.at[k, way, sub, j], p_recv.at[k, way, sub, j], nexts[k % 2][way]
        )

    def across(k, way, sub, j, src, dst):
        return remote(src, dst, s_send.at[k, way, sub, j], s_recv.at[k, way, sub, j], sibling)

    def keep(k, sub):
        return pltpu.make_async_copy(
            source(k, sub), slot(k, sub, own_so, own_to, core), own_sem.at[k, sub]
        )

    def begin(ks):
        for sub in range(2):
            for way in range(2):
                for k in ks:
                    dst = slot(k, sub, own_so, own_to, core)
                    onward(k, way, sub, 0, source(k, sub), dst).start()
        for k in ks:
            for sub in range(2):
                dst = slot(k, sub, own_so, own_to, core)
                across(k, 0, sub, 0, source(k, sub), dst).start()
                keep(k, sub).start()

    def gather_step(ks, j):
        froms = origins(j + 1)
        for sub in range(2):
            for way in range(2):
                for k in ks:

                    @pl.when(j < 8 - way)
                    def _(k=k, way=way, sub=sub):
                        block = slot(k, sub, *froms[k % 2][way], core)
                        onward(k, way, sub, j, block, block).wait_recv()

                        @pl.when(j < 7 - way)
                        def _():
                            onward(k, way, sub, j + 1, block, block).start()

                        across(k, way, sub, j + 1, block, block).start()

    def gather_end(ks):
        def one(j, _):
            froms = origins(j + 1)
            for k in ks:
                for sub in range(2):
                    for way in range(2):

                        @pl.when(j < 8 - way)
                        def _(k=k, way=way, sub=sub):
                            src = source(k, sub)
                            block = slot(k, sub, *froms[k % 2][way], 1 - core)
                            onward(k, way, sub, j, src, src).wait_send()
                            across(k, way, sub, j + 1, src, src).wait_send()
                            across(k, way, sub, j + 1, block, block).wait_recv()

            return 0

        lax.fori_loop(0, 8, one, 0)
        for k in ks:
            for sub in range(2):
                src = source(k, sub)
                block = slot(k, sub, own_so, own_to, 1 - core)
                across(k, 0, sub, 0, src, src).wait_send()
                across(k, 0, sub, 0, block, block).wait_recv()
                keep(k, sub).wait()


    def tell(r):
        device, g = peer(r)
        return remote(stat, stats.at[group], st_send.at[r], st_recv.at[group], device)

    lax.fori_loop(1, 16, lambda r, _: (tell(r).start(), 0)[1], 0)
    half = pl.ds(pl.multiple_of(t * 256, 256), 256)
    rest = pl.ds(pl.multiple_of((1 - t) * 256, 256), 256)
    weights = ((wk_own, wk), (wv_own, wv), (wq_own, wq))
    swaps = [
        remote(w.at[:, rest], w_all.at[t], w_send.at[n], w_recv.at[n], partner)
        for n, (w, w_all) in enumerate(weights)
    ] + [remote(wo_own.at[rest, :], wo.at[t], w_send.at[3], w_recv.at[3], partner)]
    keeps = [
        pltpu.make_async_copy(w.at[:, half], w_all.at[t], w_own.at[n])
        for n, (w, w_all) in enumerate(weights)
    ] + [pltpu.make_async_copy(wo_own.at[half, :], wo.at[t], w_own.at[3])]
    for copy in swaps[:2]:
        copy.start()
    for copy in keeps:
        copy.start()
    stats[group] = stat[...]

    def hear(r, _):
        device, g = peer(r)
        remote(stat, stats.at[g], st_send.at[r], st_recv.at[g], device).wait_recv()
        return 0

    lax.fori_loop(1, 16, hear, 0)
    total = stats[0]
    for g in range(1, 16):
        total = total + stats[g]
    squares[...] = total
    scale = lax.rsqrt(total / WIDTH + EPS)
    scales = [jnp.broadcast_to(scale[n : n + 1], (128, 128)).T[:, :1] for n in range(3)]
    for n in range(2):
        rows = neigh[n * 128 : (n + 1) * 128].astype(F32)
        normed = rows * scales[n + 1] * enc_gain[...]
        enc[n * 128 : (n + 1) * 128] = normed.astype(BF16)
    begin((2, 3))
    rows = hidden[...].reshape(128, 512).astype(F32)
    dec[...] = (rows * scales[0] * dec_gain[...]).astype(BF16).reshape(2, 64, 512)

    def enc_step(j, _):
        gather_step((2, 3), j)

        @pl.when(j == 4)
        def _():
            begin((0, 1))

        @pl.when(j >= 6)
        def _():
            gather_step((0, 1), j - 6)

        return 0

    lax.fori_loop(0, 8, enc_step, 0)

    def zero(n, _):
        kv_recv[n, 0] = jnp.zeros((512, 256), BF16)
        qa_recv[n, 0] = jnp.zeros((256, 256), BF16)
        return 0

    lax.fori_loop(0, 4, zero, 0)
    for copy in swaps[2:]:
        copy.start()
    for copy in keeps:
        copy.wait()

    def swapped(n):
        swaps[n].wait_send()
        if n < 3:
            w, w_all = weights[n]
            dst = w_all.at[1 - t]
            remote(w.at[:, rest], dst, w_send.at[n], w_recv.at[n], partner).wait_recv()
        else:
            dst = wo.at[1 - t]
            remote(wo_own.at[rest, :], dst, w_send.at[n], w_recv.at[n], partner).wait_recv()

    swapped(0)
    swapped(1)
    gather_end((2, 3))
    stores = [
        pltpu.make_async_copy(src, dst, out_sem.at[n])
        for n, (src, dst) in enumerate(
            (
                (cot_v, cot_all),
                (dec_v, dec_all),
                (enc_v, enc_all),
                (wk, wk_out),
                (wv, wv_out),
                (wq, wq_out),
                (wo, wo_out),
            )
        )
    ]
    for copy in stores[2:5]:
        copy.start()


    def pair_part(d, h):
        stored = pl.ds(pl.multiple_of(d * 512 + h * 256, 256), 256)
        first, second = enc_v[0, stored, :], enc_v[1, stored, :]
        k = dot(first, wk[0]) + dot(second, wk[1])
        v = dot(first, wv[0]) + dot(second, wv[1])
        return ((0, 256, k), (256, 512, v))

    def query_part(d, h):
        j = d * 4 + h * 2
        b0, b1 = inverse[j], inverse[j + 1]
        q = a = 0.0
        for f in range(2):
            q = q + dot(jnp.concatenate([dec_v[f, b0], dec_v[f, b1]], axis=0), wq[f])
            a = a + dot_t(jnp.concatenate([cot_v[f, b0], cot_v[f, b1]], axis=0), wo[f])
        return ((0, 128, q), (128, 256, a))

    pairs = (kv_send, kv_recv, kv_ssem, kv_rsem, kv_fin, pair_part)
    queries = (qa_send, qa_recv, qa_ssem, qa_rsem, qa_fin, query_part)

    def chain(which, n, j, sign):
        sendb, recvb, ssem, rsem = which[:4]
        device = {"section": lax.rem(z + DEPTH + sign, DEPTH)}
        return remote(
            sendb.at[n, j], recvb.at[n, j + 1], ssem.at[n, j], rsem.at[n, j], device
        )

    def item(which, w):
        n, j = lax.rem(w, 4), lax.div(w, 4)
        h = lax.rem(n, 2)
        sign = 1 - 2 * lax.rem(h + lax.div(n, 2), 2)
        length = 4 - lax.div(n, 2)
        parts = which[5](lax.rem(z + DEPTH + sign * (length - j), DEPTH), h)

        @pl.when(j > 0)
        def _():
            chain(which, n, j - 1, sign).wait_recv()

        for lo, hi, part in parts:
            which[0][n, j, lo:hi] = (part + which[1][n, j, lo:hi].astype(F32)).astype(BF16)
        chain(which, n, j, sign).start()

    def last(which):
        def one(h, _):
            parts = which[5](z, h)
            chain(which, h, 3, 1).wait_recv()
            chain(which, h + 2, 2, 1).wait_recv()
            for lo, hi, part in parts:
                total = part + which[1][h, 4, lo:hi].astype(F32)
                total = total + which[1][h + 2, 3, lo:hi].astype(F32)
                which[4][h, lo:hi] = total.astype(BF16)
            return 0

        lax.fori_loop(0, 2, one, 0)

    def pair_item(w, _):
        item(pairs, w)

        @pl.when((lax.rem(w, 2) == 1) & (w > 2))
        def _():
            gather_step((0, 1), lax.div(w, 2) + 1)

        return 0

    lax.fori_loop(0, 14, pair_item, 0)
    gather_end((0, 1))
    swapped(2)
    swapped(3)
    for copy in stores[:2] + stores[5:]:
        copy.start()

    def query_item(w, _):
        item(queries, w)

        @pl.when(w == 7)
        def _():
            last(pairs)

        return 0

    lax.fori_loop(0, 14, query_item, 0)
    last(queries)

    for h in range(2):
        places = [(u, slice(g * 128, (g + 1) * 128)) for u in range(2) for g in range(2)]
        results = attend(
            [
                (
                    qa_fin[h, u * 64 : (u + 1) * 64, head],
                    qa_fin[h, 128 + u * 64 : 128 + (u + 1) * 64, head],
                    kv_fin[h, u * 128 : (u + 1) * 128, head],
                    kv_fin[h, 256 + u * 128 : 256 + (u + 1) * 128, head],
                    bias[pl.ds(z * 4 + h * 2 + u, 1), :],
                )
                for u, head in places
            ]
        )
        for (u, head), (attended, query_grad, key_grad, value_grad) in zip(places, results):
            n = h * 2 + u
            att[n, :, head] = attended
            qg[n, :, head] = query_grad
            kg[n * 128 : (n + 1) * 128, head] = key_grad
            vg[n * 128 : (n + 1) * 128, head] = value_grad

    def chain_end(w, _):
        chain(pairs, lax.rem(w, 4), lax.div(w, 4), 1).wait_send()
        chain(queries, lax.rem(w, 4), lax.div(w, 4), 1).wait_send()
        return 0

    lax.fori_loop(0, 14, chain_end, 0)
    lax.fori_loop(1, 16, lambda r, _: (tell(r).wait_send(), 0)[1], 0)
    for copy in stores:
        copy.wait()


def front(*args):
    sds = jax.ShapeDtypeStruct
    return pl.pallas_call(
        front_kernel,
        out_shape=[
            sds((2, 32, 64, 512), BF16),
            sds((2, 32, 64, 512), BF16),
            sds((2, 4096, 512), BF16),
            sds((2, 512, 256), BF16),
            sds((2, 512, 256), BF16),
            sds((2, 512, 256), BF16),
            sds((2, 256, 512), BF16),
            sds((4, 64, 256), BF16),
            sds((4, 64, 256), BF16),
            sds((512, 256), BF16),
            sds((512, 256), BF16),
            sds((8, 128), F32),
        ],
        in_specs=[VMEM] * 5 + [ANY] * 4 + [VMEM, SMEM],
        out_specs=[ANY] * 7 + [VMEM] * 5,
        scratch_shapes=[
            pltpu.VMEM((2, 32, 64, 512), BF16),
            pltpu.VMEM((2, 32, 64, 512), BF16),
            pltpu.VMEM((2, 4096, 512), BF16),
            pltpu.VMEM((2, 512, 256), BF16),
            pltpu.VMEM((2, 512, 256), BF16),
            pltpu.VMEM((2, 512, 256), BF16),
            pltpu.VMEM((2, 256, 512), BF16),
            pltpu.VMEM((2, 64, 512), BF16),
            pltpu.VMEM((256, 512), BF16),
            pltpu.VMEM((8, 128), F32),
            pltpu.VMEM((16, 8, 128), F32),
            pltpu.VMEM((4, 4, 512, 256), BF16),
            pltpu.VMEM((4, 5, 512, 256), BF16),
            pltpu.VMEM((4, 4, 256, 256), BF16),
            pltpu.VMEM((4, 5, 256, 256), BF16),
            pltpu.VMEM((2, 512, 256), BF16),
            pltpu.VMEM((2, 256, 256), BF16),
            DMA((16,)),
            DMA((16,)),
            DMA((4, 2, 2, 8)),
            DMA((4, 2, 2, 8)),
            DMA((4, 2, 2, 9)),
            DMA((4, 2, 2, 9)),
            DMA((4, 2)),
            DMA((4,)),
            DMA((4,)),
            DMA((4,)),
            DMA((7,)),
            DMA((4, 4)),
            DMA((4, 4)),
            DMA((4, 4)),
            DMA((4, 4)),
        ],
        compiler_params=params(1, 60),
    )(*args)


def back_kernel(
    att_own,
    qg_own,
    kg_own,
    vg_own,
    wq_hbm,
    wk_hbm,
    wv_hbm,
    wo_hbm,
    cot_hbm,
    dec_hbm,
    enc_hbm,
    ids,
    hidden,
    neigh,
    dec_gain,
    enc_gain,
    squares,
    dec_out,
    out_out,
    enc_out,
    grads,
    out_grad,
    grads_in,
    out_grad_in,
    inner_out,
    gain_out,
    att_all,
    qg_all,
    kg_all,
    vg_all,
    att,
    qg,
    cot,
    dec,
    enc,
    wq,
    wk,
    wv,
    wo,
    sib_out,
    sib_in,
    chain_out,
    chain_in,
    mine,
    acc,
    out_acc,
    pair_acc,
    grads_out,
    out_grad_out,
    inner,
    gains,
    inners,
    gainses,
    e_send,
    e_recv,
    g_send,
    g_recv,
    own_sem,
    x_sem,
    s_send,
    s_recv,
    c_send,
    c_recv,
    w_send,
    w_recv,
    o_sem,
):
    z, s, t, x, y, core = place()
    sibling = {"seq": s + 1 - 2 * core}
    partner = {"tensor": 1 - t}
    position = (ring_position(0, x, y), ring_position(1, x, y))
    loads = [
        pltpu.make_async_copy(src, dst, x_sem.at[n])
        for n, (src, dst) in enumerate(
            (
                (cot_hbm, cot),
                (dec_hbm, dec),
                (enc_hbm, enc),
                (wq_hbm, wq),
                (wk_hbm, wk),
                (wv_hbm, wv),
                (wo_hbm, wo),
            )
        )
    ]
    nexts = [
        [ring_device(ring, position[ring] + 1 - 2 * way, core) for way in range(2)]
        for ring in range(2)
    ]
    owns = (att_own, qg_own, kg_own, vg_own)
    alls = (att_all, qg_all, kg_all, vg_all)
    group = z * 2 + t
    sums = ((inner, inners, inner_out, group), (gains, gainses, gain_out, s))

    def peer(n, r):
        g = lax.rem(sums[n][3] + r, 16)
        return ({"section": lax.div(g, 2), "tensor": lax.rem(g, 2)} if n == 0 else {"seq": g}), g

    barrier = pltpu.get_barrier_semaphore()
    near = plane_neighbours(x, y, core, s)
    for device in near:
        pl.semaphore_signal(barrier, inc=1, device_id=device, device_id_type=MESH)

    def hello(r, _):
        for n in range(2):
            pl.semaphore_signal(barrier, inc=1, device_id=peer(n, r)[0], device_id_type=MESH)
        return 0

    lax.fori_loop(1, 16, hello, 0)
    pl.semaphore_wait(barrier, len(near) + 30)


    def ring_block(n, place_z):
        if n < 2:
            return alls[n].at[pl.ds(place_z * 4, 4)]
        return alls[n].at[pl.ds(pl.multiple_of(place_z * 512, 512), 512)]

    def ring_hops(n, way):
        return 4 if n % 2 == way else 3

    def ring_copy(n, way, j, src=None):
        sign = 1 - 2 * way
        block = ring_block(n, lax.rem(z + DEPTH - sign * j, DEPTH))
        device = {"section": lax.rem(z + DEPTH + sign, DEPTH)}
        return remote(
            block if src is None else src, block, g_send.at[n, way, j], g_recv.at[n, way, j], device
        )

    def ring_first(ns):
        for n in ns:
            for way in range(2):
                ring_copy(n, way, 0, owns[n]).start()

    def ring_step(ns, j):
        for n in ns:
            for way in range(2):

                @pl.when(j < ring_hops(n, way))
                def _(n=n, way=way):
                    sign = 1 - 2 * way
                    block = ring_block(n, lax.rem(z + DEPTH - sign * (j + 1), DEPTH))
                    remote(
                        block,
                        block,
                        g_send.at[n, way, j],
                        g_recv.at[n, way, j],
                        ring_neighbours(z)[0],
                    ).wait_recv()

                    @pl.when(j + 1 < ring_hops(n, way))
                    def _():
                        ring_copy(n, way, j + 1).start()

    def keep(n):
        return pltpu.make_async_copy(owns[n], ring_block(n, z), own_sem.at[n])

    ring_first((0, 1))
    for n in range(4):
        keep(n).start()
    for copy in loads[2:] + loads[:2]:
        copy.start()
    for k in range(4):
        for way in range(2):
            for sub in range(2):
                chain_in[k, way, sub, 0] = jnp.zeros((64, 512), BF16)

    def pair_weights(place_z):
        rows = pl.ds(pl.multiple_of(place_z * 512, 512), 512)
        block = jnp.concatenate([kg_all[rows, :], vg_all[rows, :]], axis=1)
        for f in range(2):
            pair_acc[f] += t_dot(enc[f, rows, :], block)

    pair_acc[...] = jnp.zeros((2, 512, 512), F32)

    def first_steps(j, _):
        ring_step((0, 1), j)

        @pl.when(j == 1)
        def _():
            loads[2].wait()
            keep(2).wait()
            keep(3).wait()
            pair_weights(z)

        @pl.when(j == 2)
        def _():
            ring_first((2, 3))

        return 0

    lax.fori_loop(0, 4, first_steps, 0)
    keep(0).wait()
    keep(1).wait()
    for copy in loads[3:]:
        copy.wait()

    def token_order(b, _):
        rows = pl.ds(pl.multiple_of(b * 64, 64), 64)
        att[rows, :] = att_all[ids[b]]
        qg[rows, :] = qg_all[ids[b]]
        return 0

    lax.fori_loop(0, 32, token_order, 0)


    def dest(ring, offset):
        cx, cy = ring_chip(ring, lax.rem(position[ring] + offset, RING))
        return seq_tensor(cx, cy, 0)

    def both(ref, base, stride):
        return jnp.concatenate(
            [
                ref[pl.ds(pl.multiple_of(base + c * stride, 128), 128), :]
                for c in (core, 1 - core)
            ],
            axis=0,
        )

    def product(k, offset):
        sd, td = dest(k % 2, offset)
        if k == 0:
            return dot_t(both(qg, sd * 128, 128), wq[td])
        if k == 1:
            return dot(both(att, sd * 128, 128), wo[td])
        base = sd * 256 + (k - 2) * 128
        return dot_t(both(kg_all, base, 256), wk[td]) + dot_t(both(vg_all, base, 256), wv[td])

    def across(k, i, four=0):
        return remote(
            sib_out.at[k, four],
            sib_in.at[k, i],
            s_send.at[k, i],
            s_recv.at[k, i],
            sibling,
        )

    def give(ks, i):
        half = lax.div(i, 2)
        four = lax.rem(i, 4)
        offset = 8 - half + (i - 2 * half) * (2 * half + 1)
        for k in ks:
            total = product(k, offset)

            @pl.when(i >= 4)
            def _(k=k):
                across(k, i - 4, four).wait_send()

            sib_out[k, four] = total[128:].astype(BF16)
            across(k, i, four).start()
            mine[k % 2, four] = total[:128]

    def onward(k, way, sub, j, two):
        return remote(
            chain_out.at[k, way, sub, two],
            chain_in.at[k, way, sub, j + 1],
            c_send.at[k, way, sub, j],
            c_recv.at[k, way, sub, j],
            nexts[k % 2][way],
        )

    def chain_step(ks, j):
        two = lax.rem(j, 2)
        for sub in range(2):
            part = slice(sub * 64, (sub + 1) * 64)
            for way in range(2):
                for k in ks:

                    @pl.when(j < 8 - way)
                    def _(k=k, way=way, sub=sub, part=part):
                        i = 2 * j + way
                        four = 2 * two + way
                        if sub == 0:
                            across(k, i).wait_recv()

                        @pl.when(j > 0)
                        def _():
                            onward(k, way, sub, j - 1, two).wait_recv()

                        @pl.when(j > 1)
                        def _():
                            onward(k, way, sub, j - 2, two).wait_send()

                        total = mine[k % 2, four, part] + sib_in[k, i, part].astype(F32)
                        total = total + chain_in[k, way, sub, j].astype(F32)
                        chain_out[k, way, sub, two] = total.astype(BF16)
                        onward(k, way, sub, j, two).start()

    def own_store(n):
        if n == 0:
            src, dst = acc, grads.at[0]
        elif n == 3:
            src, dst = out_acc, out_grad
        else:
            src, dst = pair_acc.at[t, :, pl.ds((n - 1) * 256, 256)], grads.at[n]
        return pltpu.make_async_copy(src, dst, o_sem.at[n])

    def query_swap():
        return remote(
            grads_out.at[0], grads_in.at[0], w_send.at[0, 0], w_recv.at[0, 0], partner
        )

    def out_swap():
        return remote(out_grad_out, out_grad_in, w_send.at[3, 0], w_recv.at[3, 0], partner)

    def pair_swap(j):
        n, m = 1 + lax.div(j, 4), lax.rem(j, 4)
        rows = pl.ds(pl.multiple_of(m * 128, 128), 128)
        return remote(
            grads_out.at[n, rows], grads_in.at[n, rows], w_send.at[n, m], w_recv.at[n, m], partner
        )

    def weight_step(j):
        f = 1 - t + lax.div(j, 4) * (2 * t - 1)
        here = pl.ds(pl.multiple_of(lax.rem(j, 4) * 512, 512), 512)

        @pl.when(lax.rem(j, 4) == 0)
        def _():
            acc[...] = jnp.zeros((512, 256), F32)
            out_acc[...] = jnp.zeros((256, 512), F32)

        acc[...] += t_dot(dec[f, here, :], qg[here, :])
        out_acc[...] += t_dot(att[here, :], cot[f, here, :])

        @pl.when(j == 3)
        def _():
            grads_out[0] = acc[...].astype(BF16)
            out_grad_out[...] = out_acc[...].astype(BF16)
            query_swap().start()
            out_swap().start()

        @pl.when(j == 7)
        def _():
            own_store(0).start()
            own_store(3).start()

    def scatter(ks, filler):
        give(ks, 0)
        give(ks, 1)

        def step(j, _):
            chain_step(ks, j)

            @pl.when(j < 7)
            def _():
                lax.fori_loop(2 * j + 2, 2 * j + 4, lambda i, _: (give(ks, i), 0)[1], 0)

            filler(j)
            return 0

        lax.fori_loop(0, 8, step, 0)
        outs = {
            0: dec_out,
            1: out_out,
            2: enc_out.at[pl.ds(0, 128)],
            3: enc_out.at[pl.ds(128, 128)],
        }
        for k in ks:
            across(k, 15).wait_recv()
            for sub in range(2):
                part = pl.ds(sub * 64, 64)
                total = mine[k % 2, 3, part] + sib_in[k, 15, part].astype(F32)
                for way in range(2):
                    onward(k, way, sub, 7 - way, 0).wait_recv()
                    total = total + chain_in[k, way, sub, 8 - way].astype(F32)
                outs[k][part, :] = total
        for k in ks:
            for i in range(12, 16):
                across(k, i).wait_send()
            for way in range(2):
                for sub in range(2):
                    onward(k, way, sub, 6 - way, 0).wait_send()
                    onward(k, way, sub, 7 - way, 1).wait_send()

    def token_filler(j):
        @pl.when(j == 0)
        def _():
            loads[0].wait()
            loads[1].wait()

        weight_step(j)

        @pl.when((lax.rem(j, 2) == 0) & (j > 0))
        def _():
            distance = lax.div(j, 2)
            pair_weights(lax.rem(z + distance, DEPTH))
            pair_weights(lax.rem(z + DEPTH - distance, DEPTH))

        @pl.when(lax.rem(j, 2) == 1)
        def _():
            ring_step((2, 3), lax.div(j, 2))

    inner[...] = jnp.zeros((8, 128), F32)
    gains[...] = jnp.zeros((8, 128), F32)
    scale = lax.rsqrt(squares[...] / WIDTH + EPS)
    scales = [jnp.broadcast_to(scale[n : n + 1], (128, 128)).T[:, :1] for n in range(3)]
    scatter((0, 1), token_filler)

    def sum_rows(n):
        part = slice(max(n - 1, 0) * 128, max(n - 1, 0) * 128 + 128)
        upstream = dec_out[...] if n == 0 else enc_out[part, :]
        unit = (hidden if n == 0 else neigh)[part, :].astype(F32) * scales[n]
        product_of = upstream * unit
        gain = (dec_gain if n == 0 else enc_gain)[...]
        column = jnp.sum(product_of * gain, axis=1, keepdims=True)
        inner[n : n + 1] = jnp.broadcast_to(column, (128, 128)).T[:1]
        row = jnp.sum(product_of, axis=0, keepdims=True)
        first = 0 if n == 0 else 4
        for m in range(4):
            gains[first + m : first + m + 1] += row[:, m * 128 : (m + 1) * 128]

    def pair_filler(j):
        @pl.when(j == 0)
        def _():
            pair_weights(lax.rem(z + 4, DEPTH))
            for a in range(2):
                half = slice(a * 256, (a + 1) * 256)
                grads_out[1 + a] = pair_acc[1 - t, :, half].astype(BF16)
                own_store(1 + a).start()

        pair_swap(j).start()

        @pl.when(j == 1)
        def _():
            sum_rows(0)

    scatter((2, 3), pair_filler)


    sum_rows(1)
    sum_rows(2)

    def tell(n, r):
        src, slots, _out, own = sums[n]
        return remote(src, slots.at[own], e_send.at[n, r], e_recv.at[n, own], peer(n, r)[0])

    def tell_all(r, _):
        for n in range(2):
            tell(n, r).start()
        return 0

    def hear_all(r, _):
        for n in range(2):
            src, slots, _out, own = sums[n]
            device, g = peer(n, r)
            remote(src, slots.at[g], e_send.at[n, r], e_recv.at[n, g], device).wait_recv()
        return 0

    def told_all(r, _):
        for n in range(2):
            tell(n, r).wait_send()
        return 0

    lax.fori_loop(1, 16, tell_all, 0)
    for src, slots, _out, own in sums:
        slots[own] = src[...]

    for n in range(4):
        for way in range(2):
            for j in range(ring_hops(n, way)):
                ring_copy(n, way, j).wait_send()
    query_swap().wait()
    out_swap().wait()
    for n in range(4):
        own_store(n).wait()
    lax.fori_loop(0, 8, lambda j, _: (pair_swap(j).wait(), 0)[1], 0)
    lax.fori_loop(1, 16, hear_all, 0)
    for src, slots, out, own in sums:
        total = slots[0]
        for g in range(1, 16):
            total = total + slots[g]
        out[...] = total
    lax.fori_loop(1, 16, told_all, 0)


def back(*args):
    sds = jax.ShapeDtypeStruct
    return pl.pallas_call(
        back_kernel,
        out_shape=[
            sds((128, 512), F32),
            sds((128, 512), F32),
            sds((256, 512), F32),
            sds((3, 512, 256), F32),
            sds((256, 512), F32),
            sds((3, 512, 256), BF16),
            sds((256, 512), BF16),
            sds((8, 128), F32),
            sds((8, 128), F32),
        ],
        in_specs=[VMEM] * 4 + [ANY] * 7 + [SMEM] + [VMEM] * 5,
        out_specs=[VMEM] * 3 + [ANY] * 4 + [VMEM] * 2,
        scratch_shapes=[
            pltpu.VMEM((32, 64, 256), BF16),
            pltpu.VMEM((32, 64, 256), BF16),
            pltpu.VMEM((4096, 256), BF16),
            pltpu.VMEM((4096, 256), BF16),
            pltpu.VMEM((2048, 256), BF16),
            pltpu.VMEM((2048, 256), BF16),
            pltpu.VMEM((2, 2048, 512), BF16),
            pltpu.VMEM((2, 2048, 512), BF16),
            pltpu.VMEM((2, 4096, 512), BF16),
            pltpu.VMEM((2, 512, 256), BF16),
            pltpu.VMEM((2, 512, 256), BF16),
            pltpu.VMEM((2, 512, 256), BF16),
            pltpu.VMEM((2, 256, 512), BF16),
            pltpu.VMEM((4, 4, 128, 512), BF16),
            pltpu.VMEM((4, 16, 128, 512), BF16),
            pltpu.VMEM((4, 2, 2, 2, 64, 512), BF16),
            pltpu.VMEM((4, 2, 2, 9, 64, 512), BF16),
            pltpu.VMEM((2, 4, 128, 512), F32),
            pltpu.VMEM((512, 256), F32),
            pltpu.VMEM((256, 512), F32),
            pltpu.VMEM((2, 512, 512), F32),
            pltpu.VMEM((3, 512, 256), BF16),
            pltpu.VMEM((256, 512), BF16),
            pltpu.VMEM((8, 128), F32),
            pltpu.VMEM((8, 128), F32),
            pltpu.VMEM((16, 8, 128), F32),
            pltpu.VMEM((16, 8, 128), F32),
            DMA((2, 16)),
            DMA((2, 16)),
            DMA((4, 2, 4)),
            DMA((4, 2, 4)),
            DMA((4,)),
            DMA((7,)),
            DMA((4, 16)),
            DMA((4, 16)),
            DMA((4, 2, 2, 8)),
            DMA((4, 2, 2, 8)),
            DMA((4, 4)),
            DMA((4, 4)),
            DMA((4,)),
        ],
        compiler_params=params(2, 63),
    )(*args)


def join_kernel(tensor, own, got, out_own, out_got, q_out, k_out, v_out, o_out):
    t = tensor[0]
    step = pl.program_id(0)
    mine = pl.ds(pl.multiple_of(t * 256, 256), 256)
    theirs = pl.ds(pl.multiple_of((1 - t) * 256, 256), 256)
    for n, out in enumerate((q_out, k_out, v_out)):
        out[:, mine] = own[n]
        out[:, theirs] = got[n].astype(F32)
    o_out[pl.ds(pl.multiple_of(t * 256 + step * 64, 64), 64), :] = out_own[...]
    o_out[pl.ds(pl.multiple_of((1 - t) * 256 + step * 64, 64), 64), :] = out_got[...].astype(F32)


def join(tensor, own, got, out_own, out_got):
    triple = pl.BlockSpec((3, 128, 256), lambda i: (0, i, 0))
    strip = pl.BlockSpec((64, 512), lambda i: (i, 0))
    block = pl.BlockSpec((128, 512), lambda i: (i, 0))
    return pl.pallas_call(
        join_kernel,
        grid=(4,),
        out_shape=[jax.ShapeDtypeStruct((512, 512), F32)] * 4,
        in_specs=[SMEM, triple, triple, strip, strip],
        out_specs=[block] * 3 + [pl.BlockSpec((512, 512), lambda i: (0, 0))],
    )(tensor, own, got, out_own, out_got)


def body(
    hidden,
    dec_gain,
    neigh_states,
    enc_gain,
    w_query,
    w_key,
    w_value,
    w_out,
    neighbour_ids,
    neighbour_len,
    cotangent,
):
    t = lax.axis_index("tensor")
    rows = hidden.shape[0]
    dec_rows = hidden.astype(F32)
    enc_rows = neigh_states.astype(F32)
    count = neighbour_ids.shape[0]
    inverse = jnp.sum(
        jnp.where(
            neighbour_ids[None, :] == jnp.arange(count, dtype=jnp.int32)[:, None],
            jnp.arange(count, dtype=jnp.int32)[None, :],
            0,
        ),
        axis=1,
    )
    slots = jnp.arange(128, dtype=jnp.int32)[None, :]
    bias = jnp.where(slots < neighbour_len[:, None], 0.0, -jnp.inf).astype(F32)
    cot_all, dec_all, enc_all, wq, wk, wv, wo, att, qg, kg, vg, squares = front(
        cotangent.reshape(2, 64, 512),
        hidden.reshape(2, 64, 512),
        neigh_states,
        dec_gain[None],
        enc_gain[None],
        w_query,
        w_key,
        w_value,
        w_out,
        bias,
        inverse,
    )
    dec_input, out_total, enc_input, own, out_own, got, out_got, inner, gains = back(
        att,
        qg,
        kg,
        vg,
        wq,
        wk,
        wv,
        wo,
        cot_all.reshape(2, 2048, 512),
        dec_all.reshape(2, 2048, 512),
        enc_all,
        neighbour_ids,
        hidden,
        neigh_states,
        dec_gain[None],
        enc_gain[None],
        squares,
    )
    scales = lax.rsqrt(squares.reshape(-1)[:384] / WIDTH + EPS)
    dec_scale, enc_scale = scales[:rows, None], scales[rows:, None]
    dec_hat = dec_rows * dec_scale
    enc_hat = enc_rows * enc_scale
    joined = join(jnp.full((1,), t, jnp.int32), own, got, out_own, out_got)
    layer_out = (dec_rows + out_total).astype(BF16)
    dec_scaled = dec_gain * dec_input
    enc_scaled = enc_gain * enc_input
    inner = inner.reshape(-1)[:384] / WIDTH
    gains = gains.reshape(-1)
    hidden_grad = cotangent.astype(F32) + dec_scale * (
        dec_scaled - dec_hat * inner[:rows, None]
    )
    neighbour_grad = enc_scale * (enc_scaled - enc_hat * inner[rows:, None])
    return (
        layer_out,
        hidden_grad,
        neighbour_grad,
        gains[:512],
        gains[512:],
        *joined,
    )


def solution(mesh):
    features = ("section", "tensor")
    rows = P("seq", features)
    vector = P(features)
    columns = P(features, "seq")
    return jax.shard_map(
        body,
        mesh=mesh,
        in_specs=(
            rows,
            vector,
            rows,
            vector,
            columns,
            columns,
            columns,
            rows,
            P(),
            P(),
            rows,
        ),
        out_specs=(rows, rows, rows, vector, vector, columns, columns, columns, rows),
        check_vma=False,
    )
```
